128 devices in a mesh: seq: 32 (over z, y_hi, x), exp: 4 (over y_lo, core).
Axes of the slice: x: 4, y: 4 (y_hi: 2, y_lo: 2; y = y_hi * 2 + y_lo), z: 4, core: 2. Of those that a mesh axis runs over, the one named last changes fastest.
Arguments:
- hidden_in: bfloat16 [8192, 1536], P('seq'), may hold values from -6 to 6
- attn_gain: float32 [1536], replicated, may hold values from 0.1 to 1.9
- q_weight: bfloat16 [1536, 1536], P(None, 'exp'), may hold values from -1.25 to 1.25
- k_weight: bfloat16 [1536, 512], P(None, 'exp'), may hold values from -0.625 to 0.625
- v_weight: bfloat16 [1536, 512], P(None, 'exp'), may hold values from -0.15625 to 0.15625
- o_weight: bfloat16 [1536, 1536], P('exp'), may hold values from -0.15625 to 0.15625
- cache_kv: bfloat16 [16384, 1024], P('seq', 'exp'), may hold values from -216 to 216
- moe_gain: float32 [1536], replicated, may hold values from 0.1 to 1.9
- expert_in: bfloat16 [32, 1536, 1024], P('seq'), may hold values from -0.15625 to 0.15625
- expert_out: bfloat16 [32, 512, 1536], P('seq'), may hold values from -0.25 to 0.25
- routes: int32 [8192, 8], P(('seq', 'exp')), may hold values from 0 to 31, all different within a row; in each aligned block of 64 rows (0 to 63, 64 to 127, ...) at most 32 rows name the same one
- route_prob: float32 [8192, 8], P(('seq', 'exp')), may hold values from 0.05 to 1
- page_slot: int32 [1024], replicated, may hold values from 0 to 31, as said below
Outputs:
- hidden_out: bfloat16 [8192, 1536], P(('seq', 'exp'))
- decode_pages: bfloat16 [1024, 8, 2, 512], P('seq', 'exp')
The draws below stay inside these ranges and needn't reach their ends.
Inputs may be any that keep to these rules, and one draw needn't show every extreme that they name: `routes`: in each aligned block of 64 rows (the rows of one device) no expert is named by more than 32 rows; a row names 8 different experts. `page_slot`: for each r, the 32 blocks b with b mod (32) == r have different slots.
All inputs are finite; a program needn't handle non-finite values.
Results may differ from the reference program's by a relative error of at most 0.0074.
Values may be sent and summed in bfloat16 or wider, within the bound.
A program may use at most 128 MiB of HBM per device.

```python
import math
import jax
import jax.numpy as jnp
import numpy as np
from jax import lax

D = 1536
HEADS = 24
KV_HEADS = 8
HEAD_DIM = 64
FF = 512
EXPERTS = 32
TOPK = 8
PAGE = 8
NEW = 8192
PROMPT = 4096
CACHE = 16384
ROWS_DEV = 64
CAP = 32
PAGES_SEQ = 32
NPAGES = 1024
N_SEQ = 32


def draw_cache_kv(key, part):
    shape = (CACHE, KV_HEADS, 2, HEAD_DIM)
    kind_scale = jnp.array([4.0, 1.0], jnp.float32)[None, None, :, None]
    base = jnp.clip(jax.random.normal(key, shape, jnp.float32), -6.0, 6.0)
    return (base * kind_scale).reshape(CACHE, KV_HEADS * 2 * HEAD_DIM).astype(jnp.bfloat16)


def draw_page_slot(key, part):
    groups = NPAGES // PAGES_SEQ
    group_keys = jax.random.split(key, groups)
    orders = jax.vmap(lambda group_key: jax.random.permutation(group_key, PAGES_SEQ))(group_keys)
    return orders.T.reshape(NPAGES).astype(jnp.int32)


def shard_levels(rng, extent, cuts, smallest, high):
    level, own = 1.0, jax.random.fold_in(rng, 6)
    for position, shards_of in cuts:
        draws = jnp.exp(jax.random.uniform(jax.random.fold_in(own, position), (shards_of,), jnp.float32, smallest / len(cuts), high / len(cuts)))
        level = level * jnp.repeat(draws, extent[position] // shards_of).reshape([-1 if axis == position else 1 for axis in range(len(extent))])
    return level


def assign_block(stream_key, own, number, rows, count, top, most, lean):
    ranking = jax.random.permutation(stream_key, count)
    packed, usual = portions_of(count, rows * top, most, lean, True), portions_of(count, rows * top, most, lean, False)
    places = jnp.arange(count)

    def named(lengths, turn):
        used = int((lengths > 0).sum())
        fixed = max(1, used // 4)
        shifted = fixed + (places - fixed + turn * (used - fixed)) % max(1, count - fixed)
        return jnp.zeros((count,), jnp.int32).at[ranking[jnp.where(places < fixed, places, shifted)]].set(jnp.asarray(lengths, jnp.int32))

    lengths = jnp.where(number % 4 == 0, named(packed, number // 4), named(usual, number - number // 4 - 1))
    mixed = jax.random.permutation(jax.random.fold_in(own, 3), count)
    source_of, receiver = mixed[0:count // 2 * 2:2], mixed[1:count // 2 * 2:2]
    margin = jnp.minimum(lengths[source_of] - 1, most - lengths[receiver]) // 2
    margin = jnp.where((source_of == ranking[0]) | (receiver == ranking[0]) | (lengths[receiver] == 0), 0, jnp.maximum(margin, 0))
    shifted = jax.random.randint(jax.random.fold_in(own, 4), (count // 2,), 0, 1 << 20) % (margin + 1)
    lengths = lengths.at[source_of].add(-shifted).at[receiver].add(shifted)
    members = jnp.searchsorted(jnp.cumsum(lengths), jnp.arange(rows * top), side="right").astype(jnp.int32)
    listing = members.reshape(top, rows).T
    listing = listing[jax.random.permutation(jax.random.fold_in(own, 1), rows)]
    turn = jax.random.randint(jax.random.fold_in(own, 2), (rows, 1), 0, top)
    return jnp.take_along_axis(listing, (jnp.arange(top)[None, :] + turn) % top, axis=1)


def portions_of(count, total, most, slope, full):
    weights = [(1 << 20) // math.isqrt(grade ** slope) + 1 for grade in range(1, count + 1)]
    largest = most if full else min(most, max(-(-total // count), total * weights[0] // sum(weights)))
    least = 1 if total - largest >= count - 1 else 0
    given, surplus = [largest] + [least] * (count - 1), total - largest - least * (count - 1)
    while surplus > 0:
        candidates = [i for i in range(1, count) if given[i] < largest] or [i for i in range(1, count) if given[i] < most]
        whole, left = sum([weights[i] for i in candidates]), surplus
        for i in candidates:
            more = min(most - given[i], max(1, left * weights[i] // whole), surplus)
            given[i] = given[i] + more
            surplus = surplus - more
    return np.array(given)


def noise(stream_key, extent, width, bound, pieces=(), kind=jnp.bfloat16):
    entries = width * jax.random.normal(stream_key, extent, jnp.float32)
    if pieces:
        entries = entries * shard_levels(stream_key, extent, pieces, -0.22, 0.18)
    return jnp.clip(entries, -bound, bound).astype(kind)


def setup_inputs(seed: int = 0) -> dict:
    streams_of = jax.random.split(jax.random.key(seed), 14)
    hidden_in = noise(streams_of[0], (NEW, D), 1.0, 6.0, ((0, 32),))
    attn_gain = jnp.clip(1.0 + 0.18 * jax.random.normal(streams_of[1], (D,), jnp.float32), 0.1, 1.9)
    q_weight = noise(streams_of[2], (D, HEADS * HEAD_DIM), (D // 64) ** -0.5, 1.25, ((1, 4),))
    k_weight = noise(streams_of[3], (D, KV_HEADS * HEAD_DIM), (D // 16) ** -0.5, 0.625, ((1, 4),))
    v_weight = noise(streams_of[4], (D, KV_HEADS * HEAD_DIM), D ** -0.5, 0.15625, ((1, 4),))
    o_weight = noise(streams_of[5], (HEADS * HEAD_DIM, D), (HEADS * HEAD_DIM) ** -0.5, 0.15625, ((0, 4),))
    cache_kv = draw_cache_kv(jax.random.fold_in(streams_of[13], 71), 0)
    moe_gain = jnp.clip(1.0 + 0.18 * jax.random.normal(streams_of[7], (D,), jnp.float32), 0.1, 1.9)
    expert_in = noise(streams_of[8], (EXPERTS, D, 2 * FF), D ** -0.5, 0.15625, ((0, 32),))
    expert_out = noise(streams_of[9], (EXPERTS, FF, D), FF ** -0.5, 0.25, ((0, 32),))
    routes_keys = jax.random.split(jax.random.fold_in(streams_of[10], 1), NEW // ROWS_DEV)
    routes_turns = jax.random.permutation(jax.random.fold_in(streams_of[10], 3), NEW // ROWS_DEV)
    routes = jax.vmap(lambda own, number: assign_block(jax.random.fold_in(streams_of[10], 2), own, number, ROWS_DEV, EXPERTS, TOPK, CAP, 2))(routes_keys, routes_turns).reshape((NEW, TOPK))
    route_prob = jnp.clip(0.05 + 0.95 * jax.random.uniform(streams_of[11], (NEW, TOPK), jnp.float32) ** shard_levels(streams_of[11], (NEW, TOPK), ((0, 128),), -0.2, 0.2), 0.05, 1.0)
    page_slot = draw_page_slot(jax.random.fold_in(streams_of[13], 71), 0)
    return {"hidden_in": hidden_in, "attn_gain": attn_gain, "q_weight": q_weight, "k_weight": k_weight, "v_weight": v_weight, "o_weight": o_weight, "cache_kv": cache_kv, "moe_gain": moe_gain, "expert_in": expert_in, "expert_out": expert_out, "routes": routes, "route_prob": route_prob, "page_slot": page_slot}


norm_epsilon = 1e-06
attention_scale = 0.015625
residual_scale = 0.22
masked_score = -1e+30

def rms_norm(values, gain_row):
    widened = values.astype(jnp.float32)
    spread = lax.rsqrt(lax.optimization_barrier(jnp.mean(widened * widened, axis=-1, keepdims=True)) + norm_epsilon)
    return (widened * spread * gain_row).astype(jnp.bfloat16)

def attend_all(queries, keys, values):
    block_rows = math.gcd(NEW, 512)
    key_count = CACHE + NEW
    key_index = jnp.arange(key_count, dtype=jnp.int32)
    key_new = key_index - CACHE
    key_cache = key_index < CACHE
    key_second = key_new >= PROMPT
    query_blocks = queries.reshape(NEW // block_rows, block_rows, KV_HEADS, HEADS // KV_HEADS, HEAD_DIM)
    block_starts = block_rows * jnp.arange(NEW // block_rows, dtype=jnp.int32)

    def one_block(pair_in):
        query_block, block_start = pair_in
        query_index = block_start + jnp.arange(block_rows, dtype=jnp.int32)
        query_second = query_index >= PROMPT
        visible = jnp.where(key_cache[None, :], jnp.logical_not(query_second)[:, None], (key_second[None, :] == query_second[:, None]) & (key_new[None, :] <= query_index[:, None]))

        def one_head(head_id):
            query_head = query_block[:, head_id].astype(jnp.float32)
            key_head = keys[:, head_id].astype(jnp.float32)
            value_head = values[:, head_id].astype(jnp.float32)
            scores = jnp.einsum('tgd,nd->gtn', query_head, key_head) * attention_scale
            scores = jnp.where(visible[None], scores, masked_score)
            row_best = lax.optimization_barrier(jnp.max(scores, axis=-1, keepdims=True))
            weights = jnp.where(visible[None], jnp.exp(scores - row_best), 0.0)
            total_sum = lax.optimization_barrier(jnp.sum(weights, axis=-1, keepdims=True))
            rounded = lax.optimization_barrier(weights.astype(jnp.bfloat16))
            summed = jnp.einsum('gtn,nd->gtd', rounded.astype(jnp.float32), value_head)
            return summed / total_sum
        head_outs = lax.map(one_head, jnp.arange(KV_HEADS, dtype=jnp.int32))
        return head_outs.transpose(2, 0, 1, 3).reshape(block_rows, HEADS * HEAD_DIM).astype(jnp.bfloat16)
    block_outs = lax.map(one_block, (query_blocks, block_starts))
    return block_outs.reshape(NEW, HEADS * HEAD_DIM)

def reference(hidden_in, attn_gain, q_weight, k_weight, v_weight, o_weight, cache_kv, moe_gain, expert_in, expert_out, routes, route_prob, page_slot):
    normed = rms_norm(hidden_in, attn_gain)
    queries = jnp.dot(normed, q_weight, preferred_element_type=jnp.float32).astype(jnp.bfloat16)
    queries = queries.reshape(NEW, KV_HEADS, HEADS // KV_HEADS, HEAD_DIM)
    keys_new = jnp.dot(normed, k_weight, preferred_element_type=jnp.float32).astype(jnp.bfloat16).reshape(NEW, KV_HEADS, HEAD_DIM)
    values_new = jnp.dot(normed, v_weight, preferred_element_type=jnp.float32).astype(jnp.bfloat16).reshape(NEW, KV_HEADS, HEAD_DIM)
    cache_rows = cache_kv.reshape(CACHE, KV_HEADS, 2, HEAD_DIM)
    keys = jnp.concatenate([cache_rows[:, :, 0], keys_new], axis=0)
    values = jnp.concatenate([cache_rows[:, :, 1], values_new], axis=0)
    attended = attend_all(queries, keys, values)
    mixed_rows = jnp.dot(attended, o_weight, preferred_element_type=jnp.float32)
    residual = hidden_in.astype(jnp.float32) + residual_scale * mixed_rows
    moe_in = rms_norm(residual, moe_gain)
    flat_ids = routes.reshape(-1).astype(jnp.int32)
    flat_weights = (route_prob / lax.optimization_barrier(jnp.sum(route_prob, axis=-1, keepdims=True))).reshape(-1)
    assign_count = NEW * TOPK
    load_bound = NEW // ROWS_DEV * CAP

    def one_expert(total_moe, expert):
        picked_ids = jnp.nonzero(flat_ids == expert, size=load_bound, fill_value=assign_count)[0].astype(jnp.int32)
        is_valid = picked_ids < assign_count
        clipped = jnp.minimum(picked_ids, assign_count - 1)
        token_ids = clipped // TOPK
        rows_in = moe_in[token_ids]
        hidden = jnp.dot(rows_in, expert_in[expert], preferred_element_type=jnp.float32)
        active = (jax.nn.silu(hidden[:, :FF]) * hidden[:, FF:]).astype(jnp.bfloat16)
        produced = jnp.dot(active, expert_out[expert], preferred_element_type=jnp.float32).astype(jnp.bfloat16)
        share = jnp.where(is_valid, flat_weights[clipped], 0.0)
        total_moe = total_moe.at[token_ids].add(share[:, None] * produced.astype(jnp.float32))
        return (total_moe, None)
    moe, _ = lax.scan(one_expert, jnp.zeros((NEW, D), jnp.float32), jnp.arange(EXPERTS, dtype=jnp.int32))
    hidden_out = (residual + residual_scale * moe).astype(jnp.bfloat16)
    pair_rows = jnp.stack([keys_new, values_new], axis=2).reshape(NPAGES, PAGE, KV_HEADS, 2, HEAD_DIM)
    block_ids = jnp.arange(NPAGES, dtype=jnp.int32)
    target = block_ids % N_SEQ * PAGES_SEQ + page_slot.astype(jnp.int32)
    placed = jnp.zeros_like(pair_rows).at[target].set(pair_rows)
    decode_pages = placed.transpose(0, 2, 3, 1, 4).reshape(NPAGES, KV_HEADS, 2, PAGE * HEAD_DIM)
    return (hidden_out, decode_pages)
```

```python
import functools

import jax
import jax.numpy as jnp
from jax import lax
from jax.experimental import pallas as pl
from jax.experimental.pallas import tpu as pltpu
from jax.sharding import PartitionSpec as P

HEADS_HERE = 6
KV_HERE = 2
GROUP = 3
HEAD_DIM = 64
EXPERTS = 32
CAP = 32
PAGE = 8
PLANES = 4
LINE = 8
ROWS = 256
CACHE_HERE = 512

norm_epsilon = 1e-06
attention_scale = 0.015625
residual_scale = 0.22
masked_score = -1e30

PLANE_GROUPS = [[z * LINE + i for i in range(LINE)] for z in range(PLANES)]
LINE_GROUPS = [[z * LINE + i for z in range(PLANES)] for i in range(LINE)]


def rms_norm(values, gain_row):
    widened = values.astype(jnp.float32)
    spread = lax.rsqrt(jnp.mean(widened * widened, axis=-1, keepdims=True) + norm_epsilon)
    return (widened * spread * gain_row).astype(jnp.bfloat16)


def flash_kernel(q_ref, cache_ref, new_ref, out_ref, cache_val, new_val, qs, best, acc):
    seq_index = lax.axis_index("seq")
    plane = seq_index // LINE
    place = seq_index % LINE
    lane = lax.broadcasted_iota(jnp.int32, (ROWS, 2 * HEAD_DIM), 1)
    low = lane < HEAD_DIM

    def fill(source, target):
        @pl.loop(0, source.shape[0] // ROWS)
        def _(step):
            rows = pl.ds(pl.multiple_of(step * ROWS, ROWS), ROWS)
            for g in range(KV_HERE):
                cols = slice(g * 128, (g + 1) * 128)
                target[rows, cols] = jnp.where(low, jnp.ones((), jnp.bfloat16), source[rows, cols])

    fill(cache_ref, cache_val)
    fill(new_ref, new_val)

    def update(g, key_block, value_block, masked):
        for a in range(GROUP):
            rows = slice(a * ROWS, (a + 1) * ROWS)
            scores = lax.dot_general(
                qs[rows, :], key_block, (((1,), (1,)), ((), ())), preferred_element_type=jnp.float32
            )
            if masked:
                r = lax.broadcasted_iota(jnp.int32, scores.shape, 0)
                c = lax.broadcasted_iota(jnp.int32, scores.shape, 1)
                scores = jnp.where(c <= r, scores, masked_score)
            old = best[rows, :]
            new = jnp.maximum(old, jnp.max(scores, axis=-1, keepdims=True))
            best[rows, :] = new
            weights = jnp.exp(scores - new[:, :1]).astype(jnp.bfloat16)
            acc[rows, :] = acc[rows, :] * jnp.exp(old - new) + jnp.dot(
                weights, value_block, preferred_element_type=jnp.float32
            )

    BK = 1024

    @pl.loop(0, PLANES)
    def _(t):
        is_own = t == plane
        is_full = jnp.logical_and(plane % 2 == 0, t == plane + 1)
        cache_steps = jnp.where(t < 2, PLANES * 1024 // BK, 0)
        full_steps = jnp.where(is_own, place, jnp.where(is_full, LINE, 0))
        heads = []
        for g in range(KV_HERE):
            cols = slice(g * 128, (g + 1) * 128)
            for a in range(GROUP):
                h = g * GROUP + a
                slab = q_ref[t, :, (h // 2) * 128 : (h // 2 + 1) * 128]
                slab = slab.astype(jnp.float32) * attention_scale
                if h % 2:
                    slab = pltpu.roll(slab, HEAD_DIM, 1)
                qs[a * ROWS : (a + 1) * ROWS, :] = jnp.where(low, slab, 0.0).astype(jnp.bfloat16)
            best[...] = jnp.full_like(best, masked_score)
            acc[...] = jnp.zeros_like(acc)

            @pl.loop(0, cache_steps)
            def _(step):
                rows = pl.ds(pl.multiple_of(step * BK, BK), BK)
                update(g, cache_ref[rows, cols], cache_val[rows, cols], False)

            @pl.loop(0, full_steps)
            def _(step):
                rows = pl.ds(pl.multiple_of(step * ROWS, ROWS), ROWS)
                update(g, new_ref[rows, cols], new_val[rows, cols], False)

            @pl.when(is_own)
            def _():
                rows = pl.ds(pl.multiple_of(place * ROWS, ROWS), ROWS)
                update(g, new_ref[rows, cols], new_val[rows, cols], True)

            for a in range(GROUP):
                rows = slice(a * ROWS, (a + 1) * ROWS)
                part = acc[rows, :]
                total = part[:, :1]
                safe = jnp.where(total > 0.0, total, 1.0)
                heads.append((part / safe, jnp.where(total > 0.0, best[rows, :1] + jnp.log(safe), masked_score)))
        for p in range(HEADS_HERE // 2):
            pair = jnp.where(low, pltpu.roll(heads[2 * p][0], HEAD_DIM, 1), heads[2 * p + 1][0])
            out_ref[t, :, p * 128 : (p + 1) * 128] = pair.astype(jnp.bfloat16)
        levels = jnp.zeros((ROWS, 128), jnp.float32)
        for h in range(HEADS_HERE):
            levels = jnp.where(lane % 8 == h, heads[h][1], levels)
        high = levels.astype(jnp.bfloat16).astype(jnp.float32)
        rest = levels - high
        middle = rest.astype(jnp.bfloat16).astype(jnp.float32)
        split = jnp.where(lane < 8, high, jnp.where(lane < 16, middle, rest - middle))
        out_ref[t, :, 384:512] = split.astype(jnp.bfloat16)


def flash(queries, cache_rows, new_rows):
    vmem = pl.BlockSpec(memory_space=pltpu.VMEM)
    return pl.pallas_call(
        flash_kernel,
        out_shape=jax.ShapeDtypeStruct((PLANES, ROWS, 512), jnp.bfloat16),
        in_specs=[vmem] * 3,
        out_specs=vmem,
        scratch_shapes=[
            pltpu.VMEM(cache_rows.shape, jnp.bfloat16),
            pltpu.VMEM(new_rows.shape, jnp.bfloat16),
            pltpu.VMEM((GROUP * ROWS, 128), jnp.bfloat16),
            pltpu.VMEM((GROUP * ROWS, 128), jnp.float32),
            pltpu.VMEM((GROUP * ROWS, 128), jnp.float32),
        ],
        compiler_params=pltpu.CompilerParams(vmem_limit_bytes=48 * 1024 * 1024),
        name="flash",
    )(queries, cache_rows, new_rows)


def pages(pairs_new, page_slot, seq_index):
    seq_count = 32
    blocks_here = ROWS // PAGE
    outgoing = pairs_new.reshape(seq_count, PAGE * 256)
    received = lax.all_to_all(outgoing, "seq", split_axis=0, concat_axis=0, tiled=True)
    slots = lax.dynamic_index_in_dim(page_slot.reshape(seq_count, seq_count), seq_index, 1, keepdims=False)
    place = (slots[None, :] == jnp.arange(blocks_here, dtype=jnp.int32)[:, None]).astype(jnp.bfloat16)
    placed = jnp.dot(place, received, preferred_element_type=jnp.float32).astype(jnp.bfloat16)
    page_rows = placed.reshape(blocks_here, PAGE, KV_HERE, 2, HEAD_DIM).transpose(0, 2, 3, 1, 4)
    return page_rows.reshape(blocks_here, KV_HERE, 2, PAGE * HEAD_DIM)


def body(
    hidden_in,
    attn_gain,
    q_weight,
    k_weight,
    v_weight,
    o_weight,
    cache_kv,
    moe_gain,
    expert_in,
    expert_out,
    routes,
    route_prob,
    page_slot,
):
    seq_index = lax.axis_index("seq")
    exp_index = lax.axis_index("exp")
    cache_rows = lax.all_gather(cache_kv, "seq", axis_index_groups=PLANE_GROUPS, tiled=True)
    normed = rms_norm(hidden_in, attn_gain)
    pair_weight = jnp.concatenate(
        [k_weight[:, :64], v_weight[:, :64], k_weight[:, 64:], v_weight[:, 64:]], axis=1
    )
    pairs_new = jnp.dot(normed, pair_weight, preferred_element_type=jnp.float32).astype(jnp.bfloat16)
    new_rows = lax.all_gather(pairs_new, "seq", axis_index_groups=PLANE_GROUPS, tiled=True)
    queries = jnp.dot(normed, q_weight, preferred_element_type=jnp.float32).astype(jnp.bfloat16)
    line_queries = lax.all_gather(queries, "seq", axis_index_groups=LINE_GROUPS)
    partial = flash(line_queries, cache_rows, new_rows)
    parts = lax.all_to_all(
        partial, "seq", split_axis=0, concat_axis=0, axis_index_groups=LINE_GROUPS, tiled=True
    ).astype(jnp.float32)
    levels = parts[..., 384:390] + parts[..., 392:398] + parts[..., 400:406]
    shares = jnp.exp(levels - jnp.max(levels, axis=0, keepdims=True))
    shares = shares / jnp.sum(shares, axis=0, keepdims=True)
    outs = parts[..., :384].reshape(PLANES, ROWS, HEADS_HERE, HEAD_DIM)
    attended = jnp.sum(outs * shares[..., None], axis=0).reshape(ROWS, 384).astype(jnp.bfloat16)

    page_rows = pages(pairs_new, page_slot, seq_index)

    mixed_rows = lax.psum_scatter(
        jnp.dot(attended, o_weight, preferred_element_type=jnp.float32).astype(jnp.bfloat16),
        "exp",
        scatter_dimension=0,
        tiled=True,
    ).astype(jnp.float32)
    moe_rows = mixed_rows.shape[0]
    residual = (
        lax.dynamic_slice_in_dim(hidden_in, exp_index * moe_rows, moe_rows, 0).astype(jnp.float32)
        + residual_scale * mixed_rows
    )
    moe_in = rms_norm(residual, moe_gain)

    named = (routes[:, :, None] == jnp.arange(EXPERTS, dtype=jnp.int32)).astype(jnp.float32)
    hit = jnp.sum(named, axis=1)
    share = route_prob / jnp.sum(route_prob, axis=-1, keepdims=True)
    share_of = jnp.sum(named * share[..., None], axis=1)
    before = jnp.tril(jnp.ones((moe_rows, moe_rows), jnp.bfloat16), -1)
    rank = jnp.dot(before, hit.astype(jnp.bfloat16), preferred_element_type=jnp.float32)
    slot = jnp.arange(CAP, dtype=jnp.float32)
    chosen = jnp.where(hit[..., None] > 0, (rank[..., None] == slot).astype(jnp.float32), 0.0)
    chosen = chosen.reshape(moe_rows, EXPERTS * CAP)
    mixing = chosen * jnp.repeat(share_of, CAP, axis=1)
    dispatched = lax.dot_general(
        chosen.astype(jnp.bfloat16), moe_in, (((0,), (0,)), ((), ())), preferred_element_type=jnp.float32
    ).astype(jnp.bfloat16)
    arrived = lax.all_to_all(
        dispatched.reshape(EXPERTS, CAP, -1), "seq", split_axis=0, concat_axis=0, tiled=True
    ).reshape(EXPERTS * CAP, -1)
    hidden = jnp.dot(arrived, expert_in[0], preferred_element_type=jnp.float32)
    half_width = hidden.shape[-1] // 2
    active = (jax.nn.silu(hidden[:, :half_width]) * hidden[:, half_width:]).astype(jnp.bfloat16)
    produced = jnp.dot(active, expert_out[0], preferred_element_type=jnp.float32).astype(jnp.bfloat16)
    returned = lax.all_to_all(
        produced.reshape(EXPERTS, CAP, -1), "seq", split_axis=0, concat_axis=0, tiled=True
    ).reshape(EXPERTS * CAP, -1)
    high = mixing.astype(jnp.bfloat16)
    low = (mixing - high.astype(jnp.float32)).astype(jnp.bfloat16)
    moe = jnp.dot(high, returned, preferred_element_type=jnp.float32) + jnp.dot(
        low, returned, preferred_element_type=jnp.float32
    )
    hidden_out = (residual + residual_scale * moe).astype(jnp.bfloat16)
    return (hidden_out, page_rows)


def solution(mesh):
    return jax.shard_map(
        body,
        mesh=mesh,
        in_specs=(
            P("seq", None),
            P(),
            P(None, "exp"),
            P(None, "exp"),
            P(None, "exp"),
            P("exp", None),
            P("seq", "exp"),
            P(),
            P("seq", None, None),
            P("seq", None, None),
            P(("seq", "exp"), None),
            P(("seq", "exp"), None),
            P(),
        ),
        out_specs=(P(("seq", "exp"), None), P("seq", "exp", None, None)),
        check_vma=False,
    )
```

```python
import functools

import jax
import jax.numpy as jnp
from jax import lax
from jax.experimental import pallas as pl
from jax.experimental.pallas import tpu as pltpu
from jax.sharding import PartitionSpec as P

HEADS_HERE = 6
KV_HERE = 2
GROUP = 3
HEAD_DIM = 64
EXPERTS = 32
CAP = 32
PAGE = 8
PLANES = 4
LINE = 8
ROWS = 256
CACHE_HERE = 512

norm_epsilon = 1e-06
attention_scale = 0.015625
residual_scale = 0.22
masked_score = -1e30


def rms_norm(values, gain_row):
    widened = values.astype(jnp.float32)
    spread = lax.rsqrt(jnp.mean(widened * widened, axis=-1, keepdims=True) + norm_epsilon)
    return (widened * spread * gain_row).astype(jnp.bfloat16)


def attend_kernel(
    q_ref, cache_ref, new_ref, out_ref,
    q_all, cache_all, new_all, cache_val, new_val, qs, best, acc, part_send, part_recv,
    q_out, q_in, cache_out, cache_in, new_out, new_in, part_out, part_in,
):
    seq_index = lax.axis_index("seq")
    plane = seq_index // LINE
    place = seq_index % LINE
    even = plane % 2 == 0
    lane = lax.broadcasted_iota(jnp.int32, (ROWS, 2 * HEAD_DIM), 1)
    low = lane < HEAD_DIM
    one = jnp.ones((), jnp.bfloat16)

    def send(source, target, out_sem, in_sem, to):
        return pltpu.make_async_remote_copy(
            src_ref=source, dst_ref=target, send_sem=out_sem, recv_sem=in_sem,
            device_id={"seq": to}, device_id_type=pl.DeviceIdType.MESH,
        )

    def peer(j):
        return plane * LINE + lax.rem(place + j, LINE)

    def line_peer(k):
        return lax.rem(plane + k, PLANES) * LINE + place

    def cache_copy(j):
        return send(cache_ref, cache_all.at[j], cache_out.at[j], cache_in.at[j], peer(j))

    def new_copy(j):
        return send(new_ref, new_all.at[j], new_out.at[j], new_in.at[j], peer(j))

    def query_copy(k):
        return send(q_ref, q_all.at[plane], q_out.at[k], q_in.at[k], line_peer(k))

    def part_copy(k):
        return send(
            part_send.at[k], part_recv.at[k], part_out.at[k], part_in.at[k], line_peer(k)
        )

    def sends_query(k):
        return jnp.logical_or(plane < 2, plane == 3) if k == 3 else plane < 2

    def gets_query(k):
        origin = lax.rem(plane + PLANES - k, PLANES)
        return jnp.logical_or(origin < 2, origin == 3) if k == 3 else origin < 2

    def sends_part(k):
        target = lax.rem(plane + k, PLANES)
        return jnp.logical_or(target < 2, target == 3) if k == 1 else target < 2

    def gets_part(k):
        return jnp.logical_or(plane < 2, plane == 3) if k == 1 else plane < 2

    barrier = pltpu.get_barrier_semaphore()

    @pl.loop(1, LINE)
    def _(j):
        pl.semaphore_signal(barrier, inc=1, device_id={"seq": peer(j)}, device_id_type=pl.DeviceIdType.MESH)

    for k in range(1, PLANES):
        pl.semaphore_signal(
            barrier, inc=1, device_id={"seq": line_peer(k)}, device_id_type=pl.DeviceIdType.MESH
        )

    q_all[plane] = q_ref[...]
    cache_all[0] = cache_ref[...]
    new_all[0] = new_ref[...]
    best[...] = jnp.full_like(best, masked_score)
    acc[...] = jnp.zeros_like(acc)
    for k in range(1, PLANES):
        @pl.when(jnp.logical_not(gets_part(k)))
        def _():
            part_recv[k, :, :384] = jnp.zeros((ROWS, 384), jnp.bfloat16)
            part_recv[k, :, 384:] = jnp.full((ROWS, 128), masked_score, jnp.bfloat16)

    pl.semaphore_wait(barrier, LINE - 1 + PLANES - 1)

    for k in range(1, PLANES):
        @pl.when(sends_query(k))
        def _():
            query_copy(k).start()

    @pl.loop(1, LINE)
    def _(j):
        cache_copy(j).start()
        new_copy(j).start()

    def prepare(t):
        for h in range(HEADS_HERE):
            slab = q_all[t, :, (h // 2) * 128 : (h // 2 + 1) * 128]
            slab = slab.astype(jnp.float32) * attention_scale
            if h % 2:
                slab = pltpu.roll(slab, HEAD_DIM, 1)
            a = h % GROUP
            qs[t, h // GROUP, a * ROWS : (a + 1) * ROWS, :] = jnp.where(low, slab, 0.0).astype(jnp.bfloat16)

    def update(t, g, key_block, value_block, masked):
        for a in range(GROUP):
            rows = slice(a * ROWS, (a + 1) * ROWS)
            scores = lax.dot_general(
                qs[t, g, rows, :], key_block, (((1,), (1,)), ((), ())), preferred_element_type=jnp.float32
            )
            if masked:
                r = lax.broadcasted_iota(jnp.int32, scores.shape, 0)
                c = lax.broadcasted_iota(jnp.int32, scores.shape, 1)
                scores = jnp.where(c <= r, scores, masked_score)
            old = best[t, g, rows, :]
            new = jnp.maximum(old, jnp.max(scores, axis=-1, keepdims=True))
            best[t, g, rows, :] = new
            weights = jnp.exp(scores - new[:, :1]).astype(jnp.bfloat16)
            acc[t, g, rows, :] = acc[t, g, rows, :] * jnp.exp(old - new) + jnp.dot(
                weights, value_block, preferred_element_type=jnp.float32
            )

    def slab_of(g):
        return slice(g * 128, (g + 1) * 128)

    def fill_new(j):
        for g in range(KV_HERE):
            new_val[:, slab_of(g)] = jnp.where(low, one, new_all[j, :, slab_of(g)])

    prepare(plane)
    fill_new(0)
    for g in range(KV_HERE):
        update(plane, g, new_ref[:, slab_of(g)], new_val[:, slab_of(g)], True)

    for k in range(1, PLANES):
        @pl.when(gets_query(k))
        def _():
            query_copy(k).wait_recv()
            prepare(lax.rem(plane + PLANES - k, PLANES))

    @pl.loop(0, LINE)
    def _(j):
        @pl.when(j > 0)
        def _():
            cache_copy(j).wait_recv()
            new_copy(j).wait_recv()

        for half in range(CACHE_HERE // ROWS):
            rows = slice(half * ROWS, (half + 1) * ROWS)
            for g in range(KV_HERE):
                cache_val[rows, slab_of(g)] = jnp.where(low, one, cache_all[j, rows, slab_of(g)])

        @pl.loop(0, 2)
        def _(t):
            for g in range(KV_HERE):
                update(t, g, cache_all[j, :, slab_of(g)], cache_val[:, slab_of(g)], False)

        fill_new(j)
        first = jnp.where(jnp.logical_and(j > 0, j <= place), 0, 1)
        last = jnp.where(even, 2, 1)

        @pl.loop(first, last)
        def _(step):
            for g in range(KV_HERE):
                update(plane + step, g, new_all[j, :, slab_of(g)], new_val[:, slab_of(g)], False)

    def finish(t):
        heads = []
        for h in range(HEADS_HERE):
            g, rows = h // GROUP, slice((h % GROUP) * ROWS, (h % GROUP + 1) * ROWS)
            part = acc[t, g, rows, :]
            total = part[:, :1]
            heads.append((part / total, best[t, g, rows, :] + jnp.log(total)))
        levels = jnp.zeros((ROWS, 128), jnp.float32)
        for h in range(HEADS_HERE):
            levels = jnp.where(lane % 8 == h, heads[h][1], levels)
        return [
            jnp.where(low, pltpu.roll(heads[2 * p][0], HEAD_DIM, 1), heads[2 * p + 1][0])
            for p in range(HEADS_HERE // 2)
        ], levels

    for k in range(1, PLANES):
        @pl.when(sends_part(k))
        def _():
            pairs, levels = finish(lax.rem(plane + k, PLANES))
            for p in range(HEADS_HERE // 2):
                part_send[k, :, p * 128 : (p + 1) * 128] = pairs[p].astype(jnp.bfloat16)
            high = levels.astype(jnp.bfloat16).astype(jnp.float32)
            rest = levels - high
            middle = rest.astype(jnp.bfloat16).astype(jnp.float32)
            split = jnp.where(lane < 8, high, jnp.where(lane < 16, middle, rest - middle))
            part_send[k, :, 384:512] = split.astype(jnp.bfloat16)
            part_copy(k).start()

    pairs, own_level = finish(plane)
    for k in range(1, PLANES):
        @pl.when(gets_part(k))
        def _():
            part_copy(k).wait_recv()
    levels = [own_level]
    for k in range(1, PLANES):
        slab = part_recv[k, :, 384:512].astype(jnp.float32)
        levels.append(slab + pltpu.roll(slab, 120, 1) + pltpu.roll(slab, 112, 1))
    top = functools.reduce(jnp.maximum, levels)
    shares = [jnp.exp(level - top) for level in levels]
    whole = functools.reduce(jnp.add, shares)
    shares = [share / whole for share in shares]

    def spread(share, p):
        return jnp.where(low, share[:, 2 * p : 2 * p + 1], share[:, 2 * p + 1 : 2 * p + 2])

    for p in range(HEADS_HERE // 2):
        cols = slice(p * 128, (p + 1) * 128)
        value = pairs[p] * spread(shares[0], p)
        for k in range(1, PLANES):
            value = value + part_recv[k, :, cols].astype(jnp.float32) * spread(shares[k], p)
        out_ref[:, cols] = value.astype(jnp.bfloat16)

    @pl.loop(1, LINE)
    def _(j):
        cache_copy(j).wait_send()
        new_copy(j).wait_send()

    for k in range(1, PLANES):
        @pl.when(sends_query(k))
        def _():
            query_copy(k).wait_send()

        @pl.when(sends_part(k))
        def _():
            part_copy(k).wait_send()


def attend(queries, cache_rows, new_rows):
    vmem = pl.BlockSpec(memory_space=pltpu.VMEM)
    state = pltpu.VMEM((PLANES, KV_HERE, GROUP * ROWS, 128), jnp.float32)
    return pl.pallas_call(
        attend_kernel,
        out_shape=jax.ShapeDtypeStruct((ROWS, 384), jnp.bfloat16),
        in_specs=[vmem] * 3,
        out_specs=vmem,
        scratch_shapes=[
            pltpu.VMEM((PLANES, ROWS, 384), jnp.bfloat16),
            pltpu.VMEM((LINE, CACHE_HERE, 256), jnp.bfloat16),
            pltpu.VMEM((LINE, ROWS, 256), jnp.bfloat16),
            pltpu.VMEM((CACHE_HERE, 256), jnp.bfloat16),
            pltpu.VMEM((ROWS, 256), jnp.bfloat16),
            pltpu.VMEM((PLANES, KV_HERE, GROUP * ROWS, 128), jnp.bfloat16),
            state,
            state,
            pltpu.VMEM((PLANES, ROWS, 512), jnp.bfloat16),
            pltpu.VMEM((PLANES, ROWS, 512), jnp.bfloat16),
        ]
        + [pltpu.SemaphoreType.DMA((n,)) for n in (4, 4, 8, 8, 8, 8, 4, 4)],
        compiler_params=pltpu.CompilerParams(
            vmem_limit_bytes=48 * 1024 * 1024, collective_id=1, has_side_effects=True
        ),
        name="attend",
    )(queries, cache_rows, new_rows)


def experts_kernel(
    att_ref, ow_ref, hid_ref, gain_ref, chosen_ref, mix_ref, win_ref, wout_ref, out_ref,
    product, sum_send, sum_recv, residual, moe_in, rows_send, rows_recv, made, rows_back, total,
    sum_out, sum_in, go_out, go_in, back_out, back_in,
):
    seq_index = lax.axis_index("seq")
    exp_index = lax.axis_index("exp")
    plane = seq_index // LINE
    place = seq_index % LINE
    MESH = pl.DeviceIdType.MESH

    def ahead(k, j):
        return lax.rem(plane + k, PLANES) * LINE + lax.rem(place + j, LINE)

    def behind(k, j):
        return lax.rem(plane + PLANES - k, PLANES) * LINE + lax.rem(place + LINE - j, LINE)

    def side(k):
        return lax.rem(exp_index + k, 4)

    def sum_copy(k):
        return pltpu.make_async_remote_copy(
            src_ref=sum_send.at[k], dst_ref=sum_recv.at[k], send_sem=sum_out.at[k], recv_sem=sum_in.at[k],
            device_id={"exp": side(k)}, device_id_type=MESH,
        )

    def go_copy(k, j):
        to = ahead(k, j)
        return pltpu.make_async_remote_copy(
            src_ref=rows_send.at[to], dst_ref=rows_recv.at[seq_index],
            send_sem=go_out.at[k * LINE + j], recv_sem=go_in.at[k * LINE + j],
            device_id={"seq": to}, device_id_type=MESH,
        )

    def back_copy(k, j):
        to = behind(k, j)
        return pltpu.make_async_remote_copy(
            src_ref=made.at[to], dst_ref=rows_back.at[seq_index],
            send_sem=back_out.at[k * LINE + j], recv_sem=back_in.at[k * LINE + j],
            device_id={"seq": to}, device_id_type=MESH,
        )

    barrier = pltpu.get_barrier_semaphore()
    for k in range(1, 4):
        pl.semaphore_signal(barrier, inc=1, device_id={"exp": side(k)}, device_id_type=MESH)

    @pl.loop(1, EXPERTS)
    def _(n):
        pl.semaphore_signal(
            barrier, inc=1, device_id={"seq": ahead(n // LINE, n % LINE)}, device_id_type=MESH
        )

    product[...] = jnp.dot(att_ref[...], ow_ref[...], preferred_element_type=jnp.float32).reshape(product.shape)
    for k in range(1, 4):
        sum_send[k] = product[side(k)].astype(jnp.bfloat16)
    pl.semaphore_wait(barrier, 3 + EXPERTS - 1)
    for k in range(1, 4):
        sum_copy(k).start()
    mixed = product[exp_index]
    for k in range(1, 4):
        sum_copy(k).wait_recv()
        mixed = mixed + sum_recv[k].astype(jnp.float32)
    rows = pl.ds(pl.multiple_of(exp_index * 64, 64), 64)
    after = hid_ref[rows, :].astype(jnp.float32) + residual_scale * mixed
    residual[...] = after
    spread = lax.rsqrt(jnp.mean(after * after, axis=-1, keepdims=True) + norm_epsilon)
    moe_in[...] = (after * spread * gain_ref[...]).astype(jnp.bfloat16)

    @pl.loop(0, PLANES)
    def _(k):
        to = lax.rem(plane + k, PLANES)
        pick = chosen_ref[pl.ds(pl.multiple_of(to * 256, 256), 256), :]
        picked = jnp.dot(pick, moe_in[...], preferred_element_type=jnp.float32).astype(jnp.bfloat16)
        rows_send[pl.ds(to * LINE, LINE)] = picked.reshape(LINE, CAP, -1)

        @pl.loop(jnp.where(k == 0, 1, 0), LINE)
        def _(j):
            go_copy(k, j).start()

        @pl.when(k == 0)
        def _():
            rows_recv[seq_index] = rows_send[seq_index]

    @pl.loop(0, PLANES)
    def _(k):
        first = jnp.where(k == 0, 1, 0)
        origin = lax.rem(plane + PLANES - k, PLANES)

        @pl.loop(first, LINE)
        def _(j):
            go_copy(k, j).wait_recv()

        arrived = rows_recv[pl.ds(origin * LINE, LINE)].reshape(LINE * CAP, -1)
        hidden = jnp.dot(arrived, win_ref[...], preferred_element_type=jnp.float32)
        gate, up = hidden[:, :512], hidden[:, 512:]
        active = (gate / (1.0 + jnp.exp(-gate)) * up).astype(jnp.bfloat16)
        done = jnp.dot(active, wout_ref[...], preferred_element_type=jnp.float32).astype(jnp.bfloat16)
        made[pl.ds(origin * LINE, LINE)] = done.reshape(LINE, CAP, -1)

        @pl.loop(first, LINE)
        def _(j):
            back_copy(k, j).start()

        @pl.when(k == 0)
        def _():
            rows_back[seq_index] = made[seq_index]

    total[...] = jnp.zeros_like(total)

    @pl.loop(0, PLANES)
    def _(k):
        @pl.loop(jnp.where(k == 0, 1, 0), LINE)
        def _(j):
            back_copy(k, j).wait_recv()

        owner = lax.rem(plane + k, PLANES)
        mix = mix_ref[:, pl.ds(pl.multiple_of(owner * 256, 256), 256)]
        total[...] += jnp.dot(
            mix, rows_back[pl.ds(owner * LINE, LINE)].reshape(LINE * CAP, -1), preferred_element_type=jnp.float32
        )

    out_ref[...] = (residual[...] + residual_scale * (total[:64] + total[64:])).astype(jnp.bfloat16)

    for k in range(1, 4):
        sum_copy(k).wait_send()

    @pl.loop(1, EXPERTS)
    def _(n):
        go_copy(n // LINE, n % LINE).wait_send()
        back_copy(n // LINE, n % LINE).wait_send()


def experts(*operands):
    vmem = pl.BlockSpec(memory_space=pltpu.VMEM)
    width = 1536
    block = pltpu.VMEM((EXPERTS, CAP, width), jnp.bfloat16)
    return pl.pallas_call(
        experts_kernel,
        out_shape=jax.ShapeDtypeStruct((64, width), jnp.bfloat16),
        in_specs=[vmem] * 8,
        out_specs=vmem,
        scratch_shapes=[
            pltpu.VMEM((4, 64, width), jnp.float32),
            pltpu.VMEM((4, 64, width), jnp.bfloat16),
            pltpu.VMEM((4, 64, width), jnp.bfloat16),
            pltpu.VMEM((64, width), jnp.float32),
            pltpu.VMEM((64, width), jnp.bfloat16),
            block,
            block,
            block,
            block,
            pltpu.VMEM((128, width), jnp.float32),
        ]
        + [pltpu.SemaphoreType.DMA((n,)) for n in (4, 4, 32, 32, 32, 32)],
        compiler_params=pltpu.CompilerParams(
            vmem_limit_bytes=48 * 1024 * 1024, collective_id=2, has_side_effects=True
        ),
        name="experts",
    )(*operands)


def pages(pairs_new, page_slot, seq_index):
    seq_count = 32
    blocks_here = ROWS // PAGE
    outgoing = pairs_new.reshape(seq_count, PAGE * 256)
    received = lax.all_to_all(outgoing, "seq", split_axis=0, concat_axis=0, tiled=True)
    slots = lax.dynamic_index_in_dim(page_slot.reshape(seq_count, seq_count), seq_index, 1, keepdims=False)
    place = (slots[None, :] == jnp.arange(blocks_here, dtype=jnp.int32)[:, None]).astype(jnp.bfloat16)
    placed = jnp.dot(place, received, preferred_element_type=jnp.float32).astype(jnp.bfloat16)
    page_rows = placed.reshape(blocks_here, PAGE, KV_HERE, 2, HEAD_DIM).transpose(0, 2, 3, 1, 4)
    return page_rows.reshape(blocks_here, KV_HERE, 2, PAGE * HEAD_DIM)


def body(
    hidden_in,
    attn_gain,
    q_weight,
    k_weight,
    v_weight,
    o_weight,
    cache_kv,
    moe_gain,
    expert_in,
    expert_out,
    routes,
    route_prob,
    page_slot,
):
    seq_index = lax.axis_index("seq")
    normed = rms_norm(hidden_in, attn_gain)
    pair_weight = jnp.concatenate(
        [k_weight[:, :64], v_weight[:, :64], k_weight[:, 64:], v_weight[:, 64:]], axis=1
    )
    pairs_new = jnp.dot(normed, pair_weight, preferred_element_type=jnp.float32).astype(jnp.bfloat16)
    queries = jnp.dot(normed, q_weight, preferred_element_type=jnp.float32).astype(jnp.bfloat16)
    attended = attend(queries, cache_kv, pairs_new)
    page_rows = pages(pairs_new, page_slot, seq_index)

    moe_rows = routes.shape[0]
    named = (routes[:, :, None] == jnp.arange(EXPERTS, dtype=jnp.int32)).astype(jnp.float32)
    hit = jnp.sum(named, axis=1)
    share = route_prob / jnp.sum(route_prob, axis=-1, keepdims=True)
    share_of = jnp.sum(named * share[..., None], axis=1)
    before = jnp.tril(jnp.ones((moe_rows, moe_rows), jnp.bfloat16), -1)
    rank = jnp.dot(before, hit.astype(jnp.bfloat16), preferred_element_type=jnp.float32)
    slot = jnp.arange(CAP, dtype=jnp.float32)
    chosen = jnp.where(hit[..., None] > 0, (rank[..., None] == slot).astype(jnp.float32), 0.0)
    chosen = chosen.reshape(moe_rows, EXPERTS * CAP)
    mixing = chosen * jnp.repeat(share_of, CAP, axis=1)
    high = mixing.astype(jnp.bfloat16)
    low = (mixing - high.astype(jnp.float32)).astype(jnp.bfloat16)
    hidden_out = experts(
        attended,
        o_weight,
        hidden_in,
        moe_gain[None, :],
        chosen.astype(jnp.bfloat16).T,
        jnp.concatenate([high, low], axis=0),
        expert_in[0],
        expert_out[0],
    )
    return (hidden_out, page_rows)


def solution(mesh):
    return jax.shard_map(
        body,
        mesh=mesh,
        in_specs=(
            P("seq", None),
            P(),
            P(None, "exp"),
            P(None, "exp"),
            P(None, "exp"),
            P("exp", None),
            P("seq", "exp"),
            P(),
            P("seq", None, None),
            P("seq", None, None),
            P(("seq", "exp"), None),
            P(("seq", "exp"), None),
            P(),
        ),
        out_specs=(P(("seq", "exp"), None), P("seq", "exp", None, None)),
        check_vma=False,
    )
```

```python
import functools

import jax
import jax.numpy as jnp
from jax import lax
from jax.experimental import pallas as pl
from jax.experimental.pallas import tpu as pltpu
from jax.sharding import PartitionSpec as P

HEADS_HERE = 6
KV_HERE = 2
GROUP = 3
HEAD_DIM = 64
EXPERTS = 32
CAP = 32
PAGE = 8
PLANES = 4
LINE = 8
ROWS = 256
CACHE_HERE = 512

norm_epsilon = 1e-06
attention_scale = 0.015625
residual_scale = 0.22
masked_score = -1e30


NEAR = ((0, 0), (0, 1), (1, 0), (0, 3), (1, 1), (0, 2), (1, 3), (1, 2))


def attend_kernel(
    hid_ref, gain_ref, qw_ref, kw_ref, vw_ref, cache_ref, slot_ref, out_ref, page_ref,
    normed, query, q_all, cache_all, new_own, new_all, cache_val, new_val, qs, best, acc,
    part_send, part_recv, page_send, page_recv,
    q_out, q_in, cache_out, cache_in, new_out, new_in, part_out, part_in, page_out, page_in,
):
    seq_index = lax.axis_index("seq")
    plane = seq_index // LINE
    place = seq_index % LINE
    even = plane % 2 == 0
    MESH = pl.DeviceIdType.MESH
    lane = lax.broadcasted_iota(jnp.int32, (ROWS, 2 * HEAD_DIM), 1)
    low = lane < HEAD_DIM
    one = jnp.ones((), jnp.bfloat16)

    def send(source, target, out_sem, in_sem, to):
        return pltpu.make_async_remote_copy(
            src_ref=source, dst_ref=target, send_sem=out_sem, recv_sem=in_sem,
            device_id={"seq": to}, device_id_type=MESH,
        )

    def peer(n):
        h, x = NEAR[n]
        return plane * LINE + lax.rem(place // 4 + h, 2) * 4 + lax.rem(place % 4 + x, 4)

    def line_peer(k):
        return lax.rem(plane + k, PLANES) * LINE + place

    def ahead(n):
        return lax.rem(seq_index + n, 32)

    def cache_copy(n):
        rows = pl.ds((n % 2) * CACHE_HERE, CACHE_HERE)
        return send(cache_ref, cache_all.at[n // 2, rows], cache_out.at[n], cache_in.at[n], peer(n))

    def new_copy(n):
        return send(new_own, new_all.at[place], new_out.at[n], new_in.at[n], peer(n))

    def query_copy(k):
        return send(query, q_all.at[plane], q_out.at[k], q_in.at[k], line_peer(k))

    def part_copy(k):
        return send(part_send.at[k], part_recv.at[k], part_out.at[k], part_in.at[k], line_peer(k))

    def page_copy(n):
        rows = pl.ds(pl.multiple_of(ahead(n) * PAGE, PAGE), PAGE)
        return send(page_send.at[rows], page_recv.at[seq_index], page_out.at[n], page_in.at[n], ahead(n))

    def sends_query(k):
        return jnp.logical_or(plane < 2, plane == 3) if k == 3 else plane < 2

    def gets_query(k):
        origin = lax.rem(plane + PLANES - k, PLANES)
        return jnp.logical_or(origin < 2, origin == 3) if k == 3 else origin < 2

    def sends_part(k):
        target = lax.rem(plane + k, PLANES)
        return jnp.logical_or(target < 2, target == 3) if k == 1 else target < 2

    def gets_part(k):
        return jnp.logical_or(plane < 2, plane == 3) if k == 1 else plane < 2

    barrier = pltpu.get_barrier_semaphore()

    @pl.loop(1, 32)
    def _(n):
        pl.semaphore_signal(barrier, inc=1, device_id={"seq": ahead(n)}, device_id_type=MESH)

    cache_all[0, :CACHE_HERE] = cache_ref[...]
    for k in range(1, PLANES):
        @pl.when(jnp.logical_not(gets_part(k)))
        def _():
            part_recv[k, :, :384] = jnp.zeros((ROWS, 384), jnp.bfloat16)
            part_recv[k, :, 384:] = jnp.full((ROWS, 128), masked_score, jnp.bfloat16)

    pl.semaphore_wait(barrier, 31)
    for n in range(1, 4):
        cache_copy(n).start()

    @pl.loop(0, ROWS // 64)
    def _(step):
        rows = pl.ds(pl.multiple_of(step * 64, 64), 64)
        wide = hid_ref[rows, :].astype(jnp.float32)
        spread = lax.rsqrt(jnp.mean(wide * wide, axis=-1, keepdims=True) + norm_epsilon)
        normed[rows, :] = (wide * spread * gain_ref[...]).astype(jnp.bfloat16)

    query[...] = jnp.dot(normed[...], qw_ref[...], preferred_element_type=jnp.float32).astype(jnp.bfloat16)
    for k in range(1, PLANES):
        @pl.when(sends_query(k))
        def _():
            query_copy(k).start()

    keys = jnp.dot(normed[...], kw_ref[...], preferred_element_type=jnp.float32)
    values = jnp.dot(normed[...], vw_ref[...], preferred_element_type=jnp.float32)
    slabs = [
        jnp.where(low, keys, pltpu.roll(values, HEAD_DIM, 1)).astype(jnp.bfloat16),
        jnp.where(low, pltpu.roll(keys, HEAD_DIM, 1), values).astype(jnp.bfloat16),
    ]
    for g in range(KV_HERE):
        new_own[:, g * 128 : (g + 1) * 128] = slabs[g]
        page_send[:, g * 128 : (g + 1) * 128] = slabs[g].astype(jnp.float32)
    for n in range(1, LINE):
        new_copy(n).start()
    for n in range(4, LINE):
        cache_copy(n).start()

    @pl.loop(1, 32)
    def _(n):
        page_copy(n).start()

    q_all[plane] = query[...]
    new_all[place] = new_own[...]
    own_rows = pl.ds(pl.multiple_of(seq_index * PAGE, PAGE), PAGE)
    page_recv[seq_index] = page_send[own_rows, :]
    best[...] = jnp.full_like(best, masked_score)
    acc[...] = jnp.zeros_like(acc)

    def prepare(t):
        for h in range(HEADS_HERE):
            slab = q_all[t, :, (h // 2) * 128 : (h // 2 + 1) * 128]
            slab = slab.astype(jnp.float32) * attention_scale
            if h % 2:
                slab = pltpu.roll(slab, HEAD_DIM, 1)
            a = h % GROUP
            qs[t, h // GROUP, a * ROWS : (a + 1) * ROWS, :] = jnp.where(low, slab, 0.0).astype(jnp.bfloat16)

    def slab_of(g):
        return slice(g * 128, (g + 1) * 128)

    def update(turns, keys_of, values_of, first_key=None):
        chains = [(t, g, slice(a * ROWS, (a + 1) * ROWS)) for t in turns for g in range(KV_HERE) for a in range(GROUP)]
        raw = [
            lax.dot_general(
                qs[t, g, rows, :], keys_of(g), (((1,), (1,)), ((), ())), preferred_element_type=jnp.float32
            )
            for t, g, rows in chains
        ]
        for (t, g, rows), scores in zip(chains, raw):
            if first_key is not None:
                r = lax.broadcasted_iota(jnp.int32, scores.shape, 0)
                c = lax.broadcasted_iota(jnp.int32, scores.shape, 1)
                scores = jnp.where(c - r <= place * ROWS - first_key, scores, masked_score)
            old = best[t, g, rows, :]
            new = jnp.maximum(old, jnp.max(scores, axis=-1, keepdims=True))
            best[t, g, rows, :] = new
            weights = jnp.exp(scores - new[:, :1]).astype(jnp.bfloat16)
            acc[t, g, rows, :] = acc[t, g, rows, :] * jnp.exp(old - new) + jnp.dot(
                weights, values_of(g), preferred_element_type=jnp.float32
            )

    prepare(plane)
    for k in range(1, PLANES):
        @pl.when(gets_query(k))
        def _():
            query_copy(k).wait_recv()
            prepare(lax.rem(plane + PLANES - k, PLANES))

    def cache_pair(m):
        for part in range(4):
            rows = slice(part * ROWS, (part + 1) * ROWS)
            for g in range(KV_HERE):
                cache_val[rows, slab_of(g)] = jnp.where(low, one, cache_all[m, rows, slab_of(g)])
        update((0, 1), lambda g: cache_all[m, :, slab_of(g)], lambda g: cache_val[:, slab_of(g)])

    def cache_pairs(start):
        @pl.loop(start, start + 2)
        def _(m):
            @pl.when(m > 0)
            def _():
                send(
                    cache_ref, cache_all.at[m, pl.ds(0, CACHE_HERE)],
                    cache_out.at[2 * m], cache_in.at[2 * m], peer(1),
                ).wait_recv()

            send(
                cache_ref, cache_all.at[m, pl.ds(CACHE_HERE, CACHE_HERE)],
                cache_out.at[2 * m + 1], cache_in.at[2 * m + 1], peer(1),
            ).wait_recv()
            cache_pair(m)

    cache_pairs(0)
    for n in range(1, LINE):
        h, x = NEAR[n]
        origin = lax.rem(place // 4 + h, 2) * 4 + lax.rem(place % 4 + 4 - x, 4)
        send(new_own, new_all.at[origin], new_out.at[n], new_in.at[n], peer(n)).wait_recv()

    @pl.loop(0, LINE)
    def _(n):
        for g in range(KV_HERE):
            new_val[n, :, slab_of(g)] = jnp.where(low, one, new_all[n, :, slab_of(g)])

    def new_keys(step):
        return lambda g: new_all[pl.ds(step * 4, 4), :, slab_of(g)].reshape(1024, 128)

    def new_values(step):
        return lambda g: new_val[pl.ds(step * 4, 4), :, slab_of(g)].reshape(1024, 128)

    @pl.loop(0, place // 4 + 1)
    def _(step):
        update((plane,), new_keys(step), new_values(step), step * 1024)

    @pl.loop(0, jnp.where(even, 2, 0))
    def _(step):
        update((plane + 1,), new_keys(step), new_values(step))

    cache_pairs(2)

    def finish(t):
        heads = []
        for h in range(HEADS_HERE):
            g, rows = h // GROUP, slice((h % GROUP) * ROWS, (h % GROUP + 1) * ROWS)
            part = acc[t, g, rows, :]
            total = part[:, :1]
            heads.append((part / total, best[t, g, rows, :] + jnp.log(total)))
        levels = jnp.zeros((ROWS, 128), jnp.float32)
        for h in range(HEADS_HERE):
            levels = jnp.where(lane % 8 == h, heads[h][1], levels)
        return [
            jnp.where(low, pltpu.roll(heads[2 * p][0], HEAD_DIM, 1), heads[2 * p + 1][0])
            for p in range(HEADS_HERE // 2)
        ], levels

    for k in range(1, PLANES):
        @pl.when(sends_part(k))
        def _():
            pairs, levels = finish(lax.rem(plane + k, PLANES))
            for p in range(HEADS_HERE // 2):
                part_send[k, :, p * 128 : (p + 1) * 128] = pairs[p].astype(jnp.bfloat16)
            high = levels.astype(jnp.bfloat16).astype(jnp.float32)
            rest = levels - high
            middle = rest.astype(jnp.bfloat16).astype(jnp.float32)
            split = jnp.where(lane < 8, high, jnp.where(lane < 16, middle, rest - middle))
            part_send[k, :, 384:512] = split.astype(jnp.bfloat16)
            part_copy(k).start()

    @pl.loop(1, 32)
    def _(n):
        page_copy(n).wait_recv()

    column = lax.broadcasted_iota(jnp.int32, (32, 32), 1)
    slots = jnp.sum(
        jnp.where(column == seq_index, slot_ref[...].astype(jnp.float32), 0.0), axis=1, keepdims=True
    )
    owner = (slots == column.astype(jnp.float32)).astype(jnp.bfloat16)
    low_page = lax.broadcasted_iota(jnp.int32, (32, 128), 1) < HEAD_DIM
    tokens = [
        lax.dot_general(
            owner, page_recv[:, n, :].astype(jnp.bfloat16), (((0,), (0,)), ((), ())),
            preferred_element_type=jnp.float32,
        )
        for n in range(PAGE)
    ]
    for g in range(KV_HERE):
        for n in range(0, PAGE, 2):
            first, second = tokens[n][:, slab_of(g)], tokens[n + 1][:, slab_of(g)]
            cols = slice(n * HEAD_DIM, (n + 2) * HEAD_DIM)
            page_ref[2 * g, :, cols] = jnp.where(low_page, first, pltpu.roll(second, HEAD_DIM, 1)).astype(jnp.bfloat16)
            page_ref[2 * g + 1, :, cols] = jnp.where(low_page, pltpu.roll(first, HEAD_DIM, 1), second).astype(jnp.bfloat16)

    pairs, own_level = finish(plane)
    for k in range(1, PLANES):
        @pl.when(gets_part(k))
        def _():
            part_copy(k).wait_recv()
    levels = [own_level]
    for k in range(1, PLANES):
        slab = part_recv[k, :, 384:512].astype(jnp.float32)
        levels.append(slab + pltpu.roll(slab, 120, 1) + pltpu.roll(slab, 112, 1))
    top = functools.reduce(jnp.maximum, levels)
    shares = [jnp.exp(level - top) for level in levels]
    whole = functools.reduce(jnp.add, shares)
    shares = [share / whole for share in shares]

    def spread(share, p):
        return jnp.where(low, share[:, 2 * p : 2 * p + 1], share[:, 2 * p + 1 : 2 * p + 2])

    for p in range(HEADS_HERE // 2):
        cols = slice(p * 128, (p + 1) * 128)
        value = pairs[p] * spread(shares[0], p)
        for k in range(1, PLANES):
            value = value + part_recv[k, :, cols].astype(jnp.float32) * spread(shares[k], p)
        out_ref[:, cols] = value.astype(jnp.bfloat16)

    for n in range(1, LINE):
        cache_copy(n).wait_send()
        new_copy(n).wait_send()

    for k in range(1, PLANES):
        @pl.when(sends_query(k))
        def _():
            query_copy(k).wait_send()

        @pl.when(sends_part(k))
        def _():
            part_copy(k).wait_send()

    @pl.loop(1, 32)
    def _(n):
        page_copy(n).wait_send()


def attend(*operands):
    vmem = pl.BlockSpec(memory_space=pltpu.VMEM)
    state = pltpu.VMEM((PLANES, KV_HERE, GROUP * ROWS, 128), jnp.float32)
    return pl.pallas_call(
        attend_kernel,
        out_shape=[
            jax.ShapeDtypeStruct((ROWS, 384), jnp.bfloat16),
            jax.ShapeDtypeStruct((2 * KV_HERE, ROWS // PAGE, PAGE * HEAD_DIM), jnp.bfloat16),
        ],
        in_specs=[vmem] * 7,
        out_specs=[vmem] * 2,
        scratch_shapes=[
            pltpu.VMEM((ROWS, 1536), jnp.bfloat16),
            pltpu.VMEM((ROWS, 384), jnp.bfloat16),
            pltpu.VMEM((PLANES, ROWS, 384), jnp.bfloat16),
            pltpu.VMEM((LINE // 2, 2 * CACHE_HERE, 256), jnp.bfloat16),
            pltpu.VMEM((ROWS, 256), jnp.bfloat16),
            pltpu.VMEM((LINE, ROWS, 256), jnp.bfloat16),
            pltpu.VMEM((2 * CACHE_HERE, 256), jnp.bfloat16),
            pltpu.VMEM((LINE, ROWS, 256), jnp.bfloat16),
            pltpu.VMEM((PLANES, KV_HERE, GROUP * ROWS, 128), jnp.bfloat16),
            state,
            state,
            pltpu.VMEM((PLANES, ROWS, 512), jnp.bfloat16),
            pltpu.VMEM((PLANES, ROWS, 512), jnp.bfloat16),
            pltpu.VMEM((ROWS, 256), jnp.float32),
            pltpu.VMEM((ROWS // PAGE, PAGE, 256), jnp.float32),
        ]
        + [pltpu.SemaphoreType.DMA((n,)) for n in (4, 4, 8, 8, 8, 8, 4, 4, 32, 32)],
        compiler_params=pltpu.CompilerParams(
            vmem_limit_bytes=52 * 1024 * 1024, collective_id=1, has_side_effects=True
        ),
        name="attend",
    )(*operands)


def experts_kernel(
    att_ref, ow_ref, hid_ref, gain_ref, chosen_ref, mix_ref, win_ref, wout_ref, out_ref,
    product, sum_send, sum_recv, residual, moe_in, rows_send, rows_recv, made, rows_back, total,
    sum_out, sum_in, go_out, go_in, back_out, back_in,
):
    seq_index = lax.axis_index("seq")
    exp_index = lax.axis_index("exp")
    plane = seq_index // LINE
    place = seq_index % LINE
    MESH = pl.DeviceIdType.MESH

    def ahead(k, j):
        return lax.rem(plane + k, PLANES) * LINE + lax.rem(place + j, LINE)

    def behind(k, j):
        return lax.rem(plane + PLANES - k, PLANES) * LINE + lax.rem(place + LINE - j, LINE)

    def side(k):
        return lax.rem(exp_index + k, 4)

    def sum_copy(k):
        return pltpu.make_async_remote_copy(
            src_ref=sum_send.at[k], dst_ref=sum_recv.at[k], send_sem=sum_out.at[k], recv_sem=sum_in.at[k],
            device_id={"exp": side(k)}, device_id_type=MESH,
        )

    def go_copy(k, j):
        to = ahead(k, j)
        return pltpu.make_async_remote_copy(
            src_ref=rows_send.at[to], dst_ref=rows_recv.at[seq_index],
            send_sem=go_out.at[k * LINE + j], recv_sem=go_in.at[k * LINE + j],
            device_id={"seq": to}, device_id_type=MESH,
        )

    def back_copy(k, j):
        to = behind(k, j)
        return pltpu.make_async_remote_copy(
            src_ref=made.at[to], dst_ref=rows_back.at[seq_index],
            send_sem=back_out.at[k * LINE + j], recv_sem=back_in.at[k * LINE + j],
            device_id={"seq": to}, device_id_type=MESH,
        )

    barrier = pltpu.get_barrier_semaphore()
    for k in range(1, 4):
        pl.semaphore_signal(barrier, inc=1, device_id={"exp": side(k)}, device_id_type=MESH)

    @pl.loop(1, EXPERTS)
    def _(n):
        pl.semaphore_signal(
            barrier, inc=1, device_id={"seq": ahead(n // LINE, n % LINE)}, device_id_type=MESH
        )

    product[...] = jnp.dot(att_ref[...], ow_ref[...], preferred_element_type=jnp.float32).reshape(product.shape)
    for k in range(1, 4):
        sum_send[k] = product[side(k)].astype(jnp.bfloat16)
    pl.semaphore_wait(barrier, 3 + EXPERTS - 1)
    for k in range(1, 4):
        sum_copy(k).start()
    mixed = product[exp_index]
    for k in range(1, 4):
        sum_copy(k).wait_recv()
        mixed = mixed + sum_recv[k].astype(jnp.float32)
    rows = pl.ds(pl.multiple_of(exp_index * 64, 64), 64)
    after = hid_ref[rows, :].astype(jnp.float32) + residual_scale * mixed
    residual[...] = after
    spread = lax.rsqrt(jnp.mean(after * after, axis=-1, keepdims=True) + norm_epsilon)
    moe_in[...] = (after * spread * gain_ref[...]).astype(jnp.bfloat16)

    @pl.loop(0, PLANES)
    def _(k):
        to = lax.rem(plane + k, PLANES)
        pick = chosen_ref[pl.ds(pl.multiple_of(to * 256, 256), 256), :]
        picked = jnp.dot(pick, moe_in[...], preferred_element_type=jnp.float32).astype(jnp.bfloat16)
        rows_send[pl.ds(to * LINE, LINE)] = picked.reshape(LINE, CAP, -1)

        @pl.loop(jnp.where(k == 0, 1, 0), LINE)
        def _(j):
            go_copy(k, j).start()

        @pl.when(k == 0)
        def _():
            rows_recv[seq_index] = rows_send[seq_index]

    @pl.loop(0, PLANES)
    def _(k):
        first = jnp.where(k == 0, 1, 0)
        origin = lax.rem(plane + PLANES - k, PLANES)

        @pl.loop(first, LINE)
        def _(j):
            go_copy(k, j).wait_recv()

        arrived = rows_recv[pl.ds(origin * LINE, LINE)].reshape(LINE * CAP, -1)
        hidden = jnp.dot(arrived, win_ref[...], preferred_element_type=jnp.float32)
        gate, up = hidden[:, :512], hidden[:, 512:]
        active = (gate / (1.0 + jnp.exp(-gate)) * up).astype(jnp.bfloat16)
        done = jnp.dot(active, wout_ref[...], preferred_element_type=jnp.float32).astype(jnp.bfloat16)
        made[pl.ds(origin * LINE, LINE)] = done.reshape(LINE, CAP, -1)

        @pl.loop(first, LINE)
        def _(j):
            back_copy(k, j).start()

        @pl.when(k == 0)
        def _():
            rows_back[seq_index] = made[seq_index]

    total[...] = jnp.zeros_like(total)

    @pl.loop(0, PLANES)
    def _(k):
        @pl.loop(jnp.where(k == 0, 1, 0), LINE)
        def _(j):
            back_copy(k, j).wait_recv()

        owner = lax.rem(plane + k, PLANES)
        mix = mix_ref[:, pl.ds(pl.multiple_of(owner * 256, 256), 256)]
        total[...] += jnp.dot(
            mix, rows_back[pl.ds(owner * LINE, LINE)].reshape(LINE * CAP, -1), preferred_element_type=jnp.float32
        )

    out_ref[...] = (residual[...] + residual_scale * (total[:64] + total[64:])).astype(jnp.bfloat16)

    for k in range(1, 4):
        sum_copy(k).wait_send()

    @pl.loop(1, EXPERTS)
    def _(n):
        go_copy(n // LINE, n % LINE).wait_send()
        back_copy(n // LINE, n % LINE).wait_send()


def experts(*operands):
    vmem = pl.BlockSpec(memory_space=pltpu.VMEM)
    width = 1536
    block = pltpu.VMEM((EXPERTS, CAP, width), jnp.bfloat16)
    return pl.pallas_call(
        experts_kernel,
        out_shape=jax.ShapeDtypeStruct((64, width), jnp.bfloat16),
        in_specs=[vmem] * 8,
        out_specs=vmem,
        scratch_shapes=[
            pltpu.VMEM((4, 64, width), jnp.float32),
            pltpu.VMEM((4, 64, width), jnp.bfloat16),
            pltpu.VMEM((4, 64, width), jnp.bfloat16),
            pltpu.VMEM((64, width), jnp.float32),
            pltpu.VMEM((64, width), jnp.bfloat16),
            block,
            block,
            block,
            block,
            pltpu.VMEM((128, width), jnp.float32),
        ]
        + [pltpu.SemaphoreType.DMA((n,)) for n in (4, 4, 32, 32, 32, 32)],
        compiler_params=pltpu.CompilerParams(
            vmem_limit_bytes=48 * 1024 * 1024, collective_id=2, has_side_effects=True
        ),
        name="experts",
    )(*operands)


def body(
    hidden_in,
    attn_gain,
    q_weight,
    k_weight,
    v_weight,
    o_weight,
    cache_kv,
    moe_gain,
    expert_in,
    expert_out,
    routes,
    route_prob,
    page_slot,
):
    attended, page_slabs = attend(
        hidden_in, attn_gain[None, :], q_weight, k_weight, v_weight, cache_kv, page_slot.reshape(32, 32)
    )
    page_rows = page_slabs.transpose(1, 0, 2).reshape(ROWS // PAGE, KV_HERE, 2, PAGE * HEAD_DIM)

    moe_rows = routes.shape[0]
    named = (routes[:, :, None] == jnp.arange(EXPERTS, dtype=jnp.int32)).astype(jnp.float32)
    hit = jnp.sum(named, axis=1)
    share = route_prob / jnp.sum(route_prob, axis=-1, keepdims=True)
    share_of = jnp.sum(named * share[..., None], axis=1)
    before = jnp.tril(jnp.ones((moe_rows, moe_rows), jnp.bfloat16), -1)
    rank = jnp.dot(before, hit.astype(jnp.bfloat16), preferred_element_type=jnp.float32)
    slot = jnp.arange(CAP, dtype=jnp.float32)
    chosen = jnp.where(hit[..., None] > 0, (rank[..., None] == slot).astype(jnp.float32), 0.0)
    chosen = chosen.reshape(moe_rows, EXPERTS * CAP)
    mixing = chosen * jnp.repeat(share_of, CAP, axis=1)
    high = mixing.astype(jnp.bfloat16)
    low = (mixing - high.astype(jnp.float32)).astype(jnp.bfloat16)
    hidden_out = experts(
        attended,
        o_weight,
        hidden_in,
        moe_gain[None, :],
        chosen.astype(jnp.bfloat16).T,
        jnp.concatenate([high, low], axis=0),
        expert_in[0],
        expert_out[0],
    )
    return (hidden_out, page_rows)


def solution(mesh):
    return jax.shard_map(
        body,
        mesh=mesh,
        in_specs=(
            P("seq", None),
            P(),
            P(None, "exp"),
            P(None, "exp"),
            P(None, "exp"),
            P("exp", None),
            P("seq", "exp"),
            P(),
            P("seq", None, None),
            P("seq", None, None),
            P(("seq", "exp"), None),
            P(("seq", "exp"), None),
            P(),
        ),
        out_specs=(P(("seq", "exp"), None), P("seq", "exp", None, None)),
        check_vma=False,
    )
```

```python
import functools

import jax
import jax.numpy as jnp
from jax import lax
from jax.experimental import pallas as pl
from jax.experimental.pallas import tpu as pltpu
from jax.sharding import PartitionSpec as P

HEADS_HERE = 6
KV_HERE = 2
GROUP = 3
HEAD_DIM = 64
EXPERTS = 32
CAP = 32
PAGE = 8
PLANES = 4
LINE = 8
ROWS = 256
CACHE_HERE = 512

norm_epsilon = 1e-06
attention_scale = 0.015625
residual_scale = 0.22
masked_score = -1e30


NEAR = ((0, 0), (0, 1), (1, 0), (0, 3), (1, 1), (0, 2), (1, 3), (1, 2))


def attend_kernel(
    hid_ref, gain_ref, qw_ref, kw_ref, vw_ref, cache_ref, slot_ref, out_ref, page_ref,
    normed, query, q_all, cache_all, new_own, new_all, cache_val, new_val, qs, best, acc,
    part_send, part_recv, page_send, page_recv,
    q_out, q_in, cache_out, cache_in, new_out, new_in, part_out, part_in, page_out, page_in,
):
    seq_index = lax.axis_index("seq")
    plane = seq_index // LINE
    place = seq_index % LINE
    even = plane % 2 == 0
    MESH = pl.DeviceIdType.MESH
    lane = lax.broadcasted_iota(jnp.int32, (ROWS, 2 * HEAD_DIM), 1)
    low = lane < HEAD_DIM
    one = jnp.ones((), jnp.bfloat16)

    def send(source, target, out_sem, in_sem, to):
        return pltpu.make_async_remote_copy(
            src_ref=source, dst_ref=target, send_sem=out_sem, recv_sem=in_sem,
            device_id={"seq": to}, device_id_type=MESH,
        )

    def peer(n):
        h, x = NEAR[n]
        return plane * LINE + lax.rem(place // 4 + h, 2) * 4 + lax.rem(place % 4 + x, 4)

    def line_peer(k):
        return lax.rem(plane + k, PLANES) * LINE + place

    def ahead(n):
        return lax.rem(seq_index + n, 32)

    def cache_copy(n):
        rows = pl.ds((n % 2) * CACHE_HERE, CACHE_HERE)
        return send(cache_ref, cache_all.at[n // 2, rows], cache_out.at[n], cache_in.at[n], peer(n))

    def new_copy(n):
        return send(new_own, new_all.at[place], new_out.at[n], new_in.at[n], peer(n))

    def query_copy(k):
        return send(query, q_all.at[plane], q_out.at[k], q_in.at[k], line_peer(k))

    def part_copy(k):
        return send(part_send.at[k], part_recv.at[k], part_out.at[k], part_in.at[k], line_peer(k))

    def page_copy(n):
        rows = pl.ds(pl.multiple_of(ahead(n) * PAGE, PAGE), PAGE)
        return send(page_send.at[rows], page_recv.at[seq_index], page_out.at[n], page_in.at[n], ahead(n))

    def sends_query(k):
        return jnp.logical_or(plane < 2, plane == 3) if k == 3 else plane < 2

    def gets_query(k):
        origin = lax.rem(plane + PLANES - k, PLANES)
        return jnp.logical_or(origin < 2, origin == 3) if k == 3 else origin < 2

    def sends_part(k):
        target = lax.rem(plane + k, PLANES)
        return jnp.logical_or(target < 2, target == 3) if k == 1 else target < 2

    def gets_part(k):
        return jnp.logical_or(plane < 2, plane == 3) if k == 1 else plane < 2

    barrier = pltpu.get_barrier_semaphore()

    @pl.loop(1, 32)
    def _(n):
        pl.semaphore_signal(barrier, inc=1, device_id={"seq": ahead(n)}, device_id_type=MESH)

    cache_all[0, :CACHE_HERE] = cache_ref[...]
    for k in range(1, PLANES):
        @pl.when(jnp.logical_not(gets_part(k)))
        def _():
            part_recv[k, :, :384] = jnp.zeros((ROWS, 384), jnp.bfloat16)
            part_recv[k, :, 384:] = jnp.full((ROWS, 128), masked_score, jnp.bfloat16)

    pl.semaphore_wait(barrier, 31)
    for n in range(1, 4):
        cache_copy(n).start()

    @pl.loop(0, ROWS // 64)
    def _(step):
        rows = pl.ds(pl.multiple_of(step * 64, 64), 64)
        wide = hid_ref[rows, :].astype(jnp.float32)
        spread = lax.rsqrt(jnp.mean(wide * wide, axis=-1, keepdims=True) + norm_epsilon)
        normed[rows, :] = (wide * spread * gain_ref[...]).astype(jnp.bfloat16)

    query[...] = jnp.dot(normed[...], qw_ref[...], preferred_element_type=jnp.float32).astype(jnp.bfloat16)
    for k in range(1, PLANES):
        @pl.when(sends_query(k))
        def _():
            query_copy(k).start()

    keys = jnp.dot(normed[...], kw_ref[...], preferred_element_type=jnp.float32)
    values = jnp.dot(normed[...], vw_ref[...], preferred_element_type=jnp.float32)
    slabs = [
        jnp.where(low, keys, pltpu.roll(values, HEAD_DIM, 1)).astype(jnp.bfloat16),
        jnp.where(low, pltpu.roll(keys, HEAD_DIM, 1), values).astype(jnp.bfloat16),
    ]
    for g in range(KV_HERE):
        new_own[:, g * 128 : (g + 1) * 128] = slabs[g]
        page_send[:, g * 128 : (g + 1) * 128] = slabs[g].astype(jnp.float32)
    for n in range(1, LINE):
        new_copy(n).start()
    for n in range(4, LINE):
        cache_copy(n).start()

    @pl.loop(1, 32)
    def _(n):
        page_copy(n).start()

    q_all[plane] = query[...]
    new_all[place] = new_own[...]
    own_rows = pl.ds(pl.multiple_of(seq_index * PAGE, PAGE), PAGE)
    page_recv[seq_index] = page_send[own_rows, :]
    best[...] = jnp.full_like(best, masked_score)
    acc[...] = jnp.zeros_like(acc)

    def prepare(t):
        for h in range(HEADS_HERE):
            slab = q_all[t, :, (h // 2) * 128 : (h // 2 + 1) * 128]
            slab = slab.astype(jnp.float32) * attention_scale
            if h % 2:
                slab = pltpu.roll(slab, HEAD_DIM, 1)
            a = h % GROUP
            qs[t, h // GROUP, a * ROWS : (a + 1) * ROWS, :] = jnp.where(low, slab, 0.0).astype(jnp.bfloat16)

    def slab_of(g):
        return slice(g * 128, (g + 1) * 128)

    def update(turns, keys_of, values_of, first_key=None):
        chains = [(t, g, slice(a * ROWS, (a + 1) * ROWS)) for t in turns for g in range(KV_HERE) for a in range(GROUP)]
        raw = [
            lax.dot_general(
                qs[t, g, rows, :], keys_of(g), (((1,), (1,)), ((), ())), preferred_element_type=jnp.float32
            )
            for t, g, rows in chains
        ]
        for (t, g, rows), scores in zip(chains, raw):
            if first_key is not None:
                r = lax.broadcasted_iota(jnp.int32, scores.shape, 0)
                c = lax.broadcasted_iota(jnp.int32, scores.shape, 1)
                scores = jnp.where(c - r <= place * ROWS - first_key, scores, masked_score)
            old = best[t, g, rows, :]
            new = jnp.maximum(old, jnp.max(scores, axis=-1, keepdims=True))
            best[t, g, rows, :] = new
            weights = jnp.exp(scores - new[:, :1]).astype(jnp.bfloat16)
            acc[t, g, rows, :] = acc[t, g, rows, :] * jnp.exp(old - new) + jnp.dot(
                weights, values_of(g), preferred_element_type=jnp.float32
            )

    prepare(plane)
    for k in range(1, PLANES):
        @pl.when(gets_query(k))
        def _():
            query_copy(k).wait_recv()
            prepare(lax.rem(plane + PLANES - k, PLANES))

    def cache_pair(m):
        for part in range(4):
            rows = slice(part * ROWS, (part + 1) * ROWS)
            for g in range(KV_HERE):
                cache_val[rows, slab_of(g)] = jnp.where(low, one, cache_all[m, rows, slab_of(g)])
        update((0, 1), lambda g: cache_all[m, :, slab_of(g)], lambda g: cache_val[:, slab_of(g)])

    def cache_pairs(start):
        @pl.loop(start, start + 2)
        def _(m):
            @pl.when(m > 0)
            def _():
                send(
                    cache_ref, cache_all.at[m, pl.ds(0, CACHE_HERE)],
                    cache_out.at[2 * m], cache_in.at[2 * m], peer(1),
                ).wait_recv()

            send(
                cache_ref, cache_all.at[m, pl.ds(CACHE_HERE, CACHE_HERE)],
                cache_out.at[2 * m + 1], cache_in.at[2 * m + 1], peer(1),
            ).wait_recv()
            cache_pair(m)

    cache_pairs(0)
    for n in range(1, LINE):
        h, x = NEAR[n]
        origin = lax.rem(place // 4 + h, 2) * 4 + lax.rem(place % 4 + 4 - x, 4)
        send(new_own, new_all.at[origin], new_out.at[n], new_in.at[n], peer(n)).wait_recv()

    @pl.loop(0, LINE)
    def _(n):
        for g in range(KV_HERE):
            new_val[n, :, slab_of(g)] = jnp.where(low, one, new_all[n, :, slab_of(g)])

    def new_keys(step):
        return lambda g: new_all[pl.ds(step * 4, 4), :, slab_of(g)].reshape(1024, 128)

    def new_values(step):
        return lambda g: new_val[pl.ds(step * 4, 4), :, slab_of(g)].reshape(1024, 128)

    @pl.loop(0, place // 4 + 1)
    def _(step):
        update((plane,), new_keys(step), new_values(step), step * 1024)

    @pl.loop(0, jnp.where(even, 2, 0))
    def _(step):
        update((plane + 1,), new_keys(step), new_values(step))

    cache_pairs(2)

    def finish(t):
        heads = []
        for h in range(HEADS_HERE):
            g, rows = h // GROUP, slice((h % GROUP) * ROWS, (h % GROUP + 1) * ROWS)
            part = acc[t, g, rows, :]
            total = part[:, :1]
            heads.append((part / total, best[t, g, rows, :] + jnp.log(total)))
        levels = jnp.zeros((ROWS, 128), jnp.float32)
        for h in range(HEADS_HERE):
            levels = jnp.where(lane % 8 == h, heads[h][1], levels)
        return [
            jnp.where(low, pltpu.roll(heads[2 * p][0], HEAD_DIM, 1), heads[2 * p + 1][0])
            for p in range(HEADS_HERE // 2)
        ], levels

    for k in range(1, PLANES):
        @pl.when(sends_part(k))
        def _():
            pairs, levels = finish(lax.rem(plane + k, PLANES))
            for p in range(HEADS_HERE // 2):
                part_send[k, :, p * 128 : (p + 1) * 128] = pairs[p].astype(jnp.bfloat16)
            high = levels.astype(jnp.bfloat16).astype(jnp.float32)
            rest = levels - high
            middle = rest.astype(jnp.bfloat16).astype(jnp.float32)
            split = jnp.where(lane < 8, high, jnp.where(lane < 16, middle, rest - middle))
            part_send[k, :, 384:512] = split.astype(jnp.bfloat16)
            part_copy(k).start()

    @pl.loop(1, 32)
    def _(n):
        page_copy(n).wait_recv()

    column = lax.broadcasted_iota(jnp.int32, (32, 32), 1)
    slots = jnp.sum(
        jnp.where(column == seq_index, slot_ref[...].astype(jnp.float32), 0.0), axis=1, keepdims=True
    )
    owner = (slots == column.astype(jnp.float32)).astype(jnp.bfloat16)
    low_page = lax.broadcasted_iota(jnp.int32, (32, 128), 1) < HEAD_DIM
    tokens = [
        lax.dot_general(
            owner, page_recv[:, n, :].astype(jnp.bfloat16), (((0,), (0,)), ((), ())),
            preferred_element_type=jnp.float32,
        )
        for n in range(PAGE)
    ]
    for g in range(KV_HERE):
        for n in range(0, PAGE, 2):
            first, second = tokens[n][:, slab_of(g)], tokens[n + 1][:, slab_of(g)]
            cols = slice(n * HEAD_DIM, (n + 2) * HEAD_DIM)
            page_ref[2 * g, :, cols] = jnp.where(low_page, first, pltpu.roll(second, HEAD_DIM, 1)).astype(jnp.bfloat16)
            page_ref[2 * g + 1, :, cols] = jnp.where(low_page, pltpu.roll(first, HEAD_DIM, 1), second).astype(jnp.bfloat16)

    pairs, own_level = finish(plane)
    for k in range(1, PLANES):
        @pl.when(gets_part(k))
        def _():
            part_copy(k).wait_recv()
    levels = [own_level]
    for k in range(1, PLANES):
        slab = part_recv[k, :, 384:512].astype(jnp.float32)
        levels.append(slab + pltpu.roll(slab, 120, 1) + pltpu.roll(slab, 112, 1))
    top = functools.reduce(jnp.maximum, levels)
    shares = [jnp.exp(level - top) for level in levels]
    whole = functools.reduce(jnp.add, shares)
    shares = [share / whole for share in shares]

    def spread(share, p):
        return jnp.where(low, share[:, 2 * p : 2 * p + 1], share[:, 2 * p + 1 : 2 * p + 2])

    for p in range(HEADS_HERE // 2):
        cols = slice(p * 128, (p + 1) * 128)
        value = pairs[p] * spread(shares[0], p)
        for k in range(1, PLANES):
            value = value + part_recv[k, :, cols].astype(jnp.float32) * spread(shares[k], p)
        out_ref[:, cols] = value.astype(jnp.bfloat16)

    for n in range(1, LINE):
        cache_copy(n).wait_send()
        new_copy(n).wait_send()

    for k in range(1, PLANES):
        @pl.when(sends_query(k))
        def _():
            query_copy(k).wait_send()

        @pl.when(sends_part(k))
        def _():
            part_copy(k).wait_send()

    @pl.loop(1, 32)
    def _(n):
        page_copy(n).wait_send()


def attend(*operands):
    vmem = pl.BlockSpec(memory_space=pltpu.VMEM)
    state = pltpu.VMEM((PLANES, KV_HERE, GROUP * ROWS, 128), jnp.float32)
    return pl.pallas_call(
        attend_kernel,
        out_shape=[
            jax.ShapeDtypeStruct((ROWS, 384), jnp.bfloat16),
            jax.ShapeDtypeStruct((2 * KV_HERE, ROWS // PAGE, PAGE * HEAD_DIM), jnp.bfloat16),
        ],
        in_specs=[vmem] * 7,
        out_specs=[vmem] * 2,
        scratch_shapes=[
            pltpu.VMEM((ROWS, 1536), jnp.bfloat16),
            pltpu.VMEM((ROWS, 384), jnp.bfloat16),
            pltpu.VMEM((PLANES, ROWS, 384), jnp.bfloat16),
            pltpu.VMEM((LINE // 2, 2 * CACHE_HERE, 256), jnp.bfloat16),
            pltpu.VMEM((ROWS, 256), jnp.bfloat16),
            pltpu.VMEM((LINE, ROWS, 256), jnp.bfloat16),
            pltpu.VMEM((2 * CACHE_HERE, 256), jnp.bfloat16),
            pltpu.VMEM((LINE, ROWS, 256), jnp.bfloat16),
            pltpu.VMEM((PLANES, KV_HERE, GROUP * ROWS, 128), jnp.bfloat16),
            state,
            state,
            pltpu.VMEM((PLANES, ROWS, 512), jnp.bfloat16),
            pltpu.VMEM((PLANES, ROWS, 512), jnp.bfloat16),
            pltpu.VMEM((ROWS, 256), jnp.float32),
            pltpu.VMEM((ROWS // PAGE, PAGE, 256), jnp.float32),
        ]
        + [pltpu.SemaphoreType.DMA((n,)) for n in (4, 4, 8, 8, 8, 8, 4, 4, 32, 32)],
        compiler_params=pltpu.CompilerParams(
            vmem_limit_bytes=52 * 1024 * 1024, collective_id=1, has_side_effects=True
        ),
        name="attend",
    )(*operands)


HALF = 768


def experts_kernel(
    att_ref, ow_ref, hid_ref, gain_ref, routes_ref, prob_ref, win_ref, wout_ref, out_ref,
    product, sum_send, sum_recv, residual, info_a, info_b, got_a, got_b, send_a, send_b, recv_a, recv_b,
    made_a, made_b, back_a, back_b, part_a, part_b, red_a, red_b, acc_a, acc_b, last_send, last_recv,
    sum_out, sum_in, info_out, info_in, y_out, y_in, wide_out, wide_in, go_out, go_in,
    ret_out, ret_in, red_out, red_in, last_out, last_in,
):
    seq_index = lax.axis_index("seq")
    exp_index = lax.axis_index("exp")
    z, h, x = seq_index // 8, lax.rem(seq_index // 4, 2), lax.rem(seq_index, 4)
    MESH = pl.DeviceIdType.MESH

    def at(dz, dh, dx):
        return lax.rem(z + 4 + dz, 4) * 8 + lax.rem(h + dh, 2) * 4 + lax.rem(x + 4 + dx, 4)

    def send(source, target, out_sem, in_sem, to):
        return pltpu.make_async_remote_copy(
            src_ref=source, dst_ref=target, send_sem=out_sem, recv_sem=in_sem,
            device_id={"seq": to}, device_id_type=MESH,
        )

    def side(k):
        return lax.rem(exp_index + k, 4)

    def sum_copy(k):
        return pltpu.make_async_remote_copy(
            src_ref=sum_send.at[k], dst_ref=sum_recv.at[k], send_sem=sum_out.at[k], recv_sem=sum_in.at[k],
            device_id={"exp": side(k)}, device_id_type=MESH,
        )

    z_peers = [(i, m) for i in range(4) for m in range(2) if (i, m) != (0, 0)]
    x_peers = [(j, m) for j in range(1, 4) for m in range(2)]

    def info_copies():
        return [
            send(info_a.at[0, 0], info_a.at[i, m], info_out.at[n], info_in.at[n], at(i, m, 0))
            for n, (i, m) in enumerate(z_peers)
        ] + [
            send(info_a.at[0, 0], info_b.at[j, m], info_out.at[7 + n], info_in.at[7 + n], at(0, m, j))
            for n, (j, m) in enumerate(x_peers)
        ]

    def y_copies():
        return [
            send(got_a.at[0, 0], got_a.at[0, 1], y_out.at[0], y_in.at[0], at(0, 1, 0)),
            send(got_b.at[0, 0], got_b.at[0, 1], y_out.at[1], y_in.at[1], at(0, 1, 0)),
        ]

    def wide_a(i, m):
        return send(got_a.at[0, m], got_a.at[i, m], wide_out.at[0, m, i], wide_in.at[0, m, i], at(i, 0, 0))

    def wide_b(i, m):
        return send(got_b.at[0, m], got_b.at[i, m], wide_out.at[1, m, i], wide_in.at[1, m, i], at(0, 0, i))

    def go_a(k, i):
        return send(send_a.at[k, i], recv_a.at[k, i], go_out.at[0, k, i], go_in.at[0, k, i], at(0, 0, k))

    def go_b(k, i):
        return send(send_b.at[k, i], recv_b.at[k, i], go_out.at[1, k, i], go_in.at[1, k, i], at(k, 0, 0))

    def ret_a(k, i):
        return send(made_a.at[k, i], back_a.at[k, i], ret_out.at[k, i], ret_in.at[k, i], at(0, 0, -k))

    def ret_b(i):
        return send(made_b.at[i], back_b.at[i], ret_out.at[0, i], ret_in.at[0, i], at(-i, 0, 0))

    def sum_a(i):
        return send(part_a.at[i], red_a.at[i], red_out.at[0, i], red_in.at[0, i], at(-i, 0, 0))

    def sum_b(i):
        return send(part_b.at[i], red_b.at[i], red_out.at[1, i], red_in.at[1, i], at(0, 0, -i))

    def last_copy(n):
        return send(last_send.at[n], last_recv.at[n], last_out.at[n], last_in.at[n], at(0, 1, 0))

    barrier = pltpu.get_barrier_semaphore()
    for k in range(1, 4):
        pl.semaphore_signal(barrier, inc=1, device_id={"exp": side(k)}, device_id_type=MESH)
    for i, m in z_peers:
        pl.semaphore_signal(barrier, inc=1, device_id={"seq": at(i, m, 0)}, device_id_type=MESH)
    for j, m in x_peers:
        pl.semaphore_signal(barrier, inc=1, device_id={"seq": at(0, m, j)}, device_id_type=MESH)

    product[...] = jnp.dot(att_ref[...], ow_ref[...], preferred_element_type=jnp.float32).reshape(product.shape)
    for k in range(1, 4):
        sum_send[k] = product[side(k)].astype(jnp.bfloat16)
    pl.semaphore_wait(barrier, 3 + len(z_peers) + len(x_peers))
    for k in range(1, 4):
        sum_copy(k).start()

    chosen = routes_ref[...].astype(jnp.float32)
    prob = prob_ref[...]
    prob = prob / jnp.sum(prob, axis=0, keepdims=True)
    expert = lax.broadcasted_iota(jnp.int32, (EXPERTS, 64), 0).astype(jnp.float32)
    hit = jnp.zeros((EXPERTS, 64), jnp.float32)
    share = jnp.zeros((EXPERTS, 64), jnp.float32)
    for k in range(8):
        match = chosen[k : k + 1, :] == expert
        hit = jnp.where(match, 1.0, hit)
        share = jnp.where(match, prob[k : k + 1, :], share)
    before = (
        lax.broadcasted_iota(jnp.int32, (64, 64), 0) <= lax.broadcasted_iota(jnp.int32, (64, 64), 1)
    ).astype(jnp.bfloat16)
    rank = jnp.dot(hit.astype(jnp.bfloat16), before, preferred_element_type=jnp.float32)
    info_a[0, 0, :EXPERTS] = rank * hit
    info_a[0, 0, EXPERTS:] = share
    for copy in info_copies():
        copy.start()

    mixed = product[exp_index]
    for k in range(1, 4):
        sum_copy(k).wait_recv()
        mixed = mixed + sum_recv[k].astype(jnp.float32)
    rows = pl.ds(pl.multiple_of(exp_index * 64, 64), 64)
    after = hid_ref[rows, :].astype(jnp.float32) + residual_scale * mixed
    residual[...] = after
    spread = lax.rsqrt(jnp.mean(after * after, axis=-1, keepdims=True) + norm_epsilon)
    moe_in = (after * spread * gain_ref[...]).astype(jnp.bfloat16)
    got_a[0, 0] = moe_in[:, :HALF]
    got_b[0, 0] = moe_in[:, HALF:]
    for copy in y_copies():
        copy.start()
    for i in (1, 3, 2):
        wide_a(i, 0).start()
        wide_b(i, 0).start()
    for copy in info_copies():
        copy.wait_recv()
    info_b[0] = info_a[0]

    slot = lax.broadcasted_iota(jnp.int32, (CAP, 64), 0).astype(jnp.float32) + 1.0

    def experts_a(k):
        return z * 8 + h * 4 + lax.rem(x + k, 4)

    def experts_b(k):
        return lax.rem(z + k, 4) * 8 + h * 4 + x

    def picks(info, i, m, experts_of):
        return jnp.concatenate(
            [(info[i, m, pl.ds(experts_of(k), 1), :] == slot).astype(jnp.float32) for k in range(4)], axis=0
        ).astype(jnp.bfloat16)

    def mixes(info, i, m, experts_of):
        return jnp.concatenate(
            [
                jnp.where(
                    info[i, m, pl.ds(experts_of(k), 1), :] == slot,
                    info[i, m, pl.ds(EXPERTS + experts_of(k), 1), :],
                    0.0,
                )
                for k in range(4)
            ],
            axis=0,
        ).astype(jnp.bfloat16)

    def pick(info, got, experts_of, sends, recvs, i, m):
        taken = jnp.dot(
            picks(info, i, m, experts_of), got[i, m], preferred_element_type=jnp.float32
        ).astype(jnp.bfloat16)
        recvs[0, i, m] = taken[:CAP]
        for k in range(1, 4):
            sends[k, i, m] = taken[k * CAP : (k + 1) * CAP]

    @pl.loop(0, 4)
    def _(i):
        @pl.when(i == 0)
        def _():
            for copy in y_copies():
                copy.wait_recv()
            for n in (1, 3, 2):
                wide_a(n, 1).start()
                wide_b(n, 1).start()

        @pl.when(i > 0)
        def _():
            for m in range(2):
                wide_a(i, m).wait_recv()
                wide_b(i, m).wait_recv()

        for m in range(2):
            pick(info_a, got_a, experts_a, send_a, recv_a, i, m)
        for k in range(1, 4):
            go_a(k, i).start()
        for m in range(2):
            pick(info_b, got_b, experts_b, send_b, recv_b, i, m)
        for k in range(1, 4):
            go_b(k, i).start()

    @pl.loop(0, 4)
    def _(i):
        for k in range(1, 4):
            go_a(k, i).wait_recv()

        @pl.when(i > 0)
        def _():
            for j in range(4):
                send(
                    send_b.at[i, j], recv_b.at[i, j], go_out.at[1, i, j], go_in.at[1, i, j], at(i, 0, 0)
                ).wait_recv()

        hidden = jnp.dot(
            recv_a[:, i].reshape(256, HALF), win_ref[:HALF, :], preferred_element_type=jnp.float32
        ) + jnp.dot(recv_b[i].reshape(256, HALF), win_ref[HALF:, :], preferred_element_type=jnp.float32)
        gate, up = hidden[:, :512], hidden[:, 512:]
        active = (gate / (1.0 + jnp.exp(-gate)) * up).astype(jnp.bfloat16)
        done = jnp.dot(active, wout_ref[...], preferred_element_type=jnp.float32).astype(jnp.bfloat16)
        done_a = done[:, :HALF].reshape(4, 2, CAP, HALF)
        back_a[0, i] = done_a[0]
        for k in range(1, 4):
            made_a[k, i] = done_a[k]
            ret_a(k, i).start()
        made_b[i] = done[:, HALF:].reshape(4, 2, CAP, HALF)

        @pl.when(i > 0)
        def _():
            ret_b(i).start()

        @pl.when(i == 0)
        def _():
            back_b[0] = made_b[0]

    def mix(info, backs, experts_of, i, m):
        return lax.dot_general(
            mixes(info, i, m, experts_of), backs[:, i, m].reshape(4 * CAP, HALF),
            (((0,), (0,)), ((), ())), preferred_element_type=jnp.float32,
        )

    @pl.loop(0, 4)
    def _(i):
        for k in range(1, 4):
            ret_a(k, i).wait_recv()
        for m in range(2):
            some = mix(info_a, back_a, experts_a, i, m)
            part_a[i, m] = some.astype(jnp.bfloat16)

            @pl.when(i == 0)
            def _():
                acc_a[m] = some

        @pl.when(i > 0)
        def _():
            sum_a(i).start()

    for i in range(1, 4):
        ret_b(i).wait_recv()

    @pl.loop(0, 4)
    def _(n):
        i = 3 - n
        for m in range(2):
            some = mix(info_b, back_b, experts_b, i, m)
            part_b[i, m] = some.astype(jnp.bfloat16)

            @pl.when(i == 0)
            def _():
                acc_b[m] = some

        @pl.when(i > 0)
        def _():
            sum_b(i).start()

    for n, (copy, acc, red) in enumerate(((sum_a, acc_a, red_a), (sum_b, acc_b, red_b))):
        for i in range(1, 4):
            copy(i).wait_recv()
            acc[...] += red[i].astype(jnp.float32)
        last_send[n] = acc[1].astype(jnp.bfloat16)
        last_copy(n).start()
    for n, acc in enumerate((acc_a, acc_b)):
        last_copy(n).wait_recv()
        cols = slice(n * HALF, (n + 1) * HALF)
        moe = acc[0] + last_recv[n].astype(jnp.float32)
        out_ref[:, cols] = (residual[:, cols] + residual_scale * moe).astype(jnp.bfloat16)

    for k in range(1, 4):
        sum_copy(k).wait_send()
    for copy in info_copies() + y_copies():
        copy.wait_send()
    for n in range(2):
        last_copy(n).wait_send()

    @pl.loop(1, 4)
    def _(i):
        for m in range(2):
            wide_a(i, m).wait_send()
            wide_b(i, m).wait_send()
        ret_b(i).wait_send()
        sum_a(i).wait_send()
        sum_b(i).wait_send()

    @pl.loop(0, 4)
    def _(i):
        for k in range(1, 4):
            go_a(k, i).wait_send()
            go_b(k, i).wait_send()
            ret_a(k, i).wait_send()


def experts(*operands):
    vmem = pl.BlockSpec(memory_space=pltpu.VMEM)
    width = 1536
    table = pltpu.VMEM((4, 2, 64, 64), jnp.float32)
    blocks = pltpu.VMEM((4, 2, 64, HALF), jnp.bfloat16)
    chosen = pltpu.VMEM((4, 4, 2, CAP, HALF), jnp.bfloat16)
    pair = pltpu.VMEM((2, 64, HALF), jnp.float32)
    last = pltpu.VMEM((2, 64, HALF), jnp.bfloat16)
    counts = ((4,), (13,), (2,), (2, 2, 4), (2, 4, 4), (4, 4), (2, 4), (2,))
    return pl.pallas_call(
        experts_kernel,
        out_shape=jax.ShapeDtypeStruct((64, width), jnp.bfloat16),
        in_specs=[vmem] * 8,
        out_specs=vmem,
        scratch_shapes=[
            pltpu.VMEM((4, 64, width), jnp.float32),
            pltpu.VMEM((4, 64, width), jnp.bfloat16),
            pltpu.VMEM((4, 64, width), jnp.bfloat16),
            pltpu.VMEM((64, width), jnp.float32),
            table,
            table,
            blocks,
            blocks,
        ]
        + [chosen] * 8
        + [blocks] * 4
        + [pair, pair, last, last]
        + [pltpu.SemaphoreType.DMA(n) for n in counts for _ in range(2)],
        compiler_params=pltpu.CompilerParams(
            vmem_limit_bytes=52 * 1024 * 1024, collective_id=2, has_side_effects=True
        ),
        name="experts",
    )(*operands)


def body(
    hidden_in,
    attn_gain,
    q_weight,
    k_weight,
    v_weight,
    o_weight,
    cache_kv,
    moe_gain,
    expert_in,
    expert_out,
    routes,
    route_prob,
    page_slot,
):
    attended, page_slabs = attend(
        hidden_in, attn_gain[None, :], q_weight, k_weight, v_weight, cache_kv, page_slot.reshape(32, 32)
    )
    page_rows = page_slabs.transpose(1, 0, 2).reshape(ROWS // PAGE, KV_HERE, 2, PAGE * HEAD_DIM)

    hidden_out = experts(
        attended, o_weight, hidden_in, moe_gain[None, :], routes.T, route_prob.T, expert_in[0], expert_out[0]
    )
    return (hidden_out, page_rows)


def solution(mesh):
    return jax.shard_map(
        body,
        mesh=mesh,
        in_specs=(
            P("seq", None),
            P(),
            P(None, "exp"),
            P(None, "exp"),
            P(None, "exp"),
            P("exp", None),
            P("seq", "exp"),
            P(),
            P("seq", None, None),
            P("seq", None, None),
            P(("seq", "exp"), None),
            P(("seq", "exp"), None),
            P(),
        ),
        out_specs=(P(("seq", "exp"), None), P("seq", "exp", None, None)),
        check_vma=False,
    )
```

```python
import functools

import jax
import jax.numpy as jnp
from jax import lax
from jax.experimental import pallas as pl
from jax.experimental.pallas import tpu as pltpu
from jax.sharding import PartitionSpec as P

HEADS_HERE = 6
KV_HERE = 2
GROUP = 3
HEAD_DIM = 64
EXPERTS = 32
CAP = 32
PAGE = 8
PLANES = 4
LINE = 8
ROWS = 256
CACHE_HERE = 512

norm_epsilon = 1e-06
attention_scale = 0.015625
residual_scale = 0.22
masked_score = -1e30


NEAR = ((0, 0), (0, 1), (1, 0), (0, 3), (1, 1), (0, 2), (1, 3), (1, 2))
HALF = 768


def layer_kernel(
    hid_hbm, attn_gain_ref, qw_hbm, kw_hbm, vw_hbm, cache_hbm, slot_ref,
    ow_hbm, moe_gain_ref, routes_ref, prob_ref, win_hbm, wout_hbm, out_ref, page_ref,
    hid_ref, qw_ref, kw_ref, vw_ref, ow_ref, win_ref, wout_ref, att_ref,
    query, q_all, cache_all, new_own, new_all, cache_val, new_val, qs, best, acc,
    part_send, part_recv, page_send, page_recv,
    product, sum_send, sum_recv, residual, info_a, info_b, got_a, got_b, send_a, send_b, recv_a, recv_b,
    made_a, made_b, back_a, back_b, sum_part_a, sum_part_b, red_a, red_b, acc_a, acc_b, last_send, last_recv,
    load_in, q_out, q_in, cache_out, cache_in, new_out, new_in, part_out, part_in, page_out, page_in,
    sum_out, sum_in, info_out, info_in, y_out, y_in, wide_out, wide_in, go_out, go_in,
    ret_out, ret_in, red_out, red_in, last_out, last_in,
):
    seq_index = lax.axis_index("seq")
    plane = seq_index // LINE
    place = seq_index % LINE
    even = plane % 2 == 0
    MESH = pl.DeviceIdType.MESH
    lane = lax.broadcasted_iota(jnp.int32, (ROWS, 2 * HEAD_DIM), 1)
    low = lane < HEAD_DIM
    one = jnp.ones((), jnp.bfloat16)

    def send(source, target, out_sem, in_sem, to):
        return pltpu.make_async_remote_copy(
            src_ref=source, dst_ref=target, send_sem=out_sem, recv_sem=in_sem,
            device_id={"seq": to}, device_id_type=MESH,
        )

    def peer(n):
        h, x = NEAR[n]
        return plane * LINE + lax.rem(place // 4 + h, 2) * 4 + lax.rem(place % 4 + x, 4)

    def line_peer(k):
        return lax.rem(plane + k, PLANES) * LINE + place

    def ahead(n):
        return lax.rem(seq_index + n, 32)

    def cache_copy(n):
        rows = pl.ds((n % 2) * CACHE_HERE, CACHE_HERE)
        return send(cache_all.at[0, pl.ds(0, CACHE_HERE)], cache_all.at[n // 2, rows], cache_out.at[n], cache_in.at[n], peer(n))

    def new_copy(n):
        return send(new_own, new_all.at[place], new_out.at[n], new_in.at[n], peer(n))

    def query_copy(k):
        return send(query, q_all.at[plane], q_out.at[k], q_in.at[k], line_peer(k))

    def part_copy(k):
        return send(part_send.at[k], part_recv.at[k], part_out.at[k], part_in.at[k], line_peer(k))

    def page_copy(n):
        rows = pl.ds(pl.multiple_of(ahead(n) * PAGE, PAGE), PAGE)
        return send(page_send.at[rows], page_recv.at[seq_index], page_out.at[n], page_in.at[n], ahead(n))

    def sends_query(k):
        return jnp.logical_or(plane < 2, plane == 3) if k == 3 else plane < 2

    def gets_query(k):
        origin = lax.rem(plane + PLANES - k, PLANES)
        return jnp.logical_or(origin < 2, origin == 3) if k == 3 else origin < 2

    def sends_part(k):
        target = lax.rem(plane + k, PLANES)
        return jnp.logical_or(target < 2, target == 3) if k == 1 else target < 2

    def gets_part(k):
        return jnp.logical_or(plane < 2, plane == 3) if k == 1 else plane < 2

    exp_index = lax.axis_index("exp")
    z, h, x = seq_index // 8, lax.rem(seq_index // 4, 2), lax.rem(seq_index, 4)

    def at(dz, dh, dx):
        return lax.rem(z + 4 + dz, 4) * 8 + lax.rem(h + dh, 2) * 4 + lax.rem(x + 4 + dx, 4)

    def side(k):
        return lax.rem(exp_index + k, 4)

    def sum_copy(k):
        return pltpu.make_async_remote_copy(
            src_ref=sum_send.at[k], dst_ref=sum_recv.at[k], send_sem=sum_out.at[k], recv_sem=sum_in.at[k],
            device_id={"exp": side(k)}, device_id_type=MESH,
        )

    z_peers = [(i, m) for i in range(4) for m in range(2) if (i, m) != (0, 0)]
    x_peers = [(j, m) for j in range(1, 4) for m in range(2)]

    def info_copies():
        return [
            send(info_a.at[0, 0], info_a.at[i, m], info_out.at[n], info_in.at[n], at(i, m, 0))
            for n, (i, m) in enumerate(z_peers)
        ] + [
            send(info_a.at[0, 0], info_b.at[j, m], info_out.at[7 + n], info_in.at[7 + n], at(0, m, j))
            for n, (j, m) in enumerate(x_peers)
        ]

    def y_copies():
        return [
            send(got_a.at[0, 0], got_a.at[0, 1], y_out.at[0], y_in.at[0], at(0, 1, 0)),
            send(got_b.at[0, 0], got_b.at[0, 1], y_out.at[1], y_in.at[1], at(0, 1, 0)),
        ]

    def wide_a(i, m):
        return send(got_a.at[0, m], got_a.at[i, m], wide_out.at[0, m, i], wide_in.at[0, m, i], at(i, 0, 0))

    def wide_b(i, m):
        return send(got_b.at[0, m], got_b.at[i, m], wide_out.at[1, m, i], wide_in.at[1, m, i], at(0, 0, i))

    def go_a(k, i):
        return send(send_a.at[k, i], recv_a.at[k, i], go_out.at[0, k, i], go_in.at[0, k, i], at(0, 0, k))

    def go_b(k, i):
        return send(send_b.at[k, i], recv_b.at[k, i], go_out.at[1, k, i], go_in.at[1, k, i], at(k, 0, 0))

    def ret_a(k, i):
        return send(made_a.at[k, i], back_a.at[k, i], ret_out.at[k, i], ret_in.at[k, i], at(0, 0, -k))

    def ret_b(i):
        return send(made_b.at[i], back_b.at[i], ret_out.at[0, i], ret_in.at[0, i], at(-i, 0, 0))

    def sum_a(i):
        return send(sum_part_a.at[i], red_a.at[i], red_out.at[0, i], red_in.at[0, i], at(-i, 0, 0))

    def sum_b(i):
        return send(sum_part_b.at[i], red_b.at[i], red_out.at[1, i], red_in.at[1, i], at(0, 0, -i))

    def last_copy(n):
        return send(last_send.at[n], last_recv.at[n], last_out.at[n], last_in.at[n], at(0, 1, 0))

    barrier = pltpu.get_barrier_semaphore()

    @pl.loop(1, 32)
    def _(n):
        pl.semaphore_signal(barrier, inc=1, device_id={"seq": ahead(n)}, device_id_type=MESH)

    for k in range(1, 4):
        pl.semaphore_signal(barrier, inc=1, device_id={"exp": side(k)}, device_id_type=MESH)

    loads = [
        pltpu.make_async_copy(source, target, load_in.at[n])
        for n, (source, target) in enumerate(
            (
                (hid_hbm, hid_ref), (qw_hbm, qw_ref), (kw_hbm, kw_ref), (vw_hbm, vw_ref), (cache_hbm, cache_all.at[0, pl.ds(0, CACHE_HERE)]),
                (ow_hbm, ow_ref), (win_hbm, win_ref), (wout_hbm, wout_ref),
            )
        )
    ]
    for load in loads:
        load.start()
    for k in range(1, PLANES):
        @pl.when(jnp.logical_not(gets_part(k)))
        def _():
            part_recv[k, :, :384] = jnp.zeros((ROWS, 384), jnp.bfloat16)
            part_recv[k, :, 384:] = jnp.full((ROWS, 128), masked_score, jnp.bfloat16)

    best[...] = jnp.full_like(best, masked_score)
    acc[...] = jnp.zeros_like(acc)
    loads[0].wait()

    @pl.loop(0, ROWS // 64)
    def _(step):
        rows = pl.ds(pl.multiple_of(step * 64, 64), 64)
        wide = hid_ref[rows, :].astype(jnp.float32)
        spread = lax.rsqrt(jnp.mean(wide * wide, axis=-1, keepdims=True) + norm_epsilon)
        sum_send[step] = (wide * spread * attn_gain_ref[...][None, :]).astype(jnp.bfloat16)

    loads[4].wait()
    loads[1].wait()
    normed = sum_send[...].reshape(ROWS, 1536)
    query[...] = jnp.dot(normed, qw_ref[...], preferred_element_type=jnp.float32).astype(jnp.bfloat16)
    pl.semaphore_wait(barrier, 31 + 3)
    for k in range(1, PLANES):
        @pl.when(sends_query(k))
        def _():
            query_copy(k).start()

    for n in range(1, 4):
        cache_copy(n).start()
    loads[2].wait()
    loads[3].wait()
    keys = jnp.dot(normed, kw_ref[...], preferred_element_type=jnp.float32)
    values = jnp.dot(normed, vw_ref[...], preferred_element_type=jnp.float32)
    slabs = [
        jnp.where(low, keys, pltpu.roll(values, HEAD_DIM, 1)).astype(jnp.bfloat16),
        jnp.where(low, pltpu.roll(keys, HEAD_DIM, 1), values).astype(jnp.bfloat16),
    ]
    for g in range(KV_HERE):
        new_own[:, g * 128 : (g + 1) * 128] = slabs[g]
        page_send[:, g * 128 : (g + 1) * 128] = slabs[g].astype(jnp.float32)
    for n in range(1, LINE):
        new_copy(n).start()
    for n in range(4, LINE):
        cache_copy(n).start()

    @pl.loop(1, 32)
    def _(n):
        page_copy(n).start()

    chosen = routes_ref[...].astype(jnp.float32)
    prob = prob_ref[...]
    prob = prob / jnp.sum(prob, axis=0, keepdims=True)
    expert = lax.broadcasted_iota(jnp.int32, (EXPERTS, 64), 0).astype(jnp.float32)
    hit = jnp.zeros((EXPERTS, 64), jnp.float32)
    share = jnp.zeros((EXPERTS, 64), jnp.float32)
    for k in range(8):
        match = chosen[k : k + 1, :] == expert
        hit = jnp.where(match, 1.0, hit)
        share = jnp.where(match, prob[k : k + 1, :], share)
    before = (
        lax.broadcasted_iota(jnp.int32, (64, 64), 0) <= lax.broadcasted_iota(jnp.int32, (64, 64), 1)
    ).astype(jnp.bfloat16)
    rank = jnp.dot(hit.astype(jnp.bfloat16), before, preferred_element_type=jnp.float32)
    info_a[0, 0, :EXPERTS] = rank * hit
    info_a[0, 0, EXPERTS:] = share
    for copy in info_copies():
        copy.start()

    q_all[plane] = query[...]
    new_all[place] = new_own[...]
    own_rows = pl.ds(pl.multiple_of(seq_index * PAGE, PAGE), PAGE)
    page_recv[seq_index] = page_send[own_rows, :]

    def prepare(t):
        for h in range(HEADS_HERE):
            slab = q_all[t, :, (h // 2) * 128 : (h // 2 + 1) * 128]
            slab = slab.astype(jnp.float32) * attention_scale
            if h % 2:
                slab = pltpu.roll(slab, HEAD_DIM, 1)
            a = h % GROUP
            qs[t, h // GROUP, a * ROWS : (a + 1) * ROWS, :] = jnp.where(low, slab, 0.0).astype(jnp.bfloat16)

    def slab_of(g):
        return slice(g * 128, (g + 1) * 128)

    def update(turns, keys_of, values_of, first_key=None):
        chains = [(t, g, slice(a * ROWS, (a + 1) * ROWS)) for t in turns for g in range(KV_HERE) for a in range(GROUP)]
        raw = [
            lax.dot_general(
                qs[t, g, rows, :], keys_of(g), (((1,), (1,)), ((), ())), preferred_element_type=jnp.float32
            )
            for t, g, rows in chains
        ]
        for (t, g, rows), scores in zip(chains, raw):
            if first_key is not None:
                r = lax.broadcasted_iota(jnp.int32, scores.shape, 0)
                c = lax.broadcasted_iota(jnp.int32, scores.shape, 1)
                scores = jnp.where(c - r <= place * ROWS - first_key, scores, masked_score)
            old = best[t, g, rows, :]
            new = jnp.maximum(old, jnp.max(scores, axis=-1, keepdims=True))
            best[t, g, rows, :] = new
            weights = jnp.exp(scores - new[:, :1]).astype(jnp.bfloat16)
            acc[t, g, rows, :] = acc[t, g, rows, :] * jnp.exp(old - new) + jnp.dot(
                weights, values_of(g), preferred_element_type=jnp.float32
            )

    prepare(plane)
    for k in range(1, PLANES):
        @pl.when(gets_query(k))
        def _():
            query_copy(k).wait_recv()
            prepare(lax.rem(plane + PLANES - k, PLANES))

    def cache_pair(m):
        for part in range(4):
            rows = slice(part * ROWS, (part + 1) * ROWS)
            for g in range(KV_HERE):
                cache_val[rows, slab_of(g)] = jnp.where(low, one, cache_all[m, rows, slab_of(g)])
        update((0, 1), lambda g: cache_all[m, :, slab_of(g)], lambda g: cache_val[:, slab_of(g)])

    def cache_pairs(start):
        @pl.loop(start, start + 2)
        def _(m):
            @pl.when(m > 0)
            def _():
                send(
                    cache_all.at[0, pl.ds(0, CACHE_HERE)], cache_all.at[m, pl.ds(0, CACHE_HERE)],
                    cache_out.at[2 * m], cache_in.at[2 * m], peer(1),
                ).wait_recv()

            send(
                cache_all.at[0, pl.ds(0, CACHE_HERE)], cache_all.at[m, pl.ds(CACHE_HERE, CACHE_HERE)],
                cache_out.at[2 * m + 1], cache_in.at[2 * m + 1], peer(1),
            ).wait_recv()
            cache_pair(m)

    cache_pairs(0)
    for n in range(1, LINE):
        dh, dx = NEAR[n]
        origin = lax.rem(place // 4 + dh, 2) * 4 + lax.rem(place % 4 + 4 - dx, 4)
        send(new_own, new_all.at[origin], new_out.at[n], new_in.at[n], peer(n)).wait_recv()

    @pl.loop(0, LINE)
    def _(n):
        for g in range(KV_HERE):
            new_val[n, :, slab_of(g)] = jnp.where(low, one, new_all[n, :, slab_of(g)])

    def new_keys(step):
        return lambda g: new_all[pl.ds(step * 4, 4), :, slab_of(g)].reshape(1024, 128)

    def new_values(step):
        return lambda g: new_val[pl.ds(step * 4, 4), :, slab_of(g)].reshape(1024, 128)

    @pl.loop(0, jnp.where(even, 2, 0))
    def _(step):
        update((plane + 1,), new_keys(step), new_values(step))

    cache_pairs(2)

    def finish(t):
        heads = []
        for h in range(HEADS_HERE):
            g, rows = h // GROUP, slice((h % GROUP) * ROWS, (h % GROUP + 1) * ROWS)
            part = acc[t, g, rows, :]
            total = part[:, :1]
            heads.append((part / total, best[t, g, rows, :] + jnp.log(total)))
        levels = jnp.zeros((ROWS, 128), jnp.float32)
        for h in range(HEADS_HERE):
            levels = jnp.where(lane % 8 == h, heads[h][1], levels)
        return [
            jnp.where(low, pltpu.roll(heads[2 * p][0], HEAD_DIM, 1), heads[2 * p + 1][0])
            for p in range(HEADS_HERE // 2)
        ], levels

    for k in range(1, PLANES):
        @pl.when(sends_part(k))
        def _():
            pairs, levels = finish(lax.rem(plane + k, PLANES))
            for p in range(HEADS_HERE // 2):
                part_send[k, :, p * 128 : (p + 1) * 128] = pairs[p].astype(jnp.bfloat16)
            high = levels.astype(jnp.bfloat16).astype(jnp.float32)
            rest = levels - high
            middle = rest.astype(jnp.bfloat16).astype(jnp.float32)
            split = jnp.where(lane < 8, high, jnp.where(lane < 16, middle, rest - middle))
            part_send[k, :, 384:512] = split.astype(jnp.bfloat16)
            part_copy(k).start()

    @pl.loop(0, place // 4 + 1)
    def _(step):
        update((plane,), new_keys(step), new_values(step), step * 1024)

    @pl.loop(1, 32)
    def _(n):
        page_copy(n).wait_recv()

    column = lax.broadcasted_iota(jnp.int32, (32, 32), 1)
    block_of = lax.broadcasted_iota(jnp.int32, (32, 1024), 0) * 32 + seq_index
    slots = jnp.sum(
        jnp.where(
            lax.broadcasted_iota(jnp.int32, (32, 1024), 1) == block_of,
            slot_ref[...].astype(jnp.float32)[None, :],
            0.0,
        ),
        axis=1,
        keepdims=True,
    )
    owner = (slots == column.astype(jnp.float32)).astype(jnp.bfloat16)
    low_page = lax.broadcasted_iota(jnp.int32, (32, 128), 1) < HEAD_DIM
    tokens = [
        lax.dot_general(
            owner, page_recv[:, n, :].astype(jnp.bfloat16), (((0,), (0,)), ((), ())),
            preferred_element_type=jnp.float32,
        )
        for n in range(PAGE)
    ]
    for g in range(KV_HERE):
        for n in range(0, PAGE, 2):
            first, second = tokens[n][:, slab_of(g)], tokens[n + 1][:, slab_of(g)]
            cols = slice(n * HEAD_DIM, (n + 2) * HEAD_DIM)
            page_ref[2 * g, :, cols] = jnp.where(low_page, first, pltpu.roll(second, HEAD_DIM, 1)).astype(jnp.bfloat16)
            page_ref[2 * g + 1, :, cols] = jnp.where(low_page, pltpu.roll(first, HEAD_DIM, 1), second).astype(jnp.bfloat16)

    pairs, own_level = finish(plane)
    for k in range(1, PLANES):
        @pl.when(gets_part(k))
        def _():
            part_copy(k).wait_recv()
    levels = [own_level]
    for k in range(1, PLANES):
        slab = part_recv[k, :, 384:512].astype(jnp.float32)
        levels.append(slab + pltpu.roll(slab, 120, 1) + pltpu.roll(slab, 112, 1))
    top = functools.reduce(jnp.maximum, levels)
    shares = [jnp.exp(level - top) for level in levels]
    whole = functools.reduce(jnp.add, shares)
    shares = [share / whole for share in shares]

    def spread(share, p):
        return jnp.where(low, share[:, 2 * p : 2 * p + 1], share[:, 2 * p + 1 : 2 * p + 2])

    for p in range(HEADS_HERE // 2):
        cols = slice(p * 128, (p + 1) * 128)
        value = pairs[p] * spread(shares[0], p)
        for k in range(1, PLANES):
            value = value + part_recv[k, :, cols].astype(jnp.float32) * spread(shares[k], p)
        att_ref[:, cols] = value.astype(jnp.bfloat16)

    for n in range(1, LINE):
        cache_copy(n).wait_send()
        new_copy(n).wait_send()

    for k in range(1, PLANES):
        @pl.when(sends_query(k))
        def _():
            query_copy(k).wait_send()

        @pl.when(sends_part(k))
        def _():
            part_copy(k).wait_send()

    @pl.loop(1, 32)
    def _(n):
        page_copy(n).wait_send()

    loads[5].wait()
    product[...] = jnp.dot(att_ref[...], ow_ref[...], preferred_element_type=jnp.float32).reshape(product.shape)
    for k in range(1, 4):
        sum_send[k] = product[side(k)].astype(jnp.bfloat16)
    for k in range(1, 4):
        sum_copy(k).start()

    mixed = product[exp_index]
    for k in range(1, 4):
        sum_copy(k).wait_recv()
        mixed = mixed + sum_recv[k].astype(jnp.float32)
    rows = pl.ds(pl.multiple_of(exp_index * 64, 64), 64)
    after = hid_ref[rows, :].astype(jnp.float32) + residual_scale * mixed
    residual[...] = after
    inverse = lax.rsqrt(jnp.mean(after * after, axis=-1, keepdims=True) + norm_epsilon)
    moe_in = (after * inverse * moe_gain_ref[...][None, :]).astype(jnp.bfloat16)
    got_a[0, 0] = moe_in[:, :HALF]
    got_b[0, 0] = moe_in[:, HALF:]
    for copy in y_copies():
        copy.start()
    for i in (1, 3, 2):
        wide_a(i, 0).start()
        wide_b(i, 0).start()
    for copy in info_copies():
        copy.wait_recv()
    info_b[0] = info_a[0]

    slot = lax.broadcasted_iota(jnp.int32, (CAP, 64), 0).astype(jnp.float32) + 1.0

    def experts_a(k):
        return z * 8 + h * 4 + lax.rem(x + k, 4)

    def experts_b(k):
        return lax.rem(z + k, 4) * 8 + h * 4 + x

    def picks(info, i, m, experts_of):
        return jnp.concatenate(
            [(info[i, m, pl.ds(experts_of(k), 1), :] == slot).astype(jnp.float32) for k in range(4)], axis=0
        ).astype(jnp.bfloat16)

    def mixes(info, i, m, experts_of):
        return jnp.concatenate(
            [
                jnp.where(
                    info[i, m, pl.ds(experts_of(k), 1), :] == slot,
                    info[i, m, pl.ds(EXPERTS + experts_of(k), 1), :],
                    0.0,
                )
                for k in range(4)
            ],
            axis=0,
        ).astype(jnp.bfloat16)

    def pick(info, got, experts_of, sends, recvs, i, m):
        taken = jnp.dot(
            picks(info, i, m, experts_of), got[i, m], preferred_element_type=jnp.float32
        ).astype(jnp.bfloat16)
        recvs[0, i, m] = taken[:CAP]
        for k in range(1, 4):
            sends[k, i, m] = taken[k * CAP : (k + 1) * CAP]

    @pl.loop(0, 4)
    def _(i):
        @pl.when(i == 0)
        def _():
            for copy in y_copies():
                copy.wait_recv()
            for n in (1, 3, 2):
                wide_a(n, 1).start()
                wide_b(n, 1).start()

        @pl.when(i > 0)
        def _():
            for m in range(2):
                wide_a(i, m).wait_recv()
                wide_b(i, m).wait_recv()

        for m in range(2):
            pick(info_a, got_a, experts_a, send_a, recv_a, i, m)
        for k in range(1, 4):
            go_a(k, i).start()
        for m in range(2):
            pick(info_b, got_b, experts_b, send_b, recv_b, i, m)
        for k in range(1, 4):
            go_b(k, i).start()

    loads[6].wait()
    loads[7].wait()

    @pl.loop(0, 4)
    def _(i):
        for k in range(1, 4):
            go_a(k, i).wait_recv()

        @pl.when(i > 0)
        def _():
            for j in range(4):
                send(
                    send_b.at[i, j], recv_b.at[i, j], go_out.at[1, i, j], go_in.at[1, i, j], at(i, 0, 0)
                ).wait_recv()

        hidden = jnp.dot(
            recv_a[:, i].reshape(256, HALF), win_ref[0, :HALF, :], preferred_element_type=jnp.float32
        ) + jnp.dot(recv_b[i].reshape(256, HALF), win_ref[0, HALF:, :], preferred_element_type=jnp.float32)
        gate, up = hidden[:, :512], hidden[:, 512:]
        active = (gate / (1.0 + jnp.exp(-gate)) * up).astype(jnp.bfloat16)
        done = jnp.dot(active, wout_ref[0], preferred_element_type=jnp.float32).astype(jnp.bfloat16)
        done_a = done[:, :HALF].reshape(4, 2, CAP, HALF)
        back_a[0, i] = done_a[0]
        for k in range(1, 4):
            made_a[k, i] = done_a[k]
            ret_a(k, i).start()
        made_b[i] = done[:, HALF:].reshape(4, 2, CAP, HALF)

        @pl.when(i > 0)
        def _():
            ret_b(i).start()

        @pl.when(i == 0)
        def _():
            back_b[0] = made_b[0]

    def mix(info, backs, experts_of, i, m):
        return lax.dot_general(
            mixes(info, i, m, experts_of), backs[:, i, m].reshape(4 * CAP, HALF),
            (((0,), (0,)), ((), ())), preferred_element_type=jnp.float32,
        )

    @pl.loop(0, 4)
    def _(i):
        for k in range(1, 4):
            ret_a(k, i).wait_recv()
        for m in range(2):
            some = mix(info_a, back_a, experts_a, i, m)
            sum_part_a[i, m] = some.astype(jnp.bfloat16)

            @pl.when(i == 0)
            def _():
                acc_a[m] = some

        @pl.when(i > 0)
        def _():
            sum_a(i).start()

    for i in range(1, 4):
        ret_b(i).wait_recv()

    @pl.loop(0, 4)
    def _(n):
        i = 3 - n
        for m in range(2):
            some = mix(info_b, back_b, experts_b, i, m)
            sum_part_b[i, m] = some.astype(jnp.bfloat16)

            @pl.when(i == 0)
            def _():
                acc_b[m] = some

        @pl.when(i > 0)
        def _():
            sum_b(i).start()

    for n, (copy, half_acc, red) in enumerate(((sum_a, acc_a, red_a), (sum_b, acc_b, red_b))):
        for i in range(1, 4):
            copy(i).wait_recv()
            half_acc[...] += red[i].astype(jnp.float32)
        last_send[n] = half_acc[1].astype(jnp.bfloat16)
        last_copy(n).start()
    for n, half_acc in enumerate((acc_a, acc_b)):
        last_copy(n).wait_recv()
        cols = slice(n * HALF, (n + 1) * HALF)
        moe = half_acc[0] + last_recv[n].astype(jnp.float32)
        out_ref[:, cols] = (residual[:, cols] + residual_scale * moe).astype(jnp.bfloat16)

    for k in range(1, 4):
        sum_copy(k).wait_send()
    for copy in info_copies() + y_copies():
        copy.wait_send()
    for n in range(2):
        last_copy(n).wait_send()

    @pl.loop(1, 4)
    def _(i):
        for m in range(2):
            wide_a(i, m).wait_send()
            wide_b(i, m).wait_send()
        ret_b(i).wait_send()
        sum_a(i).wait_send()
        sum_b(i).wait_send()

    @pl.loop(0, 4)
    def _(i):
        for k in range(1, 4):
            go_a(k, i).wait_send()
            go_b(k, i).wait_send()
            ret_a(k, i).wait_send()


def layer(*operands):
    vmem = pl.BlockSpec(memory_space=pltpu.VMEM)
    hbm = pl.BlockSpec(memory_space=pl.ANY)
    specs = [hbm, vmem, hbm, hbm, hbm, hbm, vmem, hbm, vmem, vmem, vmem, hbm, hbm]
    width = 1536

    def half(*shape):
        return pltpu.VMEM(shape, jnp.bfloat16)

    def full(*shape):
        return pltpu.VMEM(shape, jnp.float32)

    state = full(PLANES, KV_HERE, GROUP * ROWS, 128)
    table = full(4, 2, 64, 64)
    blocks = half(4, 2, 64, HALF)
    chosen = half(4, 4, 2, CAP, HALF)
    pair = full(2, 64, HALF)
    counts = [(8,)] + [
        n
        for n in ((4,), (8,), (8,), (4,), (32,), (4,), (13,), (2,), (2, 2, 4), (2, 4, 4), (4, 4), (2, 4), (2,))
        for _ in range(2)
    ]
    return pl.pallas_call(
        layer_kernel,
        out_shape=[
            jax.ShapeDtypeStruct((64, width), jnp.bfloat16),
            jax.ShapeDtypeStruct((2 * KV_HERE, ROWS // PAGE, PAGE * HEAD_DIM), jnp.bfloat16),
        ],
        in_specs=specs,
        out_specs=[vmem] * 2,
        scratch_shapes=[half(*operands[n].shape) for n in (0, 2, 3, 4, 7, 11, 12)]
        + [
            half(ROWS, 384),
            half(ROWS, 384),
            half(PLANES, ROWS, 384),
            half(LINE // 2, 2 * CACHE_HERE, 256),
            half(ROWS, 256),
            half(LINE, ROWS, 256),
            half(2 * CACHE_HERE, 256),
            half(LINE, ROWS, 256),
            half(PLANES, KV_HERE, GROUP * ROWS, 128),
            state,
            state,
            half(PLANES, ROWS, 512),
            half(PLANES, ROWS, 512),
            full(ROWS, 256),
            full(ROWS // PAGE, PAGE, 256),
            full(4, 64, width),
            half(4, 64, width),
            half(4, 64, width),
            full(64, width),
            table,
            table,
            blocks,
            blocks,
        ]
        + [chosen] * 8
        + [blocks] * 4
        + [pair, pair, half(2, 64, HALF), half(2, 64, HALF)]
        + [pltpu.SemaphoreType.DMA(n) for n in counts],
        compiler_params=pltpu.CompilerParams(
            vmem_limit_bytes=62 * 1024 * 1024, collective_id=1, has_side_effects=True
        ),
        name="layer",
    )(*operands)


def body(
    hidden_in,
    attn_gain,
    q_weight,
    k_weight,
    v_weight,
    o_weight,
    cache_kv,
    moe_gain,
    expert_in,
    expert_out,
    routes,
    route_prob,
    page_slot,
):
    hidden_out, page_slabs = layer(
        hidden_in, attn_gain, q_weight, k_weight, v_weight, cache_kv, page_slot,
        o_weight, moe_gain, routes.T, route_prob.T, expert_in, expert_out,
    )
    page_rows = page_slabs.transpose(1, 0, 2).reshape(ROWS // PAGE, KV_HERE, 2, PAGE * HEAD_DIM)
    return (hidden_out, page_rows)


def solution(mesh):
    return jax.shard_map(
        body,
        mesh=mesh,
        in_specs=(
            P("seq", None),
            P(),
            P(None, "exp"),
            P(None, "exp"),
            P(None, "exp"),
            P("exp", None),
            P("seq", "exp"),
            P(),
            P("seq", None, None),
            P("seq", None, None),
            P(("seq", "exp"), None),
            P(("seq", "exp"), None),
            P(),
        ),
        out_specs=(P(("seq", "exp"), None), P("seq", "exp", None, None)),
        check_vma=False,
    )
```

```python
import functools

import jax
import jax.numpy as jnp
from jax import lax
from jax.experimental import pallas as pl
from jax.experimental.pallas import tpu as pltpu
from jax.sharding import PartitionSpec as P

HEADS_HERE = 6
KV_HERE = 2
GROUP = 3
HEAD_DIM = 64
EXPERTS = 32
CAP = 32
PAGE = 8
PLANES = 4
LINE = 8
ROWS = 256
CACHE_HERE = 512

norm_epsilon = 1e-06
attention_scale = 0.015625
residual_scale = 0.22
masked_score = -1e30


ORDER = ((0, 0), (0, 1), (1, 0), (0, 3), (0, 2), (1, 1), (1, 3), (1, 2))


HALF = 768


def layer_kernel(
    hid_hbm, attn_gain_ref, qw_hbm, kw_hbm, vw_hbm, cache_hbm, slot_ref,
    ow_hbm, moe_gain_ref, routes_ref, prob_ref, win_hbm, wout_hbm, out_ref, page_ref,
    hid_ref, qw_ref, kw_ref, vw_ref, ow_ref, win_ref, wout_ref, att_ref,
    query, q_all, cache_all, new_all, cache_val, qs, best, acc,
    part_send, part_recv, page_send, page_recv,
    sum_send, sum_recv, residual, info_a, info_b, got_a, got_b, send_a, send_b, recv_a, recv_b,
    back_a, back_b, sum_part_a, sum_part_b, red_a, red_b, acc_a, acc_b, last_send, last_recv,
    load_in, q_out, q_in, cache_out, cache_in, new_out, new_in, part_out, part_in, page_out, page_in,
    sum_out, sum_in, info_out, info_in, y_out, y_in, wide_out, wide_in, go_out, go_in,
    ret_out, ret_in, red_out, red_in, last_out, last_in,
):
    seq_index = lax.axis_index("seq")
    plane = seq_index // LINE
    place = seq_index % LINE
    even = plane % 2 == 0
    MESH = pl.DeviceIdType.MESH
    lane = lax.broadcasted_iota(jnp.int32, (ROWS, 2 * HEAD_DIM), 1)
    low = lane < HEAD_DIM
    one = jnp.ones((), jnp.bfloat16)

    def send(source, target, out_sem, in_sem, to):
        return pltpu.make_async_remote_copy(
            src_ref=source, dst_ref=target, send_sem=out_sem, recv_sem=in_sem,
            device_id={"seq": to}, device_id_type=MESH,
        )

    def line_peer(k):
        return lax.rem(plane + k, PLANES) * LINE + place

    def ahead(n):
        return lax.rem(seq_index + n, 32)

    def route(g, n):
        m, j = ORDER[n]
        if g == 0:
            return ((0, 0), (0, 0, j)) if m == 0 else ((0, j), (0, 1, 0))
        if j == 0:
            return (0, 0), (0, 1, 0)
        return (m, 0), (0, 0, j)

    def cache_at(g, n):
        return cache_all.at[g, n // 2, pl.ds((n % 2) * CACHE_HERE, CACHE_HERE)]

    def cache_copy(g, n):
        origin, to = route(g, n)
        return send(
            cache_at(g, ORDER.index(origin)), cache_at(g, n), cache_out.at[g, n], cache_in.at[g, n], at(*to)
        )

    def new_at(g, m, j):
        return new_all.at[g, lax.rem(h + m, 2) * 4 + lax.rem(x + 4 - j, 4)]

    def new_copy(g, n):
        origin, to = route(g, n)
        block = new_at(g, *origin)
        return send(block, block, new_out.at[g, n], new_in.at[g, n], at(*to))

    def new_wait(g, n):
        block = new_at(g, *ORDER[n])
        send(block, block, new_out.at[g, n], new_in.at[g, n], at(0, 1, 0)).wait_recv()

    def query_copy(k):
        return send(query, q_all.at[plane], q_out.at[k], q_in.at[k], line_peer(k))

    def part_copy(k):
        return send(part_send.at[k], part_recv.at[k], part_out.at[k], part_in.at[k], line_peer(k))

    def page_copy(n):
        rows = pl.ds(pl.multiple_of(ahead(n) * PAGE, PAGE), PAGE)
        return send(page_send.at[rows], page_recv.at[seq_index], page_out.at[n], page_in.at[n], ahead(n))

    def sends_query(k):
        return jnp.logical_or(plane < 2, plane == 3) if k == 3 else plane < 2

    def gets_query(k):
        origin = lax.rem(plane + PLANES - k, PLANES)
        return jnp.logical_or(origin < 2, origin == 3) if k == 3 else origin < 2

    def sends_part(k):
        target = lax.rem(plane + k, PLANES)
        return jnp.logical_or(target < 2, target == 3) if k == 1 else target < 2

    def gets_part(k):
        return jnp.logical_or(plane < 2, plane == 3) if k == 1 else plane < 2

    exp_index = lax.axis_index("exp")
    z, h, x = seq_index // 8, lax.rem(seq_index // 4, 2), lax.rem(seq_index, 4)

    def at(dz, dh, dx):
        return lax.rem(z + 4 + dz, 4) * 8 + lax.rem(h + dh, 2) * 4 + lax.rem(x + 4 + dx, 4)

    def side(k):
        return lax.rem(exp_index + k, 4)

    def sum_copy(k):
        return pltpu.make_async_remote_copy(
            src_ref=sum_send.at[k], dst_ref=sum_recv.at[k], send_sem=sum_out.at[k], recv_sem=sum_in.at[k],
            device_id={"exp": side(k)}, device_id_type=MESH,
        )

    z_peers = [(i, m) for i in range(4) for m in range(2) if (i, m) != (0, 0)]
    x_peers = [(j, m) for j in range(1, 4) for m in range(2)]

    def info_copies():
        return [
            send(info_a.at[0, 0], info_a.at[i, m], info_out.at[n], info_in.at[n], at(i, m, 0))
            for n, (i, m) in enumerate(z_peers)
        ] + [
            send(info_a.at[0, 0], info_b.at[j, m], info_out.at[7 + n], info_in.at[7 + n], at(0, m, j))
            for n, (j, m) in enumerate(x_peers)
        ]

    def y_copies():
        return [
            send(got_a.at[0, 0], got_a.at[0, 1], y_out.at[0], y_in.at[0], at(0, 1, 0)),
            send(got_b.at[0, 0], got_b.at[0, 1], y_out.at[1], y_in.at[1], at(0, 1, 0)),
        ]

    def wide_a(i, m):
        return send(got_a.at[0, m], got_a.at[i, m], wide_out.at[0, m, i], wide_in.at[0, m, i], at(i, 0, 0))

    def wide_b(i, m):
        return send(got_b.at[0, m], got_b.at[i, m], wide_out.at[1, m, i], wide_in.at[1, m, i], at(0, 0, i))

    def go_a(k, i):
        return send(send_a.at[k, i], recv_a.at[k, i], go_out.at[0, k, i], go_in.at[0, k, i], at(0, 0, k))

    def go_b(k, i):
        return send(send_b.at[k, i], recv_b.at[k, i], go_out.at[1, k, i], go_in.at[1, k, i], at(k, 0, 0))

    def ret_a(k, i):
        return send(send_a.at[k, i], back_a.at[k, i], ret_out.at[k, i], ret_in.at[k, i], at(0, 0, -k))

    def ret_b(i):
        return send(send_b.at[i], back_b.at[i], ret_out.at[0, i], ret_in.at[0, i], at(-i, 0, 0))

    def sum_a(i):
        return send(sum_part_a.at[i], red_a.at[i], red_out.at[0, i], red_in.at[0, i], at(-i, 0, 0))

    def sum_b(i):
        return send(sum_part_b.at[i], red_b.at[i], red_out.at[1, i], red_in.at[1, i], at(0, 0, -i))

    def last_copy(n):
        return send(last_send.at[n], last_recv.at[n], last_out.at[n], last_in.at[n], at(0, 1, 0))

    barrier = pltpu.get_barrier_semaphore()

    @pl.loop(1, 32)
    def _(n):
        pl.semaphore_signal(barrier, inc=1, device_id={"seq": ahead(n)}, device_id_type=MESH)

    for k in range(1, 4):
        pl.semaphore_signal(barrier, inc=1, device_id={"exp": side(k)}, device_id_type=MESH)

    loads = [
        pltpu.make_async_copy(source, target, load_in.at[n])
        for n, (source, target) in enumerate(
            (
                (hid_hbm, hid_ref), (qw_hbm, qw_ref), (kw_hbm, kw_ref), (vw_hbm, vw_ref), (cache_hbm.at[:, pl.ds(0, 128)], cache_all.at[0, 0, pl.ds(0, CACHE_HERE)]),
                (cache_hbm.at[:, pl.ds(128, 128)], cache_all.at[1, 0, pl.ds(0, CACHE_HERE)]),
                (ow_hbm, ow_ref), (win_hbm, win_ref), (wout_hbm, wout_ref),
            )
        )
    ]
    for load in loads:
        load.start()
    for k in range(1, PLANES):
        @pl.when(jnp.logical_not(gets_part(k)))
        def _():
            part_recv[k, :, :384] = jnp.zeros((ROWS, 384), jnp.bfloat16)
            part_recv[k, :, 384:] = jnp.full((ROWS, 128), masked_score, jnp.bfloat16)

    best[...] = jnp.full_like(best, masked_score)
    acc[...] = jnp.zeros_like(acc)
    loads[0].wait()

    @pl.loop(0, ROWS // 64)
    def _(step):
        rows = pl.ds(pl.multiple_of(step * 64, 64), 64)
        wide = hid_ref[rows, :].astype(jnp.float32)
        spread = lax.rsqrt(jnp.mean(wide * wide, axis=-1, keepdims=True) + norm_epsilon)
        sum_send[step] = (wide * spread * attn_gain_ref[...][None, :]).astype(jnp.bfloat16)

    loads[4].wait()
    loads[5].wait()
    loads[1].wait()
    normed = sum_send[...].reshape(ROWS, 1536)
    query[...] = jnp.dot(normed, qw_ref[...], preferred_element_type=jnp.float32).astype(jnp.bfloat16)
    pl.semaphore_wait(barrier, 31 + 3)
    for k in range(1, PLANES):
        @pl.when(sends_query(k))
        def _():
            query_copy(k).start()

    first_sends = ((1, 2), (0, 1), (0, 3), (0, 4), (0, 2), (1, 1), (1, 3), (1, 4))
    for g, n in first_sends:
        cache_copy(g, n).start()
    loads[2].wait()
    loads[3].wait()
    keys = jnp.dot(normed, kw_ref[...], preferred_element_type=jnp.float32)
    values = jnp.dot(normed, vw_ref[...], preferred_element_type=jnp.float32)
    slabs = [
        jnp.where(low, keys, pltpu.roll(values, HEAD_DIM, 1)).astype(jnp.bfloat16),
        jnp.where(low, pltpu.roll(keys, HEAD_DIM, 1), values).astype(jnp.bfloat16),
    ]
    for g in range(KV_HERE):
        new_all[g, place] = slabs[g]
        page_send[:, g * 128 : (g + 1) * 128] = slabs[g].astype(jnp.float32)
    for g, n in first_sends:
        new_copy(g, n).start()

    @pl.loop(1, 32)
    def _(n):
        page_copy(n).start()

    chosen = routes_ref[...].astype(jnp.float32)
    prob = prob_ref[...]
    prob = prob / jnp.sum(prob, axis=0, keepdims=True)
    expert = lax.broadcasted_iota(jnp.int32, (EXPERTS, 64), 0).astype(jnp.float32)
    hit = jnp.zeros((EXPERTS, 64), jnp.float32)
    share = jnp.zeros((EXPERTS, 64), jnp.float32)
    for k in range(8):
        match = chosen[k : k + 1, :] == expert
        hit = jnp.where(match, 1.0, hit)
        share = jnp.where(match, prob[k : k + 1, :], share)
    before = (
        lax.broadcasted_iota(jnp.int32, (64, 64), 0) <= lax.broadcasted_iota(jnp.int32, (64, 64), 1)
    ).astype(jnp.bfloat16)
    rank = jnp.dot(hit.astype(jnp.bfloat16), before, preferred_element_type=jnp.float32)
    info_a[0, 0, :EXPERTS] = rank * hit
    info_a[0, 0, EXPERTS:] = share
    for copy in info_copies():
        copy.start()

    q_all[plane] = query[...]
    own_rows = pl.ds(pl.multiple_of(seq_index * PAGE, PAGE), PAGE)
    page_recv[seq_index] = page_send[own_rows, :]

    def prepare(t):
        for h in range(HEADS_HERE):
            slab = q_all[t, :, (h // 2) * 128 : (h // 2 + 1) * 128]
            slab = slab.astype(jnp.float32) * attention_scale
            if h % 2:
                slab = pltpu.roll(slab, HEAD_DIM, 1)
            a = h % GROUP
            qs[t, h // GROUP, a * ROWS : (a + 1) * ROWS, :] = jnp.where(low, slab, 0.0).astype(jnp.bfloat16)

    def slab_of(g):
        return slice(g * 128, (g + 1) * 128)

    def update(turns, keys_of, values_of, first_key=None):
        chains = [(t, g, slice(a * ROWS, (a + 1) * ROWS)) for t in turns for g in range(KV_HERE) for a in range(GROUP)]
        raw = [
            lax.dot_general(
                qs[t, g, rows, :], keys_of(g), (((1,), (1,)), ((), ())), preferred_element_type=jnp.float32
            )
            for t, g, rows in chains
        ]
        for (t, g, rows), scores in zip(chains, raw):
            if first_key is not None:
                r = lax.broadcasted_iota(jnp.int32, scores.shape, 0)
                c = lax.broadcasted_iota(jnp.int32, scores.shape, 1)
                scores = jnp.where(c - r <= place * ROWS - first_key, scores, masked_score)
            old = best[t, g, rows, :]
            new = jnp.maximum(old, jnp.max(scores, axis=-1, keepdims=True))
            best[t, g, rows, :] = new
            weights = jnp.exp(scores - new[:, :1]).astype(jnp.bfloat16)
            acc[t, g, rows, :] = acc[t, g, rows, :] * jnp.exp(old - new) + jnp.dot(
                weights, values_of(g), preferred_element_type=jnp.float32
            )

    prepare(plane)
    for k in range(1, PLANES):
        @pl.when(gets_query(k))
        def _():
            query_copy(k).wait_recv()
            prepare(lax.rem(plane + PLANES - k, PLANES))

    def pass_on_cache(*steps):
        for g, n, onward in steps:
            cache_copy(g, n).wait_recv()
            for later in onward:
                cache_copy(g, later).start()

    def pass_on_new(*steps):
        for g, n, onward in steps:
            new_wait(g, n)
            for later in onward:
                new_copy(g, later).start()

    def new_keys(step):
        return lambda g: new_all[g, pl.ds(step * 4, 4)].reshape(1024, 128)

    def new_values(step):
        for g in range(KV_HERE):
            for part in range(4):
                rows = slice(part * ROWS, (part + 1) * ROWS)
                cache_val[g, rows, :] = jnp.where(low, one, new_all[g, step * 4 + part])
        return lambda g: cache_val[g]

    pass_on_cache((1, 2, (5, 6, 7)), (0, 1, (5,)))
    needed = (((1, 1),), ((0, 2), (1, 3)), ((1, 4), (0, 5), (1, 5)), ((0, 6), (1, 6), (0, 7), (1, 7)))

    @pl.loop(0, 4)
    def _(pair):
        for number, waits in enumerate(needed):
            @pl.when(pair == number)
            def _():
                for g, n in waits:
                    cache_copy(g, n).wait_recv()

        for g in range(KV_HERE):
            for part in range(4):
                rows = slice(part * ROWS, (part + 1) * ROWS)
                cache_val[g, rows, :] = jnp.where(low, one, cache_all[g, pair, rows, :])
        update((0, 1), lambda g: cache_all[g, pair], lambda g: cache_val[g])

        @pl.when(pair == 0)
        def _():
            pass_on_cache((0, 3, (6,)), (0, 4, (7,)))
            pass_on_new((1, 2, (5, 6, 7)), (0, 1, (5,)))

        @pl.when(pair == 1)
        def _():
            pass_on_new((0, 3, (6,)), (0, 4, (7,)))

        @pl.when(pair == 2)
        def _():
            for g, n in ((0, 2), (1, 1), (1, 3), (1, 4), (0, 5), (1, 5), (0, 6), (1, 6), (0, 7), (1, 7)):
                new_wait(g, n)

            @pl.loop(0, jnp.where(even, 2, 0))
            def _(step):
                update((plane + 1,), new_keys(step), new_values(step))

    def finish(t):
        heads = []
        for h in range(HEADS_HERE):
            g, rows = h // GROUP, slice((h % GROUP) * ROWS, (h % GROUP + 1) * ROWS)
            part = acc[t, g, rows, :]
            total = part[:, :1]
            heads.append((part / total, best[t, g, rows, :] + jnp.log(total)))
        levels = jnp.zeros((ROWS, 128), jnp.float32)
        for h in range(HEADS_HERE):
            levels = jnp.where(lane % 8 == h, heads[h][1], levels)
        return [
            jnp.where(low, pltpu.roll(heads[2 * p][0], HEAD_DIM, 1), heads[2 * p + 1][0])
            for p in range(HEADS_HERE // 2)
        ], levels

    for k in range(1, PLANES):
        @pl.when(sends_part(k))
        def _():
            pairs, levels = finish(lax.rem(plane + k, PLANES))
            for p in range(HEADS_HERE // 2):
                part_send[k, :, p * 128 : (p + 1) * 128] = pairs[p].astype(jnp.bfloat16)
            high = levels.astype(jnp.bfloat16).astype(jnp.float32)
            rest = levels - high
            middle = rest.astype(jnp.bfloat16).astype(jnp.float32)
            split = jnp.where(lane < 8, high, jnp.where(lane < 16, middle, rest - middle))
            part_send[k, :, 384:512] = split.astype(jnp.bfloat16)
            part_copy(k).start()

    @pl.loop(0, place // 4 + 1)
    def _(step):
        update((plane,), new_keys(step), new_values(step), step * 1024)

    @pl.loop(1, 32)
    def _(n):
        page_copy(n).wait_recv()

    column = lax.broadcasted_iota(jnp.int32, (32, 32), 1)
    block_of = lax.broadcasted_iota(jnp.int32, (32, 1024), 0) * 32 + seq_index
    slots = jnp.sum(
        jnp.where(
            lax.broadcasted_iota(jnp.int32, (32, 1024), 1) == block_of,
            slot_ref[...].astype(jnp.float32)[None, :],
            0.0,
        ),
        axis=1,
        keepdims=True,
    )
    owner = (slots == column.astype(jnp.float32)).astype(jnp.bfloat16)
    low_page = lax.broadcasted_iota(jnp.int32, (32, 128), 1) < HEAD_DIM
    tokens = [
        lax.dot_general(
            owner, page_recv[:, n, :].astype(jnp.bfloat16), (((0,), (0,)), ((), ())),
            preferred_element_type=jnp.float32,
        )
        for n in range(PAGE)
    ]
    for g in range(KV_HERE):
        for n in range(0, PAGE, 2):
            first, second = tokens[n][:, slab_of(g)], tokens[n + 1][:, slab_of(g)]
            cols = slice(n * HEAD_DIM, (n + 2) * HEAD_DIM)
            page_ref[2 * g, :, cols] = jnp.where(low_page, first, pltpu.roll(second, HEAD_DIM, 1)).astype(jnp.bfloat16)
            page_ref[2 * g + 1, :, cols] = jnp.where(low_page, pltpu.roll(first, HEAD_DIM, 1), second).astype(jnp.bfloat16)

    pairs, own_level = finish(plane)
    for k in range(1, PLANES):
        @pl.when(gets_part(k))
        def _():
            part_copy(k).wait_recv()
    levels = [own_level]
    for k in range(1, PLANES):
        slab = part_recv[k, :, 384:512].astype(jnp.float32)
        levels.append(slab + pltpu.roll(slab, 120, 1) + pltpu.roll(slab, 112, 1))
    top = functools.reduce(jnp.maximum, levels)
    shares = [jnp.exp(level - top) for level in levels]
    whole = functools.reduce(jnp.add, shares)
    shares = [share / whole for share in shares]

    def spread(share, p):
        return jnp.where(low, share[:, 2 * p : 2 * p + 1], share[:, 2 * p + 1 : 2 * p + 2])

    for p in range(HEADS_HERE // 2):
        cols = slice(p * 128, (p + 1) * 128)
        value = pairs[p] * spread(shares[0], p)
        for k in range(1, PLANES):
            value = value + part_recv[k, :, cols].astype(jnp.float32) * spread(shares[k], p)
        att_ref[:, cols] = value.astype(jnp.bfloat16)

    for n in range(1, LINE):
        for g in range(KV_HERE):
            cache_copy(g, n).wait_send()
            new_copy(g, n).wait_send()

    for k in range(1, PLANES):
        @pl.when(sends_query(k))
        def _():
            query_copy(k).wait_send()

        @pl.when(sends_part(k))
        def _():
            part_copy(k).wait_send()

    @pl.loop(1, 32)
    def _(n):
        page_copy(n).wait_send()

    loads[6].wait()
    def project(k):
        rows = pl.ds(pl.multiple_of(side(k) * 64, 64), 64)
        return jnp.dot(att_ref[rows, :], ow_ref[...], preferred_element_type=jnp.float32)

    for k in (2, 1, 3):
        sum_send[k] = project(k).astype(jnp.bfloat16)
        sum_copy(k).start()
    mixed = project(0)
    for k in range(1, 4):
        sum_copy(k).wait_recv()
        mixed = mixed + sum_recv[k].astype(jnp.float32)
    rows = pl.ds(pl.multiple_of(exp_index * 64, 64), 64)
    after = hid_ref[rows, :].astype(jnp.float32) + residual_scale * mixed
    residual[...] = after
    inverse = lax.rsqrt(jnp.mean(after * after, axis=-1, keepdims=True) + norm_epsilon)
    moe_in = (after * inverse * moe_gain_ref[...][None, :]).astype(jnp.bfloat16)
    got_a[0, 0] = moe_in[:, :HALF]
    got_b[0, 0] = moe_in[:, HALF:]
    for copy in y_copies():
        copy.start()
    for i in (1, 3, 2):
        wide_a(i, 0).start()
        wide_b(i, 0).start()
    for copy in info_copies():
        copy.wait_recv()
    info_b[0] = info_a[0]

    slot = lax.broadcasted_iota(jnp.int32, (CAP, 64), 0).astype(jnp.float32) + 1.0

    def experts_a(k):
        return z * 8 + h * 4 + lax.rem(x + k, 4)

    def experts_b(k):
        return lax.rem(z + k, 4) * 8 + h * 4 + x

    def picks(info, i, m, experts_of):
        return jnp.concatenate(
            [(info[i, m, pl.ds(experts_of(k), 1), :] == slot).astype(jnp.float32) for k in range(4)], axis=0
        ).astype(jnp.bfloat16)

    def mixes(info, i, m, experts_of):
        return jnp.concatenate(
            [
                jnp.where(
                    info[i, m, pl.ds(experts_of(k), 1), :] == slot,
                    info[i, m, pl.ds(EXPERTS + experts_of(k), 1), :],
                    0.0,
                )
                for k in range(4)
            ],
            axis=0,
        ).astype(jnp.bfloat16)

    def pick(info, got, experts_of, sends, recvs, i, m):
        taken = jnp.dot(
            picks(info, i, m, experts_of), got[i, m], preferred_element_type=jnp.float32
        ).astype(jnp.bfloat16)
        recvs[0, i, m] = taken[:CAP]
        for k in range(1, 4):
            sends[k, i, m] = taken[k * CAP : (k + 1) * CAP]

    @pl.loop(0, 4)
    def _(i):
        @pl.when(i == 0)
        def _():
            for copy in y_copies():
                copy.wait_recv()
            for n in (1, 3, 2):
                wide_a(n, 1).start()
                wide_b(n, 1).start()

        @pl.when(i > 0)
        def _():
            for m in range(2):
                wide_a(i, m).wait_recv()
                wide_b(i, m).wait_recv()

        for m in range(2):
            pick(info_a, got_a, experts_a, send_a, recv_a, i, m)
        for k in range(1, 4):
            go_a(k, i).start()
        for m in range(2):
            pick(info_b, got_b, experts_b, send_b, recv_b, i, m)
        for k in range(1, 4):
            go_b(k, i).start()

    loads[7].wait()
    loads[8].wait()

    @pl.loop(0, 4)
    def _(i):
        for k in range(1, 4):
            go_a(k, i).wait_recv()
            go_a(k, i).wait_send()

        @pl.when(i > 0)
        def _():
            for j in range(4):
                copy = send(
                    send_b.at[i, j], recv_b.at[i, j], go_out.at[1, i, j], go_in.at[1, i, j], at(i, 0, 0)
                )
                copy.wait_recv()
                copy.wait_send()

        hidden = jnp.dot(
            recv_a[:, i].reshape(256, HALF), win_ref[0, :HALF, :], preferred_element_type=jnp.float32
        ) + jnp.dot(recv_b[i].reshape(256, HALF), win_ref[0, HALF:, :], preferred_element_type=jnp.float32)
        gate, up = hidden[:, :512], hidden[:, 512:]
        active = (gate / (1.0 + jnp.exp(-gate)) * up).astype(jnp.bfloat16)
        done = jnp.dot(active, wout_ref[0], preferred_element_type=jnp.float32).astype(jnp.bfloat16)
        done_a = done[:, :HALF].reshape(4, 2, CAP, HALF)
        back_a[0, i] = done_a[0]
        for k in range(1, 4):
            send_a[k, i] = done_a[k]
            ret_a(k, i).start()
        send_b[i] = done[:, HALF:].reshape(4, 2, CAP, HALF)

        @pl.when(i > 0)
        def _():
            ret_b(i).start()

        @pl.when(i == 0)
        def _():
            back_b[0] = send_b[0]

    def mix(info, backs, experts_of, i, m):
        return lax.dot_general(
            mixes(info, i, m, experts_of), backs[:, i, m].reshape(4 * CAP, HALF),
            (((0,), (0,)), ((), ())), preferred_element_type=jnp.float32,
        )

    @pl.loop(0, 4)
    def _(i):
        for k in range(1, 4):
            ret_a(k, i).wait_recv()
        for m in range(2):
            some = mix(info_a, back_a, experts_a, i, m)
            sum_part_a[i, m] = some.astype(jnp.bfloat16)

            @pl.when(i == 0)
            def _():
                acc_a[m] = some

        @pl.when(i > 0)
        def _():
            sum_a(i).start()

    for i in range(1, 4):
        ret_b(i).wait_recv()

    @pl.loop(0, 4)
    def _(n):
        i = 3 - n
        for m in range(2):
            some = mix(info_b, back_b, experts_b, i, m)
            sum_part_b[i, m] = some.astype(jnp.bfloat16)

            @pl.when(i == 0)
            def _():
                acc_b[m] = some

        @pl.when(i > 0)
        def _():
            sum_b(i).start()

    for n, (copy, half_acc, red) in enumerate(((sum_a, acc_a, red_a), (sum_b, acc_b, red_b))):
        for i in range(1, 4):
            copy(i).wait_recv()
            half_acc[...] += red[i].astype(jnp.float32)
        last_send[n] = half_acc[1].astype(jnp.bfloat16)
        last_copy(n).start()
    for n, half_acc in enumerate((acc_a, acc_b)):
        last_copy(n).wait_recv()
        cols = slice(n * HALF, (n + 1) * HALF)
        moe = half_acc[0] + last_recv[n].astype(jnp.float32)
        out_ref[:, cols] = (residual[:, cols] + residual_scale * moe).astype(jnp.bfloat16)

    for k in range(1, 4):
        sum_copy(k).wait_send()
    for copy in info_copies() + y_copies():
        copy.wait_send()
    for n in range(2):
        last_copy(n).wait_send()

    @pl.loop(1, 4)
    def _(i):
        for m in range(2):
            wide_a(i, m).wait_send()
            wide_b(i, m).wait_send()
        ret_b(i).wait_send()
        sum_a(i).wait_send()
        sum_b(i).wait_send()

    @pl.loop(0, 4)
    def _(i):
        for k in range(1, 4):
            ret_a(k, i).wait_send()


def layer(*operands):
    vmem = pl.BlockSpec(memory_space=pltpu.VMEM)
    hbm = pl.BlockSpec(memory_space=pl.ANY)
    specs = [hbm, vmem, hbm, hbm, hbm, hbm, vmem, hbm, vmem, vmem, vmem, hbm, hbm]
    width = 1536

    def half(*shape):
        return pltpu.VMEM(shape, jnp.bfloat16)

    def full(*shape):
        return pltpu.VMEM(shape, jnp.float32)

    state = full(PLANES, KV_HERE, GROUP * ROWS, 128)
    table = full(4, 2, 64, 64)
    blocks = half(4, 2, 64, HALF)
    chosen = half(4, 4, 2, CAP, HALF)
    pair = full(2, 64, HALF)
    counts = [(9,)] + [
        n
        for n in ((4,), (2, 8), (2, 8), (4,), (32,), (4,), (13,), (2,), (2, 2, 4), (2, 4, 4), (4, 4), (2, 4), (2,))
        for _ in range(2)
    ]
    return pl.pallas_call(
        layer_kernel,
        out_shape=[
            jax.ShapeDtypeStruct((64, width), jnp.bfloat16),
            jax.ShapeDtypeStruct((2 * KV_HERE, ROWS // PAGE, PAGE * HEAD_DIM), jnp.bfloat16),
        ],
        in_specs=specs,
        out_specs=[vmem] * 2,
        scratch_shapes=[half(*operands[n].shape) for n in (0, 2, 3, 4, 7, 11, 12)]
        + [
            half(ROWS, 384),
            half(ROWS, 384),
            half(PLANES, ROWS, 384),
            half(KV_HERE, LINE // 2, 2 * CACHE_HERE, 128),
            half(KV_HERE, LINE, ROWS, 128),
            half(KV_HERE, 2 * CACHE_HERE, 128),
            half(PLANES, KV_HERE, GROUP * ROWS, 128),
            state,
            state,
            half(PLANES, ROWS, 512),
            half(PLANES, ROWS, 512),
            full(ROWS, 256),
            full(ROWS // PAGE, PAGE, 256),
            half(4, 64, width),
            half(4, 64, width),
            full(64, width),
            table,
            table,
            blocks,
            blocks,
        ]
        + [chosen] * 6
        + [blocks] * 4
        + [pair, pair, half(2, 64, HALF), half(2, 64, HALF)]
        + [pltpu.SemaphoreType.DMA(n) for n in counts],
        compiler_params=pltpu.CompilerParams(
            vmem_limit_bytes=62 * 1024 * 1024, collective_id=1, has_side_effects=True
        ),
        name="layer",
    )(*operands)


def body(
    hidden_in,
    attn_gain,
    q_weight,
    k_weight,
    v_weight,
    o_weight,
    cache_kv,
    moe_gain,
    expert_in,
    expert_out,
    routes,
    route_prob,
    page_slot,
):
    hidden_out, page_slabs = layer(
        hidden_in, attn_gain, q_weight, k_weight, v_weight, cache_kv, page_slot,
        o_weight, moe_gain, routes.T, route_prob.T, expert_in, expert_out,
    )
    page_rows = page_slabs.transpose(1, 0, 2).reshape(ROWS // PAGE, KV_HERE, 2, PAGE * HEAD_DIM)
    return (hidden_out, page_rows)


def solution(mesh):
    return jax.shard_map(
        body,
        mesh=mesh,
        in_specs=(
            P("seq", None),
            P(),
            P(None, "exp"),
            P(None, "exp"),
            P(None, "exp"),
            P("exp", None),
            P("seq", "exp"),
            P(),
            P("seq", None, None),
            P("seq", None, None),
            P(("seq", "exp"), None),
            P(("seq", "exp"), None),
            P(),
        ),
        out_specs=(P(("seq", "exp"), None), P("seq", "exp", None, None)),
        check_vma=False,
    )
```

```python
import functools

import jax
import jax.numpy as jnp
from jax import lax
from jax.experimental import pallas as pl
from jax.experimental.pallas import tpu as pltpu
from jax.sharding import PartitionSpec as P

HEADS_HERE = 6
KV_HERE = 2
GROUP = 3
HEAD_DIM = 64
EXPERTS = 32
CAP = 32
PAGE = 8
PLANES = 4
LINE = 8
ROWS = 256
CACHE_HERE = 512

norm_epsilon = 1e-06
attention_scale = 0.015625
residual_scale = 0.22
masked_score = -1e30


ORDER = ((0, 0), (0, 1), (1, 0), (0, 3), (0, 2), (1, 1), (1, 3), (1, 2))


HALF = 768


def layer_kernel(
    hid_hbm, attn_gain_ref, qw_hbm, kw_hbm, vw_hbm, cache_hbm, slot_ref,
    ow_hbm, moe_gain_ref, routes_ref, prob_ref, win_hbm, wout_hbm, out_ref, page_ref,
    hid_ref, qw_ref, kw_ref, vw_ref, ow_ref, win_ref, wout_ref, att_ref,
    query, q_all, cache_all, new_all, cache_val, qs, best, acc,
    part_send, part_recv, level_send, level_recv, page_send, page_recv,
    core_send, core_recv, chip_send, chip_recv, normed, residual, info_a, info_b, got_a, got_b, send_a, send_b, recv_a, recv_b,
    back_a, back_b, sum_part_a, sum_part_b, red_a, red_b, acc_a, acc_b, last_send, last_recv,
    load_in, q_out, q_in, cache_out, cache_in, new_out, new_in, part_out, part_in, level_out, level_in, page_out, page_in,
    sum_out, sum_in, info_out, info_in, y_out, y_in, wide_out, wide_in, go_out, go_in,
    ret_out, ret_in, red_out, red_in, last_out, last_in,
):
    seq_index = lax.axis_index("seq")
    plane = seq_index // LINE
    place = seq_index % LINE
    even = plane % 2 == 0
    MESH = pl.DeviceIdType.MESH
    lane = lax.broadcasted_iota(jnp.int32, (ROWS, 2 * HEAD_DIM), 1)
    low = lane < HEAD_DIM
    one = jnp.ones((), jnp.bfloat16)

    def send(source, target, out_sem, in_sem, to):
        return pltpu.make_async_remote_copy(
            src_ref=source, dst_ref=target, send_sem=out_sem, recv_sem=in_sem,
            device_id={"seq": to}, device_id_type=MESH,
        )

    def line_peer(k):
        return lax.rem(plane + k, PLANES) * LINE + place

    def ahead(n):
        return lax.rem(seq_index + n, 32)

    def route(g, n):
        m, j = ORDER[n]
        if g == 0:
            return ((0, 0), (0, 0, j)) if m == 0 else ((0, j), (0, 1, 0))
        if j == 0:
            return (0, 0), (0, 1, 0)
        return (m, 0), (0, 0, j)

    def cache_at(g, n):
        return cache_all.at[g, n // 2, pl.ds((n % 2) * CACHE_HERE, CACHE_HERE)]

    def cache_copy(g, n):
        origin, to = route(g, n)
        return send(
            cache_at(g, ORDER.index(origin)), cache_at(g, n), cache_out.at[g, n], cache_in.at[g, n], at(*to)
        )

    def new_at(g, m, j):
        return new_all.at[g, lax.rem(h + m, 2) * 4 + lax.rem(x + 4 - j, 4)]

    def new_copy(g, n):
        origin, to = route(g, n)
        block = new_at(g, *origin)
        return send(block, block, new_out.at[g, n], new_in.at[g, n], at(*to))

    def new_wait(g, n):
        block = new_at(g, *ORDER[n])
        send(block, block, new_out.at[g, n], new_in.at[g, n], at(0, 1, 0)).wait_recv()

    def query_copy(k):
        return send(query, q_all.at[plane], q_out.at[k], q_in.at[k], line_peer(k))

    def part_copy(k):
        return send(part_send.at[k], part_recv.at[k], part_out.at[k], part_in.at[k], line_peer(k))

    def level_copy(k):
        return send(level_send.at[k], level_recv.at[k], level_out.at[k], level_in.at[k], line_peer(k))

    def page_copy(n):
        rows = pl.ds(pl.multiple_of(ahead(n) * PAGE, PAGE), PAGE)
        return send(page_send.at[rows], page_recv.at[seq_index], page_out.at[n], page_in.at[n], ahead(n))

    def sends_query(k):
        return jnp.logical_or(plane < 2, plane == 3) if k == 3 else plane < 2

    def gets_query(k):
        origin = lax.rem(plane + PLANES - k, PLANES)
        return jnp.logical_or(origin < 2, origin == 3) if k == 3 else origin < 2

    def sends_part(k):
        target = lax.rem(plane + k, PLANES)
        return jnp.logical_or(target < 2, target == 3) if k == 1 else target < 2

    def gets_part(k):
        return jnp.logical_or(plane < 2, plane == 3) if k == 1 else plane < 2

    exp_index = lax.axis_index("exp")
    z, h, x = seq_index // 8, lax.rem(seq_index // 4, 2), lax.rem(seq_index, 4)

    def at(dz, dh, dx):
        return lax.rem(z + 4 + dz, 4) * 8 + lax.rem(h + dh, 2) * 4 + lax.rem(x + 4 + dx, 4)

    def side(k):
        return lax.rem(exp_index + k, 4)

    core = lax.rem(exp_index, 2)
    chip = exp_index // 2

    def sum_copy(n):
        to = chip * 2 + 1 - core if n == 0 else (1 - chip) * 2 + core
        source, target = ((core_send, core_recv), (chip_send, chip_recv))[n]
        return pltpu.make_async_remote_copy(
            src_ref=source, dst_ref=target, send_sem=sum_out.at[n], recv_sem=sum_in.at[n],
            device_id={"exp": to}, device_id_type=MESH,
        )

    z_peers = [(i, m) for i in range(4) for m in range(2) if (i, m) != (0, 0)]
    x_peers = [(j, m) for j in range(1, 4) for m in range(2)]

    def info_copies():
        return [
            send(info_a.at[0, 0], info_a.at[i, m], info_out.at[n], info_in.at[n], at(i, m, 0))
            for n, (i, m) in enumerate(z_peers)
        ] + [
            send(info_a.at[0, 0], info_b.at[j, m], info_out.at[7 + n], info_in.at[7 + n], at(0, m, j))
            for n, (j, m) in enumerate(x_peers)
        ]

    def y_copies():
        return [
            send(got_a.at[0, 0], got_a.at[0, 1], y_out.at[0], y_in.at[0], at(0, 1, 0)),
            send(got_b.at[0, 0], got_b.at[0, 1], y_out.at[1], y_in.at[1], at(0, 1, 0)),
        ]

    def wide_a(i, m):
        return send(got_a.at[0, m], got_a.at[i, m], wide_out.at[0, m, i], wide_in.at[0, m, i], at(i, 0, 0))

    def wide_b(i, m):
        return send(got_b.at[0, m], got_b.at[i, m], wide_out.at[1, m, i], wide_in.at[1, m, i], at(0, 0, i))

    def go_a(k, i):
        return send(send_a.at[k, i], recv_a.at[k, i], go_out.at[0, k, i], go_in.at[0, k, i], at(0, 0, k))

    def go_b(k, i):
        return send(send_b.at[k, i], recv_b.at[k, i], go_out.at[1, k, i], go_in.at[1, k, i], at(k, 0, 0))

    def ret_a(k, i):
        return send(send_a.at[k, i], back_a.at[k, i], ret_out.at[k, i], ret_in.at[k, i], at(0, 0, -k))

    def ret_b(i):
        return send(send_b.at[i], back_b.at[i], ret_out.at[0, i], ret_in.at[0, i], at(-i, 0, 0))

    def sum_a(i):
        return send(sum_part_a.at[i], red_a.at[i], red_out.at[0, i], red_in.at[0, i], at(-i, 0, 0))

    def sum_b(i):
        return send(sum_part_b.at[i], red_b.at[i], red_out.at[1, i], red_in.at[1, i], at(0, 0, -i))

    def last_copy(n):
        return send(last_send.at[n], last_recv.at[n], last_out.at[n], last_in.at[n], at(0, 1, 0))

    barrier = pltpu.get_barrier_semaphore()

    @pl.loop(1, 32)
    def _(n):
        pl.semaphore_signal(barrier, inc=1, device_id={"seq": ahead(n)}, device_id_type=MESH)

    for k in range(1, 4):
        pl.semaphore_signal(barrier, inc=1, device_id={"exp": side(k)}, device_id_type=MESH)

    loads = [
        pltpu.make_async_copy(source, target, load_in.at[n])
        for n, (source, target) in enumerate(
            (
                (hid_hbm, hid_ref), (qw_hbm, qw_ref), (kw_hbm, kw_ref), (vw_hbm, vw_ref), (cache_hbm.at[:, pl.ds(0, 128)], cache_all.at[0, 0, pl.ds(0, CACHE_HERE)]),
                (cache_hbm.at[:, pl.ds(128, 128)], cache_all.at[1, 0, pl.ds(0, CACHE_HERE)]),
                (ow_hbm, ow_ref), (win_hbm, win_ref), (wout_hbm, wout_ref),
            )
        )
    ]
    for load in loads:
        load.start()
    for k in range(1, PLANES):
        @pl.when(jnp.logical_not(gets_part(k)))
        def _():
            part_recv[k] = jnp.zeros((ROWS, 384), jnp.bfloat16)
            level_recv[k] = jnp.full((8, ROWS), masked_score, jnp.float32)

    best[...] = jnp.full_like(best, masked_score)
    acc[...] = jnp.zeros_like(acc)
    loads[0].wait()

    @pl.loop(0, ROWS // 64)
    def _(step):
        rows = pl.ds(pl.multiple_of(step * 64, 64), 64)
        wide = hid_ref[rows, :].astype(jnp.float32)
        spread = lax.rsqrt(jnp.mean(wide * wide, axis=-1, keepdims=True) + norm_epsilon)
        normed[rows, :] = (wide * spread * attn_gain_ref[...][None, :]).astype(jnp.bfloat16)

    loads[4].wait()
    loads[5].wait()
    loads[1].wait()
    query[...] = jnp.dot(normed[...], qw_ref[...], preferred_element_type=jnp.float32).astype(jnp.bfloat16)
    pl.semaphore_wait(barrier, 31 + 3)
    for k in range(1, PLANES):
        @pl.when(sends_query(k))
        def _():
            query_copy(k).start()

    first_sends = ((1, 2), (0, 1), (0, 3), (0, 4), (0, 2), (1, 1), (1, 3), (1, 4))
    for g, n in first_sends:
        cache_copy(g, n).start()
    loads[2].wait()
    loads[3].wait()
    keys = jnp.dot(normed[...], kw_ref[...], preferred_element_type=jnp.float32)
    values = jnp.dot(normed[...], vw_ref[...], preferred_element_type=jnp.float32)
    slabs = [
        jnp.where(low, keys, pltpu.roll(values, HEAD_DIM, 1)).astype(jnp.bfloat16),
        jnp.where(low, pltpu.roll(keys, HEAD_DIM, 1), values).astype(jnp.bfloat16),
    ]
    for g in range(KV_HERE):
        new_all[g, place] = slabs[g]
        page_send[:, g * 128 : (g + 1) * 128] = slabs[g].astype(jnp.float32)
    for g, n in first_sends:
        new_copy(g, n).start()

    @pl.loop(1, 32)
    def _(n):
        page_copy(n).start()

    chosen = routes_ref[...].astype(jnp.float32)
    prob = prob_ref[...]
    prob = prob / jnp.sum(prob, axis=0, keepdims=True)
    expert = lax.broadcasted_iota(jnp.int32, (EXPERTS, 64), 0).astype(jnp.float32)
    hit = jnp.zeros((EXPERTS, 64), jnp.float32)
    share = jnp.zeros((EXPERTS, 64), jnp.float32)
    for k in range(8):
        match = chosen[k : k + 1, :] == expert
        hit = jnp.where(match, 1.0, hit)
        share = jnp.where(match, prob[k : k + 1, :], share)
    before = (
        lax.broadcasted_iota(jnp.int32, (64, 64), 0) <= lax.broadcasted_iota(jnp.int32, (64, 64), 1)
    ).astype(jnp.bfloat16)
    rank = jnp.dot(hit.astype(jnp.bfloat16), before, preferred_element_type=jnp.float32)
    info_a[0, 0, :EXPERTS] = rank * hit
    info_a[0, 0, EXPERTS:] = share
    for copy in info_copies():
        copy.start()

    q_all[plane] = query[...]
    own_rows = pl.ds(pl.multiple_of(seq_index * PAGE, PAGE), PAGE)
    page_recv[seq_index] = page_send[own_rows, :]

    def prepare(t):
        for h in range(HEADS_HERE):
            slab = q_all[t, :, (h // 2) * 128 : (h // 2 + 1) * 128]
            slab = slab.astype(jnp.float32) * attention_scale
            if h % 2:
                slab = pltpu.roll(slab, HEAD_DIM, 1)
            a = h % GROUP
            qs[t, h // GROUP, a * ROWS : (a + 1) * ROWS, :] = jnp.where(low, slab, 0.0).astype(jnp.bfloat16)

    def slab_of(g):
        return slice(g * 128, (g + 1) * 128)

    def update(turns, keys_of, values_of, first_key=None):
        chains = [(t, g, slice(a * ROWS, (a + 1) * ROWS)) for t in turns for g in range(KV_HERE) for a in range(GROUP)]
        raw = [
            lax.dot_general(
                qs[t, g, rows, :], keys_of(g), (((1,), (1,)), ((), ())), preferred_element_type=jnp.float32
            )
            for t, g, rows in chains
        ]
        for (t, g, rows), scores in zip(chains, raw):
            if first_key is not None:
                r = lax.broadcasted_iota(jnp.int32, scores.shape, 0)
                c = lax.broadcasted_iota(jnp.int32, scores.shape, 1)
                scores = jnp.where(c - r <= place * ROWS - first_key, scores, masked_score)
            old = best[t, g, rows, :]
            new = jnp.maximum(old, jnp.max(scores, axis=-1, keepdims=True))
            best[t, g, rows, :] = new
            weights = jnp.exp(scores - new[:, :1]).astype(jnp.bfloat16)
            acc[t, g, rows, :] = acc[t, g, rows, :] * jnp.exp(old - new) + jnp.dot(
                weights, values_of(g), preferred_element_type=jnp.float32
            )

    prepare(plane)
    for k in range(1, PLANES):
        @pl.when(gets_query(k))
        def _():
            query_copy(k).wait_recv()
            prepare(lax.rem(plane + PLANES - k, PLANES))

    def pass_on_cache(*steps):
        for g, n, onward in steps:
            cache_copy(g, n).wait_recv()
            for later in onward:
                cache_copy(g, later).start()

    def pass_on_new(*steps):
        for g, n, onward in steps:
            new_wait(g, n)
            for later in onward:
                new_copy(g, later).start()

    def new_keys(step):
        return lambda g: new_all[g, pl.ds(step * 4, 4)].reshape(1024, 128)

    def new_values(step):
        for g in range(KV_HERE):
            for part in range(4):
                rows = slice(part * ROWS, (part + 1) * ROWS)
                cache_val[g, rows, :] = jnp.where(low, one, new_all[g, step * 4 + part])
        return lambda g: cache_val[g]

    pass_on_cache((1, 2, (5, 6, 7)), (0, 1, (5,)))
    needed = (((1, 1),), ((0, 2), (1, 3)), ((1, 4), (0, 5), (1, 5)), ((0, 6), (1, 6), (0, 7), (1, 7)))

    @pl.loop(0, 4)
    def _(pair):
        for number, waits in enumerate(needed):
            @pl.when(pair == number)
            def _():
                for g, n in waits:
                    cache_copy(g, n).wait_recv()

        for g in range(KV_HERE):
            for part in range(4):
                rows = slice(part * ROWS, (part + 1) * ROWS)
                cache_val[g, rows, :] = jnp.where(low, one, cache_all[g, pair, rows, :])
        update((0, 1), lambda g: cache_all[g, pair], lambda g: cache_val[g])

        @pl.when(pair == 0)
        def _():
            pass_on_cache((0, 3, (6,)), (0, 4, (7,)))
            pass_on_new((1, 2, (5, 6, 7)), (0, 1, (5,)))

        @pl.when(pair == 1)
        def _():
            pass_on_new((0, 3, (6,)), (0, 4, (7,)))

        @pl.when(pair == 2)
        def _():
            for g, n in ((0, 2), (1, 1), (1, 3), (1, 4), (0, 5), (1, 5), (0, 6), (1, 6), (0, 7), (1, 7)):
                new_wait(g, n)

            @pl.loop(0, jnp.where(even, 2, 0))
            def _(step):
                update((plane + 1,), new_keys(step), new_values(step))

    def finish(t):
        heads = []
        for h in range(HEADS_HERE):
            g, rows = h // GROUP, slice((h % GROUP) * ROWS, (h % GROUP + 1) * ROWS)
            part = acc[t, g, rows, :]
            total = part[:, :1]
            heads.append((part / total, best[t, g, rows, :] + jnp.log(total)))
        levels = jnp.zeros((ROWS, 128), jnp.float32)
        for h in range(HEADS_HERE):
            levels = jnp.where(lane % 8 == h, heads[h][1], levels)
        return [
            jnp.where(low, pltpu.roll(heads[2 * p][0], HEAD_DIM, 1), heads[2 * p + 1][0])
            for p in range(HEADS_HERE // 2)
        ], levels

    for k in range(1, PLANES):
        @pl.when(sends_part(k))
        def _():
            pairs, levels = finish(lax.rem(plane + k, PLANES))
            for p in range(HEADS_HERE // 2):
                part_send[k, :, p * 128 : (p + 1) * 128] = pairs[p].astype(jnp.bfloat16)
            level_send[k] = levels.T[:8, :]
            level_copy(k).start()
            part_copy(k).start()

    @pl.loop(0, place // 4 + 1)
    def _(step):
        update((plane,), new_keys(step), new_values(step), step * 1024)

    @pl.loop(1, 32)
    def _(n):
        page_copy(n).wait_recv()

    column = lax.broadcasted_iota(jnp.int32, (32, 32), 1)
    block_of = lax.broadcasted_iota(jnp.int32, (32, 1024), 0) * 32 + seq_index
    slots = jnp.sum(
        jnp.where(
            lax.broadcasted_iota(jnp.int32, (32, 1024), 1) == block_of,
            slot_ref[...].astype(jnp.float32)[None, :],
            0.0,
        ),
        axis=1,
        keepdims=True,
    )
    owner = (slots == column.astype(jnp.float32)).astype(jnp.bfloat16)
    low_page = lax.broadcasted_iota(jnp.int32, (32, 128), 1) < HEAD_DIM
    tokens = [
        lax.dot_general(
            owner, page_recv[:, n, :].astype(jnp.bfloat16), (((0,), (0,)), ((), ())),
            preferred_element_type=jnp.float32,
        )
        for n in range(PAGE)
    ]
    for g in range(KV_HERE):
        for n in range(0, PAGE, 2):
            first, second = tokens[n][:, slab_of(g)], tokens[n + 1][:, slab_of(g)]
            cols = slice(n * HEAD_DIM, (n + 2) * HEAD_DIM)
            page_ref[2 * g, :, cols] = jnp.where(low_page, first, pltpu.roll(second, HEAD_DIM, 1)).astype(jnp.bfloat16)
            page_ref[2 * g + 1, :, cols] = jnp.where(low_page, pltpu.roll(first, HEAD_DIM, 1), second).astype(jnp.bfloat16)

    pairs, own_level = finish(plane)
    for k in range(1, PLANES):
        @pl.when(gets_part(k))
        def _():
            part_copy(k).wait_recv()
            level_copy(k).wait_recv()
    levels = [own_level]
    for k in range(1, PLANES):
        levels.append(jnp.concatenate([level_recv[k]] * 16, axis=0).T)
    top = functools.reduce(jnp.maximum, levels)
    shares = [jnp.exp(level - top) for level in levels]
    whole = functools.reduce(jnp.add, shares)
    shares = [share / whole for share in shares]

    def spread(share, p):
        return jnp.where(low, share[:, 2 * p : 2 * p + 1], share[:, 2 * p + 1 : 2 * p + 2])

    for p in range(HEADS_HERE // 2):
        cols = slice(p * 128, (p + 1) * 128)
        value = pairs[p] * spread(shares[0], p)
        for k in range(1, PLANES):
            value = value + part_recv[k, :, cols].astype(jnp.float32) * spread(shares[k], p)
        att_ref[:, cols] = value.astype(jnp.bfloat16)

    for n in range(1, LINE):
        for g in range(KV_HERE):
            cache_copy(g, n).wait_send()
            new_copy(g, n).wait_send()

    for k in range(1, PLANES):
        @pl.when(sends_query(k))
        def _():
            query_copy(k).wait_send()

        @pl.when(sends_part(k))
        def _():
            part_copy(k).wait_send()
            level_copy(k).wait_send()

    @pl.loop(1, 32)
    def _(n):
        page_copy(n).wait_send()

    loads[6].wait()
    def project(of_chip, of_core):
        rows = pl.ds(pl.multiple_of((of_chip * 2 + of_core) * 64, 64), 64)
        return jnp.dot(att_ref[rows, :], ow_ref[...], preferred_element_type=jnp.float32)

    core_send[0] = project(1 - chip, 1 - core).astype(jnp.bfloat16)
    core_send[1] = project(chip, 1 - core).astype(jnp.bfloat16)
    sum_copy(0).start()
    away = project(1 - chip, core)
    mixed = project(chip, core)
    sum_copy(0).wait_recv()
    chip_send[...] = (away + core_recv[0].astype(jnp.float32)).astype(jnp.bfloat16)
    sum_copy(1).start()
    mixed = mixed + core_recv[1].astype(jnp.float32)
    sum_copy(1).wait_recv()
    mixed = mixed + chip_recv[...].astype(jnp.float32)
    rows = pl.ds(pl.multiple_of(exp_index * 64, 64), 64)
    after = hid_ref[rows, :].astype(jnp.float32) + residual_scale * mixed
    residual[...] = after
    inverse = lax.rsqrt(jnp.mean(after * after, axis=-1, keepdims=True) + norm_epsilon)
    moe_in = (after * inverse * moe_gain_ref[...][None, :]).astype(jnp.bfloat16)
    got_a[0, 0] = moe_in[:, :HALF]
    got_b[0, 0] = moe_in[:, HALF:]
    for copy in y_copies():
        copy.start()
    for i in (1, 3, 2):
        wide_a(i, 0).start()
        wide_b(i, 0).start()
    for copy in info_copies():
        copy.wait_recv()
    info_b[0] = info_a[0]

    slot = lax.broadcasted_iota(jnp.int32, (CAP, 64), 0).astype(jnp.float32) + 1.0

    def experts_a(k):
        return z * 8 + h * 4 + lax.rem(x + k, 4)

    def experts_b(k):
        return lax.rem(z + k, 4) * 8 + h * 4 + x

    def picks(info, i, m, experts_of):
        return jnp.concatenate(
            [(info[i, m, pl.ds(experts_of(k), 1), :] == slot).astype(jnp.float32) for k in range(4)], axis=0
        ).astype(jnp.bfloat16)

    def mixes(info, i, m, experts_of):
        return jnp.concatenate(
            [
                jnp.where(
                    info[i, m, pl.ds(experts_of(k), 1), :] == slot,
                    info[i, m, pl.ds(EXPERTS + experts_of(k), 1), :],
                    0.0,
                )
                for k in range(4)
            ],
            axis=0,
        ).astype(jnp.bfloat16)

    def pick(info, got, experts_of, sends, recvs, i, m):
        taken = jnp.dot(
            picks(info, i, m, experts_of), got[i, m], preferred_element_type=jnp.float32
        ).astype(jnp.bfloat16)
        recvs[0, i, m] = taken[:CAP]
        for k in range(1, 4):
            sends[k, i, m] = taken[k * CAP : (k + 1) * CAP]

    @pl.loop(0, 4)
    def _(i):
        @pl.when(i == 0)
        def _():
            for copy in y_copies():
                copy.wait_recv()
            for n in (1, 3, 2):
                wide_a(n, 1).start()
                wide_b(n, 1).start()

        @pl.when(i > 0)
        def _():
            for m in range(2):
                wide_a(i, m).wait_recv()
                wide_b(i, m).wait_recv()

        for m in range(2):
            pick(info_a, got_a, experts_a, send_a, recv_a, i, m)
        for k in range(1, 4):
            go_a(k, i).start()
        for m in range(2):
            pick(info_b, got_b, experts_b, send_b, recv_b, i, m)
        for k in range(1, 4):
            go_b(k, i).start()

    loads[7].wait()
    loads[8].wait()

    @pl.loop(0, 4)
    def _(i):
        for k in range(1, 4):
            go_a(k, i).wait_recv()
            go_a(k, i).wait_send()

        @pl.when(i > 0)
        def _():
            for j in range(4):
                copy = send(
                    send_b.at[i, j], recv_b.at[i, j], go_out.at[1, i, j], go_in.at[1, i, j], at(i, 0, 0)
                )
                copy.wait_recv()
                copy.wait_send()

        hidden = jnp.dot(
            recv_a[:, i].reshape(256, HALF), win_ref[0, :HALF, :], preferred_element_type=jnp.float32
        ) + jnp.dot(recv_b[i].reshape(256, HALF), win_ref[0, HALF:, :], preferred_element_type=jnp.float32)
        gate, up = hidden[:, :512], hidden[:, 512:]
        active = (gate / (1.0 + jnp.exp(-gate)) * up).astype(jnp.bfloat16)
        done = jnp.dot(active, wout_ref[0], preferred_element_type=jnp.float32).astype(jnp.bfloat16)
        done_a = done[:, :HALF].reshape(4, 2, CAP, HALF)
        back_a[0, i] = done_a[0]
        for k in range(1, 4):
            send_a[k, i] = done_a[k]
            ret_a(k, i).start()
        send_b[i] = done[:, HALF:].reshape(4, 2, CAP, HALF)

        @pl.when(i > 0)
        def _():
            ret_b(i).start()

        @pl.when(i == 0)
        def _():
            back_b[0] = send_b[0]

    def mix(info, backs, experts_of, i, m):
        return lax.dot_general(
            mixes(info, i, m, experts_of), backs[:, i, m].reshape(4 * CAP, HALF),
            (((0,), (0,)), ((), ())), preferred_element_type=jnp.float32,
        )

    @pl.loop(0, 4)
    def _(i):
        for k in range(1, 4):
            ret_a(k, i).wait_recv()
        for m in range(2):
            some = mix(info_a, back_a, experts_a, i, m)
            sum_part_a[i, m] = some.astype(jnp.bfloat16)

            @pl.when(i == 0)
            def _():
                acc_a[m] = some

        @pl.when(i > 0)
        def _():
            sum_a(i).start()

    for i in range(1, 4):
        ret_b(i).wait_recv()

    @pl.loop(0, 4)
    def _(n):
        i = 3 - n
        for m in range(2):
            some = mix(info_b, back_b, experts_b, i, m)
            sum_part_b[i, m] = some.astype(jnp.bfloat16)

            @pl.when(i == 0)
            def _():
                acc_b[m] = some

        @pl.when(i > 0)
        def _():
            sum_b(i).start()

    for n, (copy, half_acc, red) in enumerate(((sum_a, acc_a, red_a), (sum_b, acc_b, red_b))):
        for i in range(1, 4):
            copy(i).wait_recv()
            half_acc[...] += red[i].astype(jnp.float32)
        last_send[n] = half_acc[1].astype(jnp.bfloat16)
        last_copy(n).start()
    for n, half_acc in enumerate((acc_a, acc_b)):
        last_copy(n).wait_recv()
        cols = slice(n * HALF, (n + 1) * HALF)
        moe = half_acc[0] + last_recv[n].astype(jnp.float32)
        out_ref[:, cols] = (residual[:, cols] + residual_scale * moe).astype(jnp.bfloat16)

    for n in range(2):
        sum_copy(n).wait_send()
    for copy in info_copies() + y_copies():
        copy.wait_send()
    for n in range(2):
        last_copy(n).wait_send()

    @pl.loop(1, 4)
    def _(i):
        for m in range(2):
            wide_a(i, m).wait_send()
            wide_b(i, m).wait_send()
        ret_b(i).wait_send()
        sum_a(i).wait_send()
        sum_b(i).wait_send()

    @pl.loop(0, 4)
    def _(i):
        for k in range(1, 4):
            ret_a(k, i).wait_send()


def layer(*operands):
    vmem = pl.BlockSpec(memory_space=pltpu.VMEM)
    hbm = pl.BlockSpec(memory_space=pl.ANY)
    specs = [hbm, vmem, hbm, hbm, hbm, hbm, vmem, hbm, vmem, vmem, vmem, hbm, hbm]
    width = 1536

    def half(*shape):
        return pltpu.VMEM(shape, jnp.bfloat16)

    def full(*shape):
        return pltpu.VMEM(shape, jnp.float32)

    state = full(PLANES, KV_HERE, GROUP * ROWS, 128)
    table = full(4, 2, 64, 64)
    blocks = half(4, 2, 64, HALF)
    chosen = half(4, 4, 2, CAP, HALF)
    pair = full(2, 64, HALF)
    counts = [(9,)] + [
        n
        for n in ((4,), (2, 8), (2, 8), (4,), (4,), (32,), (2,), (13,), (2,), (2, 2, 4), (2, 4, 4), (4, 4), (2, 4), (2,))
        for _ in range(2)
    ]
    return pl.pallas_call(
        layer_kernel,
        out_shape=[
            jax.ShapeDtypeStruct((64, width), jnp.bfloat16),
            jax.ShapeDtypeStruct((2 * KV_HERE, ROWS // PAGE, PAGE * HEAD_DIM), jnp.bfloat16),
        ],
        in_specs=specs,
        out_specs=[vmem] * 2,
        scratch_shapes=[half(*operands[n].shape) for n in (0, 2, 3, 4, 7, 11, 12)]
        + [
            half(ROWS, 384),
            half(ROWS, 384),
            half(PLANES, ROWS, 384),
            half(KV_HERE, LINE // 2, 2 * CACHE_HERE, 128),
            half(KV_HERE, LINE, ROWS, 128),
            half(KV_HERE, 2 * CACHE_HERE, 128),
            half(PLANES, KV_HERE, GROUP * ROWS, 128),
            state,
            state,
            half(PLANES, ROWS, 384),
            half(PLANES, ROWS, 384),
            full(PLANES, 8, ROWS),
            full(PLANES, 8, ROWS),
            full(ROWS, 256),
            full(ROWS // PAGE, PAGE, 256),
            half(2, 64, width),
            half(2, 64, width),
            half(64, width),
            half(64, width),
            half(ROWS, width),
            full(64, width),
            table,
            table,
            blocks,
            blocks,
        ]
        + [chosen] * 6
        + [blocks] * 4
        + [pair, pair, half(2, 64, HALF), half(2, 64, HALF)]
        + [pltpu.SemaphoreType.DMA(n) for n in counts],
        compiler_params=pltpu.CompilerParams(
            vmem_limit_bytes=62 * 1024 * 1024, collective_id=1, has_side_effects=True
        ),
        name="layer",
    )(*operands)


def body(
    hidden_in,
    attn_gain,
    q_weight,
    k_weight,
    v_weight,
    o_weight,
    cache_kv,
    moe_gain,
    expert_in,
    expert_out,
    routes,
    route_prob,
    page_slot,
):
    hidden_out, page_slabs = layer(
        hidden_in, attn_gain, q_weight, k_weight, v_weight, cache_kv, page_slot,
        o_weight, moe_gain, routes.T, route_prob.T, expert_in, expert_out,
    )
    page_rows = page_slabs.transpose(1, 0, 2).reshape(ROWS // PAGE, KV_HERE, 2, PAGE * HEAD_DIM)
    return (hidden_out, page_rows)


def solution(mesh):
    return jax.shard_map(
        body,
        mesh=mesh,
        in_specs=(
            P("seq", None),
            P(),
            P(None, "exp"),
            P(None, "exp"),
            P(None, "exp"),
            P("exp", None),
            P("seq", "exp"),
            P(),
            P("seq", None, None),
            P("seq", None, None),
            P(("seq", "exp"), None),
            P(("seq", "exp"), None),
            P(),
        ),
        out_specs=(P(("seq", "exp"), None), P("seq", "exp", None, None)),
        check_vma=False,
    )
```

```python
import functools

import jax
import jax.numpy as jnp
from jax import lax
from jax.experimental import pallas as pl
from jax.experimental.pallas import tpu as pltpu
from jax.sharding import PartitionSpec as P

HEADS_HERE = 6
KV_HERE = 2
GROUP = 3
HEAD_DIM = 64
EXPERTS = 32
CAP = 32
PAGE = 8
PLANES = 4
LINE = 8
ROWS = 256
CACHE_HERE = 512

norm_epsilon = 1e-06
attention_scale = 0.015625
residual_scale = 0.22
masked_score = -1e30


ORDER = ((0, 0), (0, 1), (1, 0), (0, 3), (0, 2), (1, 1), (1, 3), (1, 2))


HALF = 768


def layer_kernel(
    hid_hbm, attn_gain_ref, qw_hbm, kw_hbm, vw_hbm, cache_hbm, slot_ref,
    ow_hbm, moe_gain_ref, routes_ref, prob_ref, win_hbm, wout_hbm, out_ref, page_ref,
    hid_ref, qw_ref, kw_ref, vw_ref, ow_ref, win_ref, wout_ref, att_ref,
    query, q_all, cache_all, new_all, cache_val, qs, best, acc,
    part_send, part_recv, level_send, level_recv, page_send, page_recv,
    core_send, core_recv, chip_send, chip_recv, normed, residual, info_a, info_b, got_a, got_b, send_a, send_b, recv_a, recv_b,
    back_a, back_b, sum_part_a, sum_part_b, red_a, red_b, acc_a, acc_b, last_send, last_recv,
    load_in, q_out, q_in, cache_out, cache_in, new_out, new_in, part_out, part_in, level_out, level_in, page_out, page_in,
    sum_out, sum_in, info_out, info_in, y_out, y_in, wide_out, wide_in, go_out, go_in,
    ret_out, ret_in, red_out, red_in, last_out, last_in,
):
    seq_index = lax.axis_index("seq")
    plane = seq_index // LINE
    place = seq_index % LINE
    even = plane % 2 == 0
    MESH = pl.DeviceIdType.MESH
    lane = lax.broadcasted_iota(jnp.int32, (ROWS, 2 * HEAD_DIM), 1)
    low = lane < HEAD_DIM
    one = jnp.ones((), jnp.bfloat16)

    def send(source, target, out_sem, in_sem, to):
        return pltpu.make_async_remote_copy(
            src_ref=source, dst_ref=target, send_sem=out_sem, recv_sem=in_sem,
            device_id={"seq": to}, device_id_type=MESH,
        )

    def line_peer(k):
        return lax.rem(plane + k, PLANES) * LINE + place

    def ahead(n):
        return lax.rem(seq_index + n, 32)

    def route(g, n):
        m, j = ORDER[n]
        if g == 0:
            return ((0, 0), (0, 0, j)) if m == 0 else ((0, j), (0, 1, 0))
        if j == 0:
            return (0, 0), (0, 1, 0)
        return (m, 0), (0, 0, j)

    def cache_at(g, n):
        return cache_all.at[g, n // 2, pl.ds((n % 2) * CACHE_HERE, CACHE_HERE)]

    def cache_copy(g, n):
        origin, to = route(g, n)
        return send(
            cache_at(g, ORDER.index(origin)), cache_at(g, n), cache_out.at[g, n], cache_in.at[g, n], at(*to)
        )

    def new_at(g, m, j):
        return new_all.at[g, lax.rem(h + m, 2) * 4 + lax.rem(x + 4 - j, 4)]

    def new_copy(g, n):
        origin, to = route(g, n)
        block = new_at(g, *origin)
        return send(block, block, new_out.at[g, n], new_in.at[g, n], at(*to))

    def new_wait(g, n):
        block = new_at(g, *ORDER[n])
        send(block, block, new_out.at[g, n], new_in.at[g, n], at(0, 1, 0)).wait_recv()

    def query_copy(k):
        return send(query, q_all.at[plane], q_out.at[k], q_in.at[k], line_peer(k))

    def part_copy(k):
        return send(part_send.at[k], part_recv.at[k], part_out.at[k], part_in.at[k], line_peer(k))

    def level_copy(k):
        return send(level_send.at[k], level_recv.at[k], level_out.at[k], level_in.at[k], line_peer(k))

    def page_copy(n):
        rows = pl.ds(pl.multiple_of(ahead(n) * PAGE, PAGE), PAGE)
        return send(page_send.at[rows], page_recv.at[seq_index], page_out.at[n], page_in.at[n], ahead(n))

    def sends_query(k):
        return jnp.logical_or(plane < 2, plane == 3) if k == 3 else plane < 2

    def gets_query(k):
        origin = lax.rem(plane + PLANES - k, PLANES)
        return jnp.logical_or(origin < 2, origin == 3) if k == 3 else origin < 2

    def sends_part(k):
        target = lax.rem(plane + k, PLANES)
        return jnp.logical_or(target < 2, target == 3) if k == 1 else target < 2

    def gets_part(k):
        return jnp.logical_or(plane < 2, plane == 3) if k == 1 else plane < 2

    exp_index = lax.axis_index("exp")
    z, h, x = seq_index // 8, lax.rem(seq_index // 4, 2), lax.rem(seq_index, 4)

    def at(dz, dh, dx):
        return lax.rem(z + 4 + dz, 4) * 8 + lax.rem(h + dh, 2) * 4 + lax.rem(x + 4 + dx, 4)

    def side(k):
        return lax.rem(exp_index + k, 4)

    core = lax.rem(exp_index, 2)
    chip = exp_index // 2

    def sum_copy(n):
        to = chip * 2 + 1 - core if n == 0 else (1 - chip) * 2 + core
        source, target = ((core_send, core_recv), (chip_send, chip_recv))[n]
        return pltpu.make_async_remote_copy(
            src_ref=source, dst_ref=target, send_sem=sum_out.at[n], recv_sem=sum_in.at[n],
            device_id={"exp": to}, device_id_type=MESH,
        )

    z_peers = [(i, m) for i in range(4) for m in range(2) if (i, m) != (0, 0)]
    x_peers = [(j, m) for j in range(1, 4) for m in range(2)]

    def info_copies():
        return [
            send(info_a.at[0, 0], info_a.at[i, m], info_out.at[n], info_in.at[n], at(i, m, 0))
            for n, (i, m) in enumerate(z_peers)
        ] + [
            send(info_a.at[0, 0], info_b.at[j, m], info_out.at[7 + n], info_in.at[7 + n], at(0, m, j))
            for n, (j, m) in enumerate(x_peers)
        ]

    def y_copies():
        return [
            send(got_a.at[0, 0], got_a.at[0, 1], y_out.at[0], y_in.at[0], at(0, 1, 0)),
            send(got_b.at[0, 0], got_b.at[0, 1], y_out.at[1], y_in.at[1], at(0, 1, 0)),
        ]

    def wide_a(i, m):
        return send(got_a.at[0, m], got_a.at[i, m], wide_out.at[0, m, i], wide_in.at[0, m, i], at(i, 0, 0))

    def wide_b(i, m):
        return send(got_b.at[0, m], got_b.at[i, m], wide_out.at[1, m, i], wide_in.at[1, m, i], at(0, 0, i))

    def go_a(k, i):
        return send(send_a.at[k, i], recv_a.at[k, i], go_out.at[0, k, i], go_in.at[0, k, i], at(0, 0, k))

    def go_b(k, i):
        return send(send_b.at[k, i], recv_b.at[k, i], go_out.at[1, k, i], go_in.at[1, k, i], at(k, 0, 0))

    def ret_a(k, i):
        return send(send_a.at[k, i], back_a.at[k, i], ret_out.at[k, i], ret_in.at[k, i], at(0, 0, -k))

    def ret_b(i):
        return send(send_b.at[i], back_b.at[i], ret_out.at[0, i], ret_in.at[0, i], at(-i, 0, 0))

    def sum_a(i):
        return send(sum_part_a.at[i], red_a.at[i], red_out.at[0, i], red_in.at[0, i], at(-i, 0, 0))

    def sum_b(i):
        return send(sum_part_b.at[i], red_b.at[i], red_out.at[1, i], red_in.at[1, i], at(0, 0, -i))

    def last_copy(n):
        return send(last_send.at[n], last_recv.at[n], last_out.at[n], last_in.at[n], at(0, 1, 0))

    barrier = pltpu.get_barrier_semaphore()

    @pl.loop(1, 32)
    def _(n):
        pl.semaphore_signal(barrier, inc=1, device_id={"seq": ahead(n)}, device_id_type=MESH)

    for k in range(1, 4):
        pl.semaphore_signal(barrier, inc=1, device_id={"exp": side(k)}, device_id_type=MESH)

    loads = [
        pltpu.make_async_copy(source, target, load_in.at[n])
        for n, (source, target) in enumerate(
            (
                (hid_hbm, hid_ref), (qw_hbm, qw_ref), (kw_hbm, kw_ref), (vw_hbm, vw_ref), (cache_hbm.at[:, pl.ds(0, 128)], cache_all.at[0, 0, pl.ds(0, CACHE_HERE)]),
                (cache_hbm.at[:, pl.ds(128, 128)], cache_all.at[1, 0, pl.ds(0, CACHE_HERE)]),
                (ow_hbm, ow_ref), (win_hbm, win_ref), (wout_hbm, wout_ref),
            )
        )
    ]
    for load in loads:
        load.start()
    for k in range(1, PLANES):
        @pl.when(jnp.logical_not(gets_part(k)))
        def _():
            part_recv[k] = jnp.zeros((ROWS, 384), jnp.bfloat16)
            level_recv[k] = jnp.full((8, ROWS), masked_score, jnp.float32)

    best[...] = jnp.full_like(best, masked_score)
    acc[...] = jnp.zeros_like(acc)
    loads[0].wait()

    @pl.loop(0, ROWS // 64)
    def _(step):
        rows = pl.ds(pl.multiple_of(step * 64, 64), 64)
        wide = hid_ref[rows, :].astype(jnp.float32)
        spread = lax.rsqrt(jnp.mean(wide * wide, axis=-1, keepdims=True) + norm_epsilon)
        normed[rows, :] = (wide * spread * attn_gain_ref[...][None, :]).astype(jnp.bfloat16)

    loads[4].wait()
    loads[5].wait()
    loads[1].wait()
    query[...] = jnp.dot(normed[...], qw_ref[...], preferred_element_type=jnp.float32).astype(jnp.bfloat16)
    pl.semaphore_wait(barrier, 31 + 3)
    for k in range(1, PLANES):
        @pl.when(sends_query(k))
        def _():
            query_copy(k).start()

    first_sends = ((1, 2), (0, 1), (0, 3), (0, 4), (0, 2), (1, 1), (1, 3), (1, 4))
    for g, n in first_sends:
        cache_copy(g, n).start()
    loads[2].wait()
    loads[3].wait()
    keys = jnp.dot(normed[...], kw_ref[...], preferred_element_type=jnp.float32)
    values = jnp.dot(normed[...], vw_ref[...], preferred_element_type=jnp.float32)
    slabs = [
        jnp.where(low, keys, pltpu.roll(values, HEAD_DIM, 1)).astype(jnp.bfloat16),
        jnp.where(low, pltpu.roll(keys, HEAD_DIM, 1), values).astype(jnp.bfloat16),
    ]
    for g in range(KV_HERE):
        new_all[g, place] = slabs[g]
        page_send[:, g * 128 : (g + 1) * 128] = slabs[g].astype(jnp.float32)
    for g, n in first_sends:
        new_copy(g, n).start()

    @pl.loop(1, 32)
    def _(n):
        page_copy(n).start()

    chosen = routes_ref[...].astype(jnp.float32)
    prob = prob_ref[...]
    prob = prob / jnp.sum(prob, axis=0, keepdims=True)
    expert = lax.broadcasted_iota(jnp.int32, (EXPERTS, 64), 0).astype(jnp.float32)
    hit = jnp.zeros((EXPERTS, 64), jnp.float32)
    share = jnp.zeros((EXPERTS, 64), jnp.float32)
    for k in range(8):
        match = chosen[k : k + 1, :] == expert
        hit = jnp.where(match, 1.0, hit)
        share = jnp.where(match, prob[k : k + 1, :], share)
    before = (
        lax.broadcasted_iota(jnp.int32, (64, 64), 0) <= lax.broadcasted_iota(jnp.int32, (64, 64), 1)
    ).astype(jnp.bfloat16)
    rank = jnp.dot(hit.astype(jnp.bfloat16), before, preferred_element_type=jnp.float32)
    info_a[0, 0, :EXPERTS] = rank * hit
    info_a[0, 0, EXPERTS:] = share
    for copy in info_copies():
        copy.start()

    q_all[plane] = query[...]
    own_rows = pl.ds(pl.multiple_of(seq_index * PAGE, PAGE), PAGE)
    page_recv[seq_index] = page_send[own_rows, :]

    def prepare(t):
        for h in range(HEADS_HERE):
            slab = q_all[t, :, (h // 2) * 128 : (h // 2 + 1) * 128]
            slab = slab.astype(jnp.float32) * attention_scale
            if h % 2:
                slab = pltpu.roll(slab, HEAD_DIM, 1)
            a = h % GROUP
            qs[t, h // GROUP, a * ROWS : (a + 1) * ROWS, :] = jnp.where(low, slab, 0.0).astype(jnp.bfloat16)

    def slab_of(g):
        return slice(g * 128, (g + 1) * 128)

    def update(turns, keys_of, values_of, first_key=None):
        chains = [(t, g, slice(a * ROWS, (a + 1) * ROWS)) for t in turns for g in range(KV_HERE) for a in range(GROUP)]
        raw = [
            lax.dot_general(
                qs[t, g, rows, :], keys_of(g), (((1,), (1,)), ((), ())), preferred_element_type=jnp.float32
            )
            for t, g, rows in chains
        ]
        for (t, g, rows), scores in zip(chains, raw):
            if first_key is not None:
                r = lax.broadcasted_iota(jnp.int32, scores.shape, 0)
                c = lax.broadcasted_iota(jnp.int32, scores.shape, 1)
                scores = jnp.where(c - r <= place * ROWS - first_key, scores, masked_score)
            old = best[t, g, rows, :]
            new = jnp.maximum(old, jnp.max(scores, axis=-1, keepdims=True))
            best[t, g, rows, :] = new
            weights = jnp.exp(scores - new[:, :1]).astype(jnp.bfloat16)
            acc[t, g, rows, :] = acc[t, g, rows, :] * jnp.exp(old - new) + jnp.dot(
                weights, values_of(g), preferred_element_type=jnp.float32
            )

    prepare(plane)
    for k in range(1, PLANES):
        @pl.when(gets_query(k))
        def _():
            query_copy(k).wait_recv()
            prepare(lax.rem(plane + PLANES - k, PLANES))

    def pass_on_cache(*steps):
        for g, n, onward in steps:
            cache_copy(g, n).wait_recv()
            for later in onward:
                cache_copy(g, later).start()

    def pass_on_new(*steps):
        for g, n, onward in steps:
            new_wait(g, n)
            for later in onward:
                new_copy(g, later).start()

    def new_keys(step):
        return lambda g: new_all[g, pl.ds(step * 4, 4)].reshape(1024, 128)

    def new_values(step):
        for g in range(KV_HERE):
            for part in range(4):
                rows = slice(part * ROWS, (part + 1) * ROWS)
                cache_val[g, rows, :] = jnp.where(low, one, new_all[g, step * 4 + part])
        return lambda g: cache_val[g]

    pass_on_cache((1, 2, (5, 6, 7)), (0, 1, (5,)))
    needed = (((1, 1),), ((0, 2), (1, 3)), ((1, 4), (0, 5), (1, 5)), ((0, 6), (1, 6), (0, 7), (1, 7)))

    @pl.loop(0, 4)
    def _(pair):
        for number, waits in enumerate(needed):
            @pl.when(pair == number)
            def _():
                for g, n in waits:
                    cache_copy(g, n).wait_recv()

        for g in range(KV_HERE):
            for part in range(4):
                rows = slice(part * ROWS, (part + 1) * ROWS)
                cache_val[g, rows, :] = jnp.where(low, one, cache_all[g, pair, rows, :])
        update((0, 1), lambda g: cache_all[g, pair], lambda g: cache_val[g])

        @pl.when(pair == 0)
        def _():
            pass_on_cache((0, 3, (6,)), (0, 4, (7,)))
            pass_on_new((1, 2, (5, 6, 7)), (0, 1, (5,)))

        @pl.when(pair == 1)
        def _():
            pass_on_new((0, 3, (6,)), (0, 4, (7,)))

    def finish(t):
        heads = []
        for h in range(HEADS_HERE):
            g, rows = h // GROUP, slice((h % GROUP) * ROWS, (h % GROUP + 1) * ROWS)
            part = acc[t, g, rows, :]
            total = part[:, :1]
            heads.append((part / total, best[t, g, rows, :] + jnp.log(total)))
        levels = jnp.zeros((ROWS, 128), jnp.float32)
        for h in range(HEADS_HERE):
            levels = jnp.where(lane % 8 == h, heads[h][1], levels)
        return [
            jnp.where(low, pltpu.roll(heads[2 * p][0], HEAD_DIM, 1), heads[2 * p + 1][0])
            for p in range(HEADS_HERE // 2)
        ], levels

    def send_part(k):
        @pl.when(sends_part(k))
        def _():
            pairs, levels = finish(lax.rem(plane + k, PLANES))
            for p in range(HEADS_HERE // 2):
                part_send[k, :, p * 128 : (p + 1) * 128] = pairs[p].astype(jnp.bfloat16)
            level_send[k] = levels.T[:8, :]
            level_copy(k).start()
            part_copy(k).start()

    send_part(2)
    send_part(3)
    for g, n in ((0, 2), (1, 1), (1, 3), (1, 4), (0, 5), (1, 5), (0, 6), (1, 6), (0, 7), (1, 7)):
        new_wait(g, n)

    @pl.loop(0, jnp.where(even, 2, 0))
    def _(step):
        update((plane + 1,), new_keys(step), new_values(step))

    send_part(1)

    @pl.loop(0, place // 4 + 1)
    def _(step):
        update((plane,), new_keys(step), new_values(step), step * 1024)

    @pl.loop(1, 32)
    def _(n):
        page_copy(n).wait_recv()

    column = lax.broadcasted_iota(jnp.int32, (32, 32), 1)
    block_of = lax.broadcasted_iota(jnp.int32, (32, 1024), 0) * 32 + seq_index
    slots = jnp.sum(
        jnp.where(
            lax.broadcasted_iota(jnp.int32, (32, 1024), 1) == block_of,
            slot_ref[...].astype(jnp.float32)[None, :],
            0.0,
        ),
        axis=1,
        keepdims=True,
    )
    owner = (slots == column.astype(jnp.float32)).astype(jnp.bfloat16)
    low_page = lax.broadcasted_iota(jnp.int32, (32, 128), 1) < HEAD_DIM
    tokens = [
        lax.dot_general(
            owner, page_recv[:, n, :].astype(jnp.bfloat16), (((0,), (0,)), ((), ())),
            preferred_element_type=jnp.float32,
        )
        for n in range(PAGE)
    ]
    for g in range(KV_HERE):
        for n in range(0, PAGE, 2):
            first, second = tokens[n][:, slab_of(g)], tokens[n + 1][:, slab_of(g)]
            cols = slice(n * HEAD_DIM, (n + 2) * HEAD_DIM)
            page_ref[2 * g, :, cols] = jnp.where(low_page, first, pltpu.roll(second, HEAD_DIM, 1)).astype(jnp.bfloat16)
            page_ref[2 * g + 1, :, cols] = jnp.where(low_page, pltpu.roll(first, HEAD_DIM, 1), second).astype(jnp.bfloat16)

    pairs, own_level = finish(plane)
    for k in range(1, PLANES):
        @pl.when(gets_part(k))
        def _():
            part_copy(k).wait_recv()
            level_copy(k).wait_recv()
    levels = [own_level]
    for k in range(1, PLANES):
        levels.append(jnp.concatenate([level_recv[k]] * 16, axis=0).T)
    top = functools.reduce(jnp.maximum, levels)
    shares = [jnp.exp(level - top) for level in levels]
    whole = functools.reduce(jnp.add, shares)
    shares = [share / whole for share in shares]

    def spread(share, p):
        return jnp.where(low, share[:, 2 * p : 2 * p + 1], share[:, 2 * p + 1 : 2 * p + 2])

    for p in range(HEADS_HERE // 2):
        cols = slice(p * 128, (p + 1) * 128)
        value = pairs[p] * spread(shares[0], p)
        for k in range(1, PLANES):
            value = value + part_recv[k, :, cols].astype(jnp.float32) * spread(shares[k], p)
        att_ref[:, cols] = value.astype(jnp.bfloat16)

    for n in range(1, LINE):
        for g in range(KV_HERE):
            cache_copy(g, n).wait_send()
            new_copy(g, n).wait_send()

    for k in range(1, PLANES):
        @pl.when(sends_query(k))
        def _():
            query_copy(k).wait_send()

        @pl.when(sends_part(k))
        def _():
            part_copy(k).wait_send()
            level_copy(k).wait_send()

    @pl.loop(1, 32)
    def _(n):
        page_copy(n).wait_send()

    loads[6].wait()
    def project(of_chip, of_core):
        rows = pl.ds(pl.multiple_of((of_chip * 2 + of_core) * 64, 64), 64)
        return jnp.dot(att_ref[rows, :], ow_ref[...], preferred_element_type=jnp.float32)

    core_send[0] = project(1 - chip, 1 - core).astype(jnp.bfloat16)
    core_send[1] = project(chip, 1 - core).astype(jnp.bfloat16)
    sum_copy(0).start()
    away = project(1 - chip, core)
    mixed = project(chip, core)
    sum_copy(0).wait_recv()
    chip_send[...] = (away + core_recv[0].astype(jnp.float32)).astype(jnp.bfloat16)
    sum_copy(1).start()
    mixed = mixed + core_recv[1].astype(jnp.float32)
    sum_copy(1).wait_recv()
    mixed = mixed + chip_recv[...].astype(jnp.float32)
    rows = pl.ds(pl.multiple_of(exp_index * 64, 64), 64)
    after = hid_ref[rows, :].astype(jnp.float32) + residual_scale * mixed
    residual[...] = after
    inverse = lax.rsqrt(jnp.mean(after * after, axis=-1, keepdims=True) + norm_epsilon)
    moe_in = (after * inverse * moe_gain_ref[...][None, :]).astype(jnp.bfloat16)
    got_a[0, 0] = moe_in[:, :HALF]
    got_b[0, 0] = moe_in[:, HALF:]
    for copy in y_copies():
        copy.start()
    for i in (1, 3, 2):
        wide_a(i, 0).start()
        wide_b(i, 0).start()
    for copy in info_copies():
        copy.wait_recv()
    info_b[0] = info_a[0]

    slot = lax.broadcasted_iota(jnp.int32, (CAP, 64), 0).astype(jnp.float32) + 1.0

    def experts_a(k):
        return z * 8 + h * 4 + lax.rem(x + k, 4)

    def experts_b(k):
        return lax.rem(z + k, 4) * 8 + h * 4 + x

    def picks(info, i, m, experts_of):
        return jnp.concatenate(
            [(info[i, m, pl.ds(experts_of(k), 1), :] == slot).astype(jnp.float32) for k in range(4)], axis=0
        ).astype(jnp.bfloat16)

    def mixes(info, i, m, experts_of):
        return jnp.concatenate(
            [
                jnp.where(
                    info[i, m, pl.ds(experts_of(k), 1), :] == slot,
                    info[i, m, pl.ds(EXPERTS + experts_of(k), 1), :],
                    0.0,
                )
                for k in range(4)
            ],
            axis=0,
        ).astype(jnp.bfloat16)

    def pick(info, got, experts_of, sends, recvs, i, m):
        taken = jnp.dot(
            picks(info, i, m, experts_of), got[i, m], preferred_element_type=jnp.float32
        ).astype(jnp.bfloat16)
        recvs[0, i, m] = taken[:CAP]
        for k in range(1, 4):
            sends[k, i, m] = taken[k * CAP : (k + 1) * CAP]

    @pl.loop(0, 4)
    def _(turn):
        i = turn + (turn // 2) * (5 - 2 * turn)

        @pl.when(i == 0)
        def _():
            for copy in y_copies():
                copy.wait_recv()
            for n in (1, 3, 2):
                wide_a(n, 1).start()
                wide_b(n, 1).start()

        @pl.when(i > 0)
        def _():
            for m in range(2):
                wide_a(i, m).wait_recv()
                wide_b(i, m).wait_recv()

        for m in range(2):
            pick(info_a, got_a, experts_a, send_a, recv_a, i, m)
        for k in range(1, 4):
            go_a(k, i).start()
        for m in range(2):
            pick(info_b, got_b, experts_b, send_b, recv_b, i, m)
        for k in range(1, 4):
            go_b(k, i).start()

    loads[7].wait()
    loads[8].wait()

    @pl.loop(0, 4)
    def _(turn):
        i = turn + (turn // 2) * (5 - 2 * turn)

        for k in range(1, 4):
            go_a(k, i).wait_recv()
            go_a(k, i).wait_send()

        @pl.when(i > 0)
        def _():
            for j in range(4):
                copy = send(
                    send_b.at[i, j], recv_b.at[i, j], go_out.at[1, i, j], go_in.at[1, i, j], at(i, 0, 0)
                )
                copy.wait_recv()
                copy.wait_send()

        hidden = jnp.dot(
            recv_a[:, i].reshape(256, HALF), win_ref[0, :HALF, :], preferred_element_type=jnp.float32
        ) + jnp.dot(recv_b[i].reshape(256, HALF), win_ref[0, HALF:, :], preferred_element_type=jnp.float32)
        gate, up = hidden[:, :512], hidden[:, 512:]
        active = (gate / (1.0 + jnp.exp(-gate)) * up).astype(jnp.bfloat16)
        done = jnp.dot(active, wout_ref[0], preferred_element_type=jnp.float32).astype(jnp.bfloat16)
        done_a = done[:, :HALF].reshape(4, 2, CAP, HALF)
        back_a[0, i] = done_a[0]
        for k in range(1, 4):
            send_a[k, i] = done_a[k]
            ret_a(k, i).start()
        send_b[i] = done[:, HALF:].reshape(4, 2, CAP, HALF)

        @pl.when(i > 0)
        def _():
            ret_b(i).start()

        @pl.when(i == 0)
        def _():
            back_b[0] = send_b[0]

    def mix(info, backs, experts_of, i, m):
        return lax.dot_general(
            mixes(info, i, m, experts_of), backs[:, i, m].reshape(4 * CAP, HALF),
            (((0,), (0,)), ((), ())), preferred_element_type=jnp.float32,
        )

    @pl.loop(0, 4)
    def _(turn):
        i = turn + (turn // 2) * (5 - 2 * turn)

        for k in range(1, 4):
            ret_a(k, i).wait_recv()
        for m in range(2):
            some = mix(info_a, back_a, experts_a, i, m)
            sum_part_a[i, m] = some.astype(jnp.bfloat16)

            @pl.when(i == 0)
            def _():
                acc_a[m] = some

        @pl.when(i > 0)
        def _():
            sum_a(i).start()

    for i in range(1, 4):
        ret_b(i).wait_recv()

    @pl.loop(0, 4)
    def _(n):
        i = 3 - n
        for m in range(2):
            some = mix(info_b, back_b, experts_b, i, m)
            sum_part_b[i, m] = some.astype(jnp.bfloat16)

            @pl.when(i == 0)
            def _():
                acc_b[m] = some

        @pl.when(i > 0)
        def _():
            sum_b(i).start()

    for n, (copy, half_acc, red) in enumerate(((sum_a, acc_a, red_a), (sum_b, acc_b, red_b))):
        for i in range(1, 4):
            copy(i).wait_recv()
            half_acc[...] += red[i].astype(jnp.float32)
        last_send[n] = half_acc[1].astype(jnp.bfloat16)
        last_copy(n).start()
    for n, half_acc in enumerate((acc_a, acc_b)):
        last_copy(n).wait_recv()
        cols = slice(n * HALF, (n + 1) * HALF)
        moe = half_acc[0] + last_recv[n].astype(jnp.float32)
        out_ref[:, cols] = (residual[:, cols] + residual_scale * moe).astype(jnp.bfloat16)

    for n in range(2):
        sum_copy(n).wait_send()
    for copy in info_copies() + y_copies():
        copy.wait_send()
    for n in range(2):
        last_copy(n).wait_send()

    @pl.loop(1, 4)
    def _(i):
        for m in range(2):
            wide_a(i, m).wait_send()
            wide_b(i, m).wait_send()
        ret_b(i).wait_send()
        sum_a(i).wait_send()
        sum_b(i).wait_send()

    @pl.loop(0, 4)
    def _(i):
        for k in range(1, 4):
            ret_a(k, i).wait_send()


def layer(*operands):
    vmem = pl.BlockSpec(memory_space=pltpu.VMEM)
    hbm = pl.BlockSpec(memory_space=pl.ANY)
    specs = [hbm, vmem, hbm, hbm, hbm, hbm, vmem, hbm, vmem, vmem, vmem, hbm, hbm]
    width = 1536

    def half(*shape):
        return pltpu.VMEM(shape, jnp.bfloat16)

    def full(*shape):
        return pltpu.VMEM(shape, jnp.float32)

    state = full(PLANES, KV_HERE, GROUP * ROWS, 128)
    table = full(4, 2, 64, 64)
    blocks = half(4, 2, 64, HALF)
    chosen = half(4, 4, 2, CAP, HALF)
    pair = full(2, 64, HALF)
    counts = [(9,)] + [
        n
        for n in ((4,), (2, 8), (2, 8), (4,), (4,), (32,), (2,), (13,), (2,), (2, 2, 4), (2, 4, 4), (4, 4), (2, 4), (2,))
        for _ in range(2)
    ]
    return pl.pallas_call(
        layer_kernel,
        out_shape=[
            jax.ShapeDtypeStruct((64, width), jnp.bfloat16),
            jax.ShapeDtypeStruct((2 * KV_HERE, ROWS // PAGE, PAGE * HEAD_DIM), jnp.bfloat16),
        ],
        in_specs=specs,
        out_specs=[vmem] * 2,
        scratch_shapes=[half(*operands[n].shape) for n in (0, 2, 3, 4, 7, 11, 12)]
        + [
            half(ROWS, 384),
            half(ROWS, 384),
            half(PLANES, ROWS, 384),
            half(KV_HERE, LINE // 2, 2 * CACHE_HERE, 128),
            half(KV_HERE, LINE, ROWS, 128),
            half(KV_HERE, 2 * CACHE_HERE, 128),
            half(PLANES, KV_HERE, GROUP * ROWS, 128),
            state,
            state,
            half(PLANES, ROWS, 384),
            half(PLANES, ROWS, 384),
            full(PLANES, 8, ROWS),
            full(PLANES, 8, ROWS),
            full(ROWS, 256),
            full(ROWS // PAGE, PAGE, 256),
            half(2, 64, width),
            half(2, 64, width),
            half(64, width),
            half(64, width),
            half(ROWS, width),
            full(64, width),
            table,
            table,
            blocks,
            blocks,
        ]
        + [chosen] * 6
        + [blocks] * 4
        + [pair, pair, half(2, 64, HALF), half(2, 64, HALF)]
        + [pltpu.SemaphoreType.DMA(n) for n in counts],
        compiler_params=pltpu.CompilerParams(
            vmem_limit_bytes=62 * 1024 * 1024, collective_id=1, has_side_effects=True
        ),
        name="layer",
    )(*operands)


def body(
    hidden_in,
    attn_gain,
    q_weight,
    k_weight,
    v_weight,
    o_weight,
    cache_kv,
    moe_gain,
    expert_in,
    expert_out,
    routes,
    route_prob,
    page_slot,
):
    hidden_out, page_slabs = layer(
        hidden_in, attn_gain, q_weight, k_weight, v_weight, cache_kv, page_slot,
        o_weight, moe_gain, routes.T, route_prob.T, expert_in, expert_out,
    )
    page_rows = page_slabs.transpose(1, 0, 2).reshape(ROWS // PAGE, KV_HERE, 2, PAGE * HEAD_DIM)
    return (hidden_out, page_rows)


def solution(mesh):
    return jax.shard_map(
        body,
        mesh=mesh,
        in_specs=(
            P("seq", None),
            P(),
            P(None, "exp"),
            P(None, "exp"),
            P(None, "exp"),
            P("exp", None),
            P("seq", "exp"),
            P(),
            P("seq", None, None),
            P("seq", None, None),
            P(("seq", "exp"), None),
            P(("seq", "exp"), None),
            P(),
        ),
        out_specs=(P(("seq", "exp"), None), P("seq", "exp", None, None)),
        check_vma=False,
    )
```
